32 devices in a mesh: ply: 4 (over x, core), tile: 8 (over z, y).
Axes of the slice: x: 2, y: 2, z: 4, core: 2. Of those that a mesh axis runs over, the one named last changes fastest.
Arguments:
- displacement: float32 [3, 24, 64, 1024], P(None, 'ply', 'tile'), may hold values from -0.2 to 0.2
- angle_index: int32 [24], P('ply'), may hold values from 0 to 3
- bond_table: float32 [4, 14], replicated, may hold values from 5 to 50
- interface_stiffness: float32 [23], replicated, may hold values from 2 to 20
Outputs:
- force_density: float32 [3, 24, 64, 1024], P(None, 'ply', 'tile')
The draws below stay inside these ranges and needn't reach their ends.
Inputs may be any that keep to these rules, and one draw needn't show every extreme that they name: `angle_index`: each ply's fibre orientation is an index into the rows of bond_table.
All inputs are finite; a program needn't handle non-finite values.
Results may differ from the reference program's by a relative error of at most 0.000058.
Values sent between devices are 32-bit elements; how exact they have to be, the bound alone decides.
No kernel may reach another device: no remote copies, remote signals or barrier semaphores. Data moves between devices by JAX's collectives and lax.ppermute only.
A program may use at most 128 MiB of HBM per device.

```python
import math
import jax
import jax.numpy as jnp

NY = 1024
NANG = 4
NBOND = 14
PLIES = 24
NX = 64


def set_ends(drawn, own_key, least, largest):
    spot = [jax.random.randint(jax.random.fold_in(own_key, axis), (), 0, length) for axis, length in enumerate(drawn.shape)]
    longest = drawn.shape.index(max(drawn.shape))
    beside = spot[:longest] + [(spot[longest] + 1) % drawn.shape[longest]] + spot[longest + 1:]
    return drawn.at[tuple(spot)].set(least).at[tuple(beside)].set(largest)


def level_of(own_key, dims, cuts, low, top_value):
    factor_of, own = 1.0, jax.random.fold_in(own_key, 6)
    for dim, blocks in cuts:
        steps = jnp.exp(jax.random.uniform(jax.random.fold_in(own, dim), (blocks,), jnp.float32, low / len(cuts), top_value / len(cuts)))
        factor_of = factor_of * jnp.repeat(steps, dims[dim] // blocks).reshape([-1 if axis == dim else 1 for axis in range(len(dims))])
    return factor_of


def normal_values(key, extent, deviation, bound, shards=(), held_as=jnp.bfloat16):
    level = level_of(key, extent, shards, -0.22, 0.18) if shards else 1.0
    values = jax.random.normal(key, extent, jnp.float32) * deviation * level
    return jnp.minimum(jnp.maximum(values, -bound), bound).astype(held_as)


def setup_inputs(seed: int = 0) -> dict:
    seeds = jax.random.split(jax.random.key(seed), 5)
    return {
        "displacement": normal_values(seeds[0], (3, PLIES, NX, NY), 0.04, 0.2, ((1, 4), (2, 8)), jnp.float32),
        "angle_index": set_ends(jax.random.randint(seeds[1], (PLIES,), 0, NANG), jax.random.fold_in(seeds[1], 1), 0, NANG - 1).astype(jnp.int32),
        "bond_table": jnp.clip(jnp.exp(jax.random.uniform(seeds[2], (NANG, NBOND), jnp.float32, math.log(5.0), math.log(50.0))), 5.0, 50.0),
        "interface_stiffness": jnp.clip(jnp.exp(jax.random.uniform(seeds[3], (PLIES - 1,), jnp.float32, math.log(2.0), math.log(20.0))), 2.0, 20.0),
    }


bulk_modulus = 40.0

def bond_list():
    halves = []
    for shift_x in range(-3, 4):
        for shift_y in range(-3, 4):
            radius = shift_x * shift_x + shift_y * shift_y
            if 0 < radius <= 9 and (shift_x > 0 or (shift_x == 0 and shift_y > 0)):
                halves.append((shift_x, shift_y))
    result = []
    for shift_x in range(-3, 4):
        for shift_y in range(-3, 4):
            radius = shift_x * shift_x + shift_y * shift_y
            if 0 < radius <= 9:
                if (shift_x, shift_y) in halves:
                    column = halves.index((shift_x, shift_y))
                else:
                    column = halves.index((-shift_x, -shift_y))
                result.append((shift_x, shift_y, math.sqrt(radius), column))
    return result

def inside(x_coord, y_coord, shift_x, shift_y, x_total, y_total):
    x_next = x_coord + shift_x
    y_next = y_coord + shift_y
    return (x_next >= 0) & (x_next < x_total) & (y_next >= 0) & (y_next < y_total)

def weight_sum(x_coord, y_coord, x_total, y_total):
    total = jnp.zeros((x_coord.shape[0], y_coord.shape[1]), jnp.float32)
    for shift_x, shift_y, length, column in bond_list():
        total = total + jnp.where(inside(x_coord, y_coord, shift_x, shift_y, x_total, y_total), length, 0.0)
    return total

def stretch(anchor, neighbour, shift_x, shift_y, length):
    gap = neighbour - anchor
    sep_x = shift_x + gap[0]
    sep_y = shift_y + gap[1]
    sep_z = gap[2]
    span = jnp.sqrt(sep_x * sep_x + sep_y * sep_y + sep_z * sep_z)
    return (sep_x, sep_y, sep_z, span, span - length)

def bond_terms(theta_here, mass_here, theta_there, mass_there, shear, extension, length):
    first_side = 3.0 * bulk_modulus * theta_here / mass_here + 15.0 * shear * (extension - theta_here * length / 3.0) / (mass_here * length)
    second_side = 3.0 * bulk_modulus * theta_there / mass_there + 15.0 * shear * (extension - theta_there * length / 3.0) / (mass_there * length)
    return first_side + second_side

def reference(displacement, angle_index, bond_table, interface_stiffness):
    x_total = displacement.shape[2]
    y_total = displacement.shape[3]
    bond_set = bond_list()
    x_grid = jnp.arange(x_total, dtype=jnp.int32)[:, None]
    y_grid = jnp.arange(y_total, dtype=jnp.int32)[None, :]
    x_wide = jnp.arange(-3, x_total + 3, dtype=jnp.int32)[:, None]
    y_wide = jnp.arange(-3, y_total + 3, dtype=jnp.int32)[None, :]
    mass_here = weight_sum(x_grid, y_grid, x_total, y_total)
    mass_wide = weight_sum(x_wide, y_wide, x_total, y_total)
    mass_wide = jnp.where(mass_wide > 0, mass_wide, 1.0)
    padded = jnp.pad(displacement, ((0, 0), (0, 0), (3, 3), (3, 3)))
    dilation = jnp.zeros(displacement.shape[1:], jnp.float32)
    for shift_x, shift_y, length, column in bond_set:
        neighbour = padded[:, :, 3 + shift_x:3 + shift_x + x_total, 3 + shift_y:3 + shift_y + y_total]
        stretched = stretch(displacement, neighbour, shift_x, shift_y, length)
        dilation = dilation + jnp.where(inside(x_grid, y_grid, shift_x, shift_y, x_total, y_total), stretched[4], 0.0)
    dilation = 3.0 * dilation / mass_here
    dilation_wide = jnp.pad(dilation, ((0, 0), (3, 3), (3, 3)))
    shear_table = bond_table[angle_index]
    force_x = jnp.zeros(displacement.shape[1:], jnp.float32)
    force_y = jnp.zeros(displacement.shape[1:], jnp.float32)
    force_z = jnp.zeros(displacement.shape[1:], jnp.float32)
    for shift_x, shift_y, length, column in bond_set:
        neighbour = padded[:, :, 3 + shift_x:3 + shift_x + x_total, 3 + shift_y:3 + shift_y + y_total]
        sep_x, sep_y, sep_z, span, extension = stretch(displacement, neighbour, shift_x, shift_y, length)
        theta_there = dilation_wide[:, 3 + shift_x:3 + shift_x + x_total, 3 + shift_y:3 + shift_y + y_total]
        mass_there = mass_wide[3 + shift_x:3 + shift_x + x_total, 3 + shift_y:3 + shift_y + y_total]
        shear = shear_table[:, column][:, None, None]
        scalar = bond_terms(dilation, mass_here, theta_there, mass_there, shear, extension, length)
        scalar = jnp.where(inside(x_grid, y_grid, shift_x, shift_y, x_total, y_total), scalar / span, 0.0)
        force_x = force_x + scalar * sep_x
        force_y = force_y + scalar * sep_y
        force_z = force_z + scalar * sep_z
    zero_end = jnp.zeros((1,), jnp.float32)
    coupling = jnp.concatenate([zero_end, interface_stiffness, zero_end])
    above = coupling[1:][None, :, None, None]
    below = coupling[:-1][None, :, None, None]
    upper = jnp.pad(displacement[:, 1:], ((0, 0), (0, 1), (0, 0), (0, 0)))
    lower = jnp.pad(displacement[:, :-1], ((0, 0), (1, 0), (0, 0), (0, 0)))
    layered = above * (upper - displacement) + below * (lower - displacement)
    return jnp.stack([force_x, force_y, force_z]) + layered
```

```python
import math

import jax
import jax.numpy as jnp
from jax import lax
from jax.experimental import pallas as pl
from jax.experimental.pallas import tpu as pltpu
from jax.sharding import PartitionSpec as P

bulk_modulus = 40.0
REACH = 3
LANES = 128
VMEM_LIMIT = 48 * 1024 * 1024


def bond_columns():
    halves = []
    for a in range(-REACH, REACH + 1):
        for b in range(-REACH, REACH + 1):
            if 0 < a * a + b * b <= 9 and (a > 0 or (a == 0 and b > 0)):
                halves.append((a, b))
    columns = {}
    for index, (a, b) in enumerate(halves):
        columns[(a, b)] = index
        columns[(-a, -b)] = index
    return columns


COLUMNS = bond_columns()
BONDS = {0: (1, 2, 3), 1: (-2, -1, 0, 1, 2), 2: (-2, -1, 0, 1, 2), 3: (0,)}


def length_of(a, b):
    return math.sqrt(a * a + b * b)


class Grid:
    def __init__(self, subs):
        self.subs = subs
        self.lane = lax.broadcasted_iota(jnp.int32, (subs, LANES), 1)
        self.sub = lax.broadcasted_iota(jnp.int32, (subs, LANES), 0)
        self.y = self.sub * LANES + self.lane
        self.total = subs * LANES

    def ahead(self, row, shifts):
        after = pltpu.roll(row, self.subs - 1, axis=0)
        return {
            b: pltpu.roll(jnp.where(self.lane < b, after, row), LANES - b, axis=1) for b in shifts
        }

    def back(self, rows):
        total = None
        for b, row in rows.items():
            before = pltpu.roll(row, 1, axis=0)
            moved = pltpu.roll(jnp.where(self.lane >= LANES - b, before, row), b, axis=1)
            total = moved if total is None else total + moved
        return total

    def has_ahead(self, b):
        return self.y < self.total - b

    def ring(self, a):
        total = None
        for b in range(-REACH, REACH + 1):
            if 0 < a * a + b * b <= 9:
                exists = (self.y + b >= 0) & (self.y + b < self.total)
                term = jnp.where(exists, length_of(a, b), 0.0)
                total = term if total is None else total + term
        return total


def row_of(ref, lead, x, cols, subs):
    return ref[(*lead, pl.ds(x, subs, stride=cols), slice(None))]


def separation(here, here_x, there):
    return (there[0] - here_x, there[1] - here[1], there[2] - here[2])


def square(sep):
    return sep[0] * sep[0] + sep[1] * sep[1] + sep[2] * sep[2]


def pack_kernel(tiles, u_ref, a_ref, b_ref):
    comps, plies, depth, _ = u_ref.shape
    subs = a_ref.shape[2]
    cols = depth // subs
    odd = lax.axis_index("tile") % 2 == 1
    for c in range(comps):
        for p in range(plies):
            for j in range(REACH):
                first = row_of(u_ref, (c, p), j, cols, subs)
                last = row_of(u_ref, (c, p), cols - REACH + j, cols, subs)
                at = (c * plies + p) * REACH + j
                a_ref[0, at] = jnp.where(odd, first, last)
                b_ref[0, at] = jnp.where(odd, last, first)


def fill_rows(grid, rows_ref, x, row):
    for c in range(3):
        rows_ref[0, c, x] = row[c]
        for b, moved in grid.ahead(row[c], (1, 2, 3)).items():
            rows_ref[b, c, x] = moved + float(b) if c == 1 else moved


def add_to(ref, at, value):
    ref[at] = ref[at] + value


def inner_kernel(u_ref, t_ref, a_ref, b_ref, rows_ref, sum_ref):
    comps, plies, depth, _ = u_ref.shape
    subs = t_ref.shape[2]
    cols = depth // subs
    grid = Grid(subs)
    odd = lax.axis_index("tile") % 2 == 1

    def ply(p, carry):
        for x in range(cols):
            fill_rows(grid, rows_ref, x, [row_of(u_ref, (c, p), x, cols, subs) for c in range(3)])
        extension_sums(grid, rows_ref, sum_ref, 0, cols, lambda i, j: True, lambda b, i, j: None)
        for x in range(cols):
            t_ref[p, x] = sum_ref[x]
        for j in range(REACH):
            first = sum_ref[j]
            last = sum_ref[cols - REACH + j]
            a_ref[0, p * REACH + j] = jnp.where(odd, first, last)
            b_ref[0, p * REACH + j] = jnp.where(odd, last, first)
        return carry

    lax.fori_loop(0, plies, ply, 0)


def extension_sums(grid, rows_ref, sum_ref, first, last, wanted, side):
    sums = {}
    shifted = {}
    for b, offsets in BONDS.items():
        for i in range(first, last):
            pairs = [(a, i + a) for a in offsets if first <= i + a < last and wanted(i, i + a)]
            if not pairs:
                continue
            here = [rows_ref[0, c, i] for c in range(3)]
            for a, j in pairs:
                there = [rows_ref[b, c, j] for c in range(3)]
                sep = separation(here, here[0] - float(a) if a else here[0], there)
                q = square(sep)
                e = q * lax.rsqrt(q) - length_of(a, b)
                mask = side(b, i, j)
                if mask is not None:
                    e = jnp.where(mask, e, 0.0)
                elif b:
                    e = jnp.where(grid.has_ahead(b), e, 0.0)
                sums[i] = sums[i] + e if i in sums else e
                if b == 0:
                    sums[j] = sums[j] + e if j in sums else e
                else:
                    key = (j, b)
                    shifted[key] = shifted[key] + e if key in shifted else e
    for x in range(first, last):
        rows = {b: shifted[(x, b)] for b in (1, 2, 3) if (x, b) in shifted}
        total = grid.back(rows) if rows else None
        if x in sums:
            total = sums[x] if total is None else total + sums[x]
        if total is not None:
            sum_ref[x] = total


def force_kernel(
    ply_peers, tile_peers, angle_ref, table_ref, stiff_ref, u_ref, ua_ref, ub_ref, t_ref, ta_ref, tb_ref,
    above_ref, below_ref, out_ref, rows_ref, sum_ref, strain_ref, weight_ref, pair_ref, force_ref,
):
    comps, plies, depth, _ = u_ref.shape
    subs = t_ref.shape[2]
    cols = depth // subs
    wide = cols + 2 * REACH
    grid = Grid(subs)
    tile = lax.axis_index("tile")
    slab = lax.axis_index("ply")
    odd = tile % 2 == 1
    has_left = tile > 0
    has_right = tile < tile_peers - 1

    def is_own(x):
        return REACH <= x < REACH + cols

    def crossing(i, j):
        return is_own(i) != is_own(j)

    def needed(i, j):
        return is_own(i) or is_own(j)

    ones = jnp.ones((subs, LANES), jnp.int32)
    left_mask = ones * has_left.astype(jnp.int32) > 0
    right_mask = ones * has_right.astype(jnp.int32) > 0
    masks = {}
    for b in range(REACH + 1):
        ahead = grid.has_ahead(b)
        masks[(b, 0)] = ahead
        masks[(b, -1)] = ahead & left_mask
        masks[(b, 1)] = ahead & right_mask

    def mask_of(b, i, j):
        side = 0
        if min(i, j) < REACH:
            side = -1
        if max(i, j) >= REACH + cols:
            side = 1
        if b == 0 and side == 0:
            return None
        return masks[(b, side)]

    ring = {a: grid.ring(a) for a in range(REACH + 1)}
    for x in range(wide):
        mass = ring[0]
        for a in range(-REACH, REACH + 1):
            if a == 0:
                continue
            term = ring[abs(a)]
            if is_own(x) and x + a < REACH:
                term = jnp.where(left_mask, term, 0.0)
            if is_own(x) and x + a >= REACH + cols:
                term = jnp.where(right_mask, term, 0.0)
            mass = mass + term
        weight_ref[x] = 1.0 / mass
    slot = {}
    for x in range(wide):
        moved = grid.ahead(weight_ref[x], (1, 2, 3))
        moved[0] = weight_ref[x]
        for b, offsets in BONDS.items():
            for a in offsets:
                i = x - a
                if 0 <= i < wide and needed(i, x):
                    slot[(b, a, i)] = len(slot)
                    pair_ref[slot[(b, a, i)]] = weight_ref[i] + moved[b]

    def ply(p, carry):
        for x in range(cols):
            fill_rows(grid, rows_ref, REACH + x, [row_of(u_ref, (c, p), x, cols, subs) for c in range(3)])
        for j in range(REACH):
            at = [(c * plies + p) * REACH + j for c in range(3)]
            from_a = [ua_ref[0, at[c]] for c in range(3)]
            from_b = [ub_ref[0, at[c]] for c in range(3)]
            fill_rows(grid, rows_ref, j, [jnp.where(odd, from_a[c], from_b[c]) for c in range(3)])
            fill_rows(grid, rows_ref, REACH + cols + j, [jnp.where(odd, from_b[c], from_a[c]) for c in range(3)])
        for x in range(wide):
            sum_ref[x] = jnp.zeros((subs, LANES), jnp.float32)
        extension_sums(grid, rows_ref, sum_ref, 0, wide, crossing, mask_of)
        for x in range(wide):
            if is_own(x):
                inner = t_ref[p, x - REACH]
            else:
                j = x if x < REACH else x - REACH - cols
                from_a = ta_ref[0, p * REACH + j]
                from_b = tb_ref[0, p * REACH + j]
                inner = jnp.where(odd, from_a, from_b) if x < REACH else jnp.where(odd, from_b, from_a)
            weight = weight_ref[x]
            strain = 3.0 * (sum_ref[x] + inner) * weight * weight
            strain_ref[0, x] = strain
            for b, moved in grid.ahead(strain, (1, 2, 3)).items():
                strain_ref[b, x] = moved

        ply_total = ply_peers * plies
        layer = slab * plies + p
        up = jnp.where(layer < ply_total - 1, stiff_ref[jnp.minimum(layer, ply_total - 2)], 0.0)
        down = jnp.where(layer > 0, stiff_ref[jnp.maximum(layer - 1, 0)], 0.0)
        top = p == plies - 1
        bottom = p == 0
        for c in range(3):
            for x in range(cols):
                here = rows_ref[0, c, REACH + x]
                over = jnp.where(
                    top,
                    row_of(above_ref, (c, 0), x, cols, subs),
                    row_of(u_ref, (c, jnp.minimum(p + 1, plies - 1)), x, cols, subs),
                )
                under = jnp.where(
                    bottom,
                    row_of(below_ref, (c, 0), x, cols, subs),
                    row_of(u_ref, (c, jnp.maximum(p - 1, 0)), x, cols, subs),
                )
                force_ref[c, x] = up * (over - here) + down * (under - here)

        angle = angle_ref[p]
        shifted = {}
        for b, offsets in BONDS.items():
            for i in range(wide):
                pairs = [(a, i + a) for a in offsets if 0 <= i + a < wide and needed(i, i + a)]
                if not pairs:
                    continue
                here = [rows_ref[0, c, i] for c in range(3)]
                strain = strain_ref[0, i]
                mine = None
                for a, j in pairs:
                    length = length_of(a, b)
                    shear = table_ref[angle, COLUMNS[(a, b)]]
                    alpha = 3.0 * bulk_modulus - 5.0 * shear
                    beta = 15.0 / length * shear
                    there = [rows_ref[b, c, j] for c in range(3)]
                    sep = separation(here, here[0] - float(a) if a else here[0], there)
                    r = lax.rsqrt(square(sep))
                    f = (alpha * r) * (strain + strain_ref[b, j]) + (beta * pair_ref[slot[(b, a, i)]]) * (
                        1.0 - length * r
                    )
                    mask = mask_of(b, i, j)
                    if mask is not None:
                        f = jnp.where(mask, f, 0.0)
                    push = [f * sep[c] for c in range(3)]
                    if is_own(i):
                        mine = push if mine is None else [mine[c] + push[c] for c in range(3)]
                    if is_own(j):
                        if b == 0:
                            for c in range(3):
                                force_ref[c, j - REACH] = force_ref[c, j - REACH] - push[c]
                        else:
                            key = (j, b)
                            if key in shifted:
                                shifted[key] = [shifted[key][c] + push[c] for c in range(3)]
                            else:
                                shifted[key] = push
                if mine is not None:
                    for c in range(3):
                        add_to(force_ref, (c, i - REACH), mine[c])
        for x in range(cols):
            for c in range(3):
                rows = {b: shifted[(x + REACH, b)][c] for b in (1, 2, 3)}
                total = force_ref[c, x] - grid.back(rows)
                out_ref[c, p, pl.ds(x, subs, stride=cols), :] = total
        return carry

    lax.fori_loop(0, plies, ply, 0)


def local(displacement, angle_index, bond_table, interface_stiffness):
    comps, plies, cols, rows = displacement.shape
    subs = rows // LANES
    tiles = lax.axis_size("tile")
    slabs = lax.axis_size("ply")
    assert rows % LANES == 0 and cols >= 2 * REACH
    view = (
        displacement.reshape(comps, plies, cols, subs, LANES)
        .transpose(0, 1, 3, 2, 4)
        .reshape(comps, plies, subs * cols, LANES)
    )
    f32 = jnp.float32
    whole = pl.BlockSpec(memory_space=pltpu.VMEM)
    scalars = pl.BlockSpec(memory_space=pltpu.SMEM)
    params = pltpu.CompilerParams(vmem_limit_bytes=VMEM_LIMIT)

    swap_a = [(i, i ^ 1) for i in range(tiles) if (i ^ 1) < tiles]
    swap_b = [(i, j) for k in range(1, tiles - 1, 2) for i, j in ((k, k + 1), (k + 1, k))]
    edge = jax.ShapeDtypeStruct((1, comps * plies * REACH, subs, LANES), f32)
    edge_a, edge_b = pl.pallas_call(
        lambda *refs: pack_kernel(tiles, *refs),
        out_shape=[edge, edge],
        in_specs=[whole],
        out_specs=[whole, whole],
        compiler_params=params,
        name="pack",
    )(view)
    got_a = lax.ppermute(edge_a, "tile", swap_a)
    got_b = lax.ppermute(edge_b, "tile", swap_b)

    thin = jax.ShapeDtypeStruct((1, plies * REACH, subs, LANES), f32)
    inner, thin_a, thin_b = pl.pallas_call(
        inner_kernel,
        out_shape=[jax.ShapeDtypeStruct((plies, cols, subs, LANES), f32), thin, thin],
        in_specs=[whole],
        out_specs=[whole, whole, whole],
        scratch_shapes=[
            pltpu.VMEM((REACH + 1, 3, cols, subs, LANES), f32),
            pltpu.VMEM((cols, subs, LANES), f32),
        ],
        compiler_params=params,
        name="inner",
    )(view)
    got_thin_a = lax.ppermute(thin_a, "tile", swap_a)
    got_thin_b = lax.ppermute(thin_b, "tile", swap_b)
    above = lax.ppermute(view[:, :1], "ply", [(i + 1, i) for i in range(slabs - 1)])
    below = lax.ppermute(view[:, plies - 1 :], "ply", [(i, i + 1) for i in range(slabs - 1)])

    wide = cols + 2 * REACH
    out = pl.pallas_call(
        lambda *refs: force_kernel(slabs, tiles, *refs),
        out_shape=jax.ShapeDtypeStruct(view.shape, f32),
        in_specs=[scalars] * 3 + [whole] * 8,
        out_specs=whole,
        scratch_shapes=[
            pltpu.VMEM((REACH + 1, 3, wide, subs, LANES), f32),
            pltpu.VMEM((wide, subs, LANES), f32),
            pltpu.VMEM((REACH + 1, wide, subs, LANES), f32),
            pltpu.VMEM((wide, subs, LANES), f32),
            pltpu.VMEM((14 * wide, subs, LANES), f32),
            pltpu.VMEM((3, cols, subs, LANES), f32),
        ],
        compiler_params=params,
        name="force",
    )(
        angle_index, bond_table, interface_stiffness, view, got_a, got_b, inner, got_thin_a, got_thin_b,
        above, below,
    )
    return (
        out.reshape(comps, plies, subs, cols, LANES)
        .transpose(0, 1, 3, 2, 4)
        .reshape(comps, plies, cols, rows)
    )


def solution(mesh):
    placed = (P(None, "ply", "tile", None), P("ply"), P(), P())
    return jax.shard_map(
        local, mesh=mesh, in_specs=placed, out_specs=P(None, "ply", "tile", None), check_vma=False
    )
```

```python
import math

import jax
import jax.numpy as jnp
from jax import lax
from jax.experimental import pallas as pl
from jax.experimental.pallas import tpu as pltpu
from jax.sharding import PartitionSpec as P

bulk_modulus = 40.0
REACH = 3
LANES = 128
VMEM_LIMIT = 24 * 1024 * 1024


def bond_columns():
    halves = []
    for a in range(-REACH, REACH + 1):
        for b in range(-REACH, REACH + 1):
            if 0 < a * a + b * b <= 9 and (a > 0 or (a == 0 and b > 0)):
                halves.append((a, b))
    columns = {}
    for index, (a, b) in enumerate(halves):
        columns[(a, b)] = index
        columns[(-a, -b)] = index
    return columns


COLUMNS = bond_columns()
BONDS = {0: (1, 2, 3), 1: (-2, -1, 0, 1, 2), 2: (-2, -1, 0, 1, 2), 3: (0,)}


def length_of(a, b):
    return math.sqrt(a * a + b * b)


class Plan:
    def __init__(self, cols):
        self.cols = cols
        self.wide = cols + 2 * REACH
        self.own = range(REACH, REACH + cols)
        self.low = range(0, REACH)
        self.high = range(REACH + cols, self.wide)
        self.near_b = range(REACH, 2 * REACH)
        self.near_a = range(cols, cols + REACH)
        every = [
            (b, a, i)
            for b, offsets in BONDS.items()
            for i in range(self.wide)
            for a in offsets
            if 0 <= i + a < self.wide and (i in self.own or i + a in self.own)
        ]
        inner = [k for k in every if k[2] in self.own and k[2] + k[1] in self.own]
        self.inner_a = [k for k in inner if k[2] in self.near_a or k[2] + k[1] in self.near_a]
        self.inner_b = [k for k in inner if k not in self.inner_a]
        self.cross_a = [k for k in every if max(k[2], k[2] + k[1]) in self.high]
        self.cross_b = [k for k in every if min(k[2], k[2] + k[1]) in self.low]
        self.late = [k for k in every if min(k[2], k[2] + k[1]) < 2 * REACH]
        self.early = [k for k in every if k not in self.late]
        self.start_a = min(min(k[2], k[2] + k[1]) for k in self.inner_a)


class Grid:
    def __init__(self, subs):
        self.subs = subs
        self.lane = lax.broadcasted_iota(jnp.int32, (subs, LANES), 1)
        self.y = lax.broadcasted_iota(jnp.int32, (subs, LANES), 0) * LANES + self.lane
        self.total = subs * LANES
        self.exists = {b: self.y < self.total - b for b in range(1, REACH + 1)}

    def ahead(self, row):
        after = pltpu.roll(row, self.subs - 1, axis=0)
        return {
            b: pltpu.roll(jnp.where(self.lane < b, after, row), LANES - b, axis=1) for b in range(1, REACH + 1)
        }

    def back(self, rows):
        total = None
        for b, row in rows.items():
            before = pltpu.roll(row, 1, axis=0)
            moved = pltpu.roll(jnp.where(self.lane >= LANES - b, before, row), b, axis=1)
            total = moved if total is None else total + moved
        return total

    def ring(self, a):
        total = None
        for b in range(-REACH, REACH + 1):
            if 0 < a * a + b * b <= 9:
                exists = (self.y + b >= 0) & (self.y + b < self.total)
                term = jnp.where(exists, length_of(a, b), 0.0)
                total = term if total is None else total + term
        return total


class Store:
    def __init__(self, *parts):
        self.parts = parts

    def at(self, column, *lead):
        for ref, first, columns, head in self.parts:
            if column in columns:
                return ref, (*head, *lead, column - first)
        raise KeyError(column)

    def get(self, column, *lead):
        ref, index = self.at(column, *lead)
        return ref[index]

    def put(self, column, value, *lead):
        ref, index = self.at(column, *lead)
        ref[index] = value


def frame():
    odd = lax.axis_index("tile") % 2 == 1
    return odd, jnp.where(odd, -1.0, 1.0).astype(jnp.float32)


def sides(tiles):
    tile = lax.axis_index("tile")
    has_a = (tile % 2 == 1) | (tile + 1 < tiles)
    has_b = jnp.where(tile % 2 == 1, tile + 1 < tiles, tile > 0)
    return has_a, has_b


def keep_row(grid, rows, column, row):
    for c in range(3):
        rows.put(column, row[c], 0, c)
        for b, moved in grid.ahead(row[c]).items():
            rows.put(column, moved + float(b) if c == 1 else moved, b, c)


def separation(rows, b, a, i, here):
    there = [rows.get(i + a, b, c) for c in range(3)]
    here_x = here[0] - float(a) if a else here[0]
    return there[0] - here_x, there[1] - here[1], there[2] - here[2]


def by_row(keys):
    groups = {}
    for b, a, i in keys:
        groups.setdefault((b, i), []).append(a)
    return groups.items()


def extension_sums(grid, rows, keys, mask_of, keep):
    sums = {}
    shifted = {}
    for (b, i), offsets in by_row(keys):
        here = [rows.get(i, 0, c) for c in range(3)]
        for a in offsets:
            sep = separation(rows, b, a, i, here)
            q = sep[0] * sep[0] + sep[1] * sep[1] + sep[2] * sep[2]
            r = lax.rsqrt(q)
            keep((b, a, i), r)
            e = q * r - length_of(a, b)
            mask = mask_of(b)
            if mask is not None:
                e = jnp.where(mask, e, 0.0)
            sums[i] = sums[i] + e if i in sums else e
            if b == 0:
                sums[i + a] = sums[i + a] + e if i + a in sums else e
            else:
                key = (i + a, b)
                shifted[key] = shifted[key] + e if key in shifted else e
    for x in sorted({x for x, _ in shifted}):
        total = grid.back({b: shifted[(x, b)] for b in range(1, REACH + 1) if (x, b) in shifted})
        sums[x] = sums[x] + total if x in sums else total
    return sums


def near_a_kernel(plan, u_hbm, message, rows_ref, rest_ref, sums_ref, inverse_ref, u_ref, sems):
    comps, plies, depth, _ = u_ref.shape
    subs = depth // plan.cols
    copies = [
        pltpu.make_async_copy(u_hbm.at[:, pl.ds(p, 1)], u_ref.at[:, pl.ds(p, 1)], sems.at[p]) for p in range(plies)
    ]
    for copy in copies:
        copy.start()
    grid = Grid(subs)
    odd, sign = frame()
    slots = {key: n for n, key in enumerate(plan.inner_a)}

    def source(p, c, column):
        x = column - REACH
        at = jnp.where(odd, plan.cols - 1 - x, x)
        row = u_ref[c, p, pl.ds(at, subs, stride=plan.cols), :]
        return row * sign if c == 0 else row

    def ply(p, carry):
        pltpu.make_async_copy(u_hbm.at[:, pl.ds(p, 1)], u_ref.at[:, pl.ds(p, 1)], sems.at[p]).wait()
        rows = Store((rows_ref, plan.start_a, range(plan.start_a, plan.own.stop), (p,)))
        for x in rows.parts[0][2]:
            row = [source(p, c, x) for c in range(3)]
            keep_row(grid, rows, x, row)
            if x in plan.near_a:
                for c in range(3):
                    message[0, p, c * REACH + x - plan.near_a.start] = row[c]
        for x in range(REACH, plan.start_a):
            for c in range(3):
                rest_ref[p, c, x - REACH] = source(p, c, x)

        def keep(key, r):
            inverse_ref[p, slots[key]] = r

        sums = extension_sums(grid, rows, plan.inner_a, grid.exists.get, keep)
        for x in rows.parts[0][2]:
            sums_ref[p, x - plan.start_a] = sums[x]
            if x in plan.near_a:
                message[0, p, 3 * REACH + x - plan.near_a.start] = sums[x]
        return carry

    lax.fori_loop(0, plies, ply, 0)


def near_b_kernel(plan, rows_a_ref, rest_ref, sums_a_ref, message, rows_ref, sums_ref, inverse_ref, bottom_ref, top_ref):
    plies = rows_a_ref.shape[0]
    grid = Grid(rows_a_ref.shape[-2])
    slots = {key: n for n, key in enumerate(plan.inner_b)}
    fresh = range(REACH, plan.start_a)

    def ply(p, carry):
        rows = Store(
            (rows_ref, REACH, fresh, (p,)), (rows_a_ref, plan.start_a, range(plan.start_a, plan.own.stop), (p,))
        )
        for x in fresh:
            keep_row(grid, rows, x, [rest_ref[p, c, x - REACH] for c in range(3)])

        def keep(key, r):
            inverse_ref[p, slots[key]] = r

        sums = extension_sums(grid, rows, plan.inner_b, grid.exists.get, keep)
        for x in range(REACH, plan.near_a.start):
            total = sums[x] + sums_a_ref[p, x - plan.start_a] if x >= plan.start_a else sums[x]
            sums_ref[p, x - REACH] = total
            if x in plan.near_b:
                message[0, p, 3 * REACH + x - REACH] = total
                for c in range(3):
                    message[0, p, c * REACH + x - REACH] = rows.get(x, 0, c)
        return carry

    lax.fori_loop(0, plies, ply, 0)
    for p, ref in ((0, bottom_ref), (plies - 1, top_ref)):
        rows = Store(
            (rows_ref, REACH, fresh, (p,)), (rows_a_ref, plan.start_a, range(plan.start_a, plan.own.stop), (p,))
        )
        for c in range(3):
            for x in plan.own:
                ref[0, c, x - REACH] = rows.get(x, 0, c)


def weight_kernel(plan, tiles, weight_ref, pair_ref):
    grid = Grid(weight_ref.shape[-2])
    ones = jnp.ones((grid.subs, LANES), jnp.int32)
    has_a, has_b = (ones * side.astype(jnp.int32) > 0 for side in sides(tiles))
    ring = {a: grid.ring(a) for a in range(REACH + 1)}
    weight = {}
    for x in range(plan.wide):
        mass = ring[0]
        for a in range(-REACH, REACH + 1):
            term = ring[abs(a)]
            if x in plan.own and x + a in plan.low:
                term = jnp.where(has_b, term, 0.0)
            if x in plan.own and x + a in plan.high:
                term = jnp.where(has_a, term, 0.0)
            if a:
                mass = mass + term
        weight[x] = 1.0 / mass
        weight_ref[x] = weight[x]
    moved = {x: {0: weight[x], **grid.ahead(weight[x])} for x in range(plan.wide)}
    for n, (b, a, i) in enumerate(plan.early + plan.late):
        pair_ref[n] = weight[i] + moved[i + a][b]


def bond_forces(plan, grid, odd, table_ref, angle, rows, strains, inverse, pair, keys, mask_of, force):
    shears = {}

    def shear_of(a, b):
        if (a, b) not in shears:
            column = COLUMNS[(a, b)]
            mirrored = COLUMNS[(-a, b)]
            at = column if column == mirrored else jnp.where(odd, mirrored, column)
            shears[(a, b)] = table_ref[angle, at]
        return shears[(a, b)]

    shifted = {}
    for (b, i), offsets in by_row(keys):
        here = [rows.get(i, 0, c) for c in range(3)]
        strain = strains.get(i, 0)
        mine = None
        for a in offsets:
            j = i + a
            length = length_of(a, b)
            shear = shear_of(a, b)
            alpha = 3.0 * bulk_modulus - 5.0 * shear
            beta = 15.0 / length * shear
            sep = separation(rows, b, a, i, here)
            r = inverse((b, a, i))
            f = (alpha * r) * (strain + strains.get(j, b)) + (beta * pair((b, a, i))) * (1.0 - length * r)
            mask = mask_of(b, i, j)
            if mask is not None:
                f = jnp.where(mask, f, 0.0)
            push = [f * sep[c] for c in range(3)]
            if i in plan.own:
                mine = push if mine is None else [mine[c] + push[c] for c in range(3)]
            if j in plan.own:
                if b == 0:
                    force(j, [-push[c] for c in range(3)])
                elif (j, b) in shifted:
                    shifted[(j, b)] = [shifted[(j, b)][c] + push[c] for c in range(3)]
                else:
                    shifted[(j, b)] = push
        if mine is not None:
            force(i, mine)
    for x in sorted({x for x, _ in shifted}):
        held = {b: shifted[(x, b)] for b in range(1, REACH + 1) if (x, b) in shifted}
        force(x, [-grid.back({b: row[c] for b, row in held.items()}) for c in range(3)])


def early_kernel(
    plan, tiles, slabs, angle_ref, table_ref, stiff_ref, got_ref, rows_a_ref, rows_b_ref, sums_a_ref, sums_b_ref,
    inverse_a_ref, inverse_b_ref, weight_ref, pair_ref, above_ref, below_ref,
    force_ref, strain_ref, halo_ref, cross_ref,
):
    plies = rows_a_ref.shape[0]
    grid = Grid(rows_a_ref.shape[-2])
    odd, _ = frame()
    slab = lax.axis_index("ply")
    in_a = {key: n for n, key in enumerate(plan.inner_a)}
    in_b = {key: n for n, key in enumerate(plan.inner_b)}
    in_cross = {key: n for n, key in enumerate(plan.cross_a)}
    in_pair = {key: n for n, key in enumerate(plan.early + plan.late)}
    first = 2 * REACH
    has_a = None
    if tiles % 2:
        has_a = jnp.ones((grid.subs, LANES), jnp.int32) * sides(tiles)[0].astype(jnp.int32) > 0

    def cross_mask(b):
        mask = grid.exists.get(b)
        if has_a is None:
            return mask
        return has_a if mask is None else mask & has_a

    def mask_of(b, i, j):
        return cross_mask(b) if max(i, j) in plan.high else grid.exists.get(b)

    def ply(p, carry):
        rows = Store(
            (rows_b_ref, REACH, range(REACH, plan.start_a), (p,)),
            (rows_a_ref, plan.start_a, range(plan.start_a, plan.own.stop), (p,)),
            (halo_ref, plan.high.start, plan.high, ()),
        )
        strains = Store((strain_ref, first, range(first, plan.wide), (p,)))
        for j in range(REACH):
            row = [got_ref[0, p, c * REACH + j] for c in range(3)]
            keep_row(grid, rows, plan.wide - 1 - j, [-row[0], row[1], row[2]])

        def keep(key, r):
            cross_ref[in_cross[key]] = r

        sums = extension_sums(grid, rows, plan.cross_a, cross_mask, keep)
        for x in range(first, plan.wide):
            if x in plan.high:
                total = got_ref[0, p, 3 * REACH + plan.wide - 1 - x]
            elif x >= plan.near_a.start:
                total = sums_a_ref[p, x - plan.start_a]
            else:
                total = sums_b_ref[p, x - REACH]
            if x in sums:
                total = total + sums[x]
            strain = 3.0 * total * (weight_ref[x] * weight_ref[x])
            strains.put(x, strain, 0)
            for b, moved in grid.ahead(strain).items():
                strains.put(x, moved, b)

        layers = slabs * plies
        layer = slab * plies + p
        up = jnp.where(layer < layers - 1, stiff_ref[jnp.minimum(layer, layers - 2)], 0.0)
        down = jnp.where(layer > 0, stiff_ref[jnp.maximum(layer - 1, 0)], 0.0)
        over = Store(*((r, s, cs, (jnp.minimum(p + 1, plies - 1),)) for r, s, cs, _ in rows.parts[:2]))
        under = Store(*((r, s, cs, (jnp.maximum(p - 1, 0),)) for r, s, cs, _ in rows.parts[:2]))
        for x in plan.own:
            for c in range(3):
                here = rows.get(x, 0, c)
                above = jnp.where(p == plies - 1, above_ref[0, c, x - REACH], over.get(x, 0, c))
                below = jnp.where(p == 0, below_ref[0, c, x - REACH], under.get(x, 0, c))
                force_ref[p, c, x - REACH] = up * (above - here) + down * (below - here)

        def inverse(key):
            if key in in_cross:
                return cross_ref[in_cross[key]]
            return inverse_a_ref[p, in_a[key]] if key in in_a else inverse_b_ref[p, in_b[key]]

        def force(x, values):
            for c in range(3):
                force_ref[p, c, x - REACH] = force_ref[p, c, x - REACH] + values[c]

        bond_forces(
            plan, grid, odd, table_ref, angle_ref[p], rows, strains, inverse, lambda key: pair_ref[in_pair[key]],
            plan.early, mask_of, force,
        )
        return carry

    lax.fori_loop(0, plies, ply, 0)


def late_kernel(
    plan, tiles, angle_ref, table_ref, got_ref, rows_a_ref, rows_b_ref, sums_b_ref, inverse_a_ref, inverse_b_ref,
    weight_ref, pair_ref, force_in_ref, strain_a_ref, out_hbm, halo_ref, cross_ref, strain_ref, force_ref, out_ref, sems,
):
    plies = rows_a_ref.shape[0]
    grid = Grid(rows_a_ref.shape[-2])
    odd, sign = frame()
    in_a = {key: n for n, key in enumerate(plan.inner_a)}
    in_b = {key: n for n, key in enumerate(plan.inner_b)}
    in_cross = {key: n for n, key in enumerate(plan.cross_b)}
    in_pair = {key: n for n, key in enumerate(plan.early + plan.late)}
    first = 2 * REACH
    has_b = jnp.ones((grid.subs, LANES), jnp.int32) * sides(tiles)[1].astype(jnp.int32) > 0
    cross_masks = {b: grid.exists[b] & has_b if b else has_b for b in range(REACH + 1)}

    def mask_of(b, i, j):
        return cross_masks[b] if min(i, j) in plan.low else grid.exists.get(b)

    def ply(p, carry):
        rows = Store(
            (halo_ref, 0, plan.low, ()),
            (rows_b_ref, REACH, range(REACH, plan.start_a), (p,)),
            (rows_a_ref, plan.start_a, range(plan.start_a, plan.own.stop), (p,)),
        )
        strains = Store((strain_ref, 0, range(first), ()), (strain_a_ref, first, range(first, plan.wide), (p,)))
        for j in range(REACH):
            row = [got_ref[0, p, c * REACH + j] for c in range(3)]
            keep_row(grid, rows, REACH - 1 - j, [-row[0], row[1], row[2]])

        def keep(key, r):
            cross_ref[in_cross[key]] = r

        sums = extension_sums(grid, rows, plan.cross_b, cross_masks.get, keep)
        for x in range(first):
            total = got_ref[0, p, 3 * REACH + REACH - 1 - x] if x in plan.low else sums_b_ref[p, x - REACH]
            strain = 3.0 * (total + sums[x]) * (weight_ref[x] * weight_ref[x])
            strains.put(x, strain, 0)
            for b, moved in grid.ahead(strain).items():
                strains.put(x, moved, b)
        for c in range(3):
            for x in plan.own:
                force_ref[c, x - REACH] = force_in_ref[p, c, x - REACH]

        def inverse(key):
            if key in in_cross:
                return cross_ref[in_cross[key]]
            return inverse_a_ref[p, in_a[key]] if key in in_a else inverse_b_ref[p, in_b[key]]

        def force(x, values):
            for c in range(3):
                force_ref[c, x - REACH] = force_ref[c, x - REACH] + values[c]

        bond_forces(
            plan, grid, odd, table_ref, angle_ref[p], rows, strains, inverse, lambda key: pair_ref[in_pair[key]],
            plan.late, mask_of, force,
        )
        for x in plan.own:
            at = jnp.where(odd, plan.cols - 1 - (x - REACH), x - REACH)
            for c in range(3):
                value = force_ref[c, x - REACH]
                out_ref[c, p, pl.ds(at, grid.subs, stride=plan.cols), :] = value * sign if c == 0 else value
        pltpu.make_async_copy(out_ref.at[:, pl.ds(p, 1)], out_hbm.at[:, pl.ds(p, 1)], sems.at[p]).start()
        return carry

    lax.fori_loop(0, plies, ply, 0)
    for p in range(plies):
        pltpu.make_async_copy(out_ref.at[:, pl.ds(p, 1)], out_hbm.at[:, pl.ds(p, 1)], sems.at[p]).wait()


def local(displacement, angle_index, bond_table, interface_stiffness):
    comps, plies, cols, length = displacement.shape
    subs = length // LANES
    tiles = lax.axis_size("tile")
    slabs = lax.axis_size("ply")
    assert length % LANES == 0 and cols >= 2 * REACH
    plan = Plan(cols)
    view = (
        displacement.reshape(comps, plies, cols, subs, LANES)
        .transpose(0, 1, 3, 2, 4)
        .reshape(comps, plies, subs * cols, LANES)
    )
    whole = pl.BlockSpec(memory_space=pltpu.VMEM)
    scalars = pl.BlockSpec(memory_space=pltpu.SMEM)
    anywhere = pl.BlockSpec(memory_space=pl.ANY)

    def array(*shape):
        return jax.ShapeDtypeStruct((*shape, subs, LANES), jnp.float32)

    def scratch(*shape):
        return pltpu.VMEM((*shape, subs, LANES), jnp.float32)

    def call(body, name, ins, outs, out_specs=None, scratches=(), vectors=0):
        return pl.pallas_call(
            body,
            out_shape=outs,
            in_specs=ins,
            out_specs=out_specs or [whole] * len(outs),
            scratch_shapes=list(scratches),
            compiler_params=pltpu.CompilerParams(vmem_limit_bytes=VMEM_LIMIT),
            cost_estimate=pl.CostEstimate(flops=vectors * subs * LANES, bytes_accessed=1 << 20, transcendentals=0),
            name=name,
        )

    swap_a = [(i, i ^ 1) for i in range(tiles) if (i ^ 1) < tiles]
    swap_b = [(i, j) for k in range(1, tiles - 1, 2) for i, j in ((k, k + 1), (k + 1, k))]
    tall = plan.own.stop - plan.start_a
    short = plan.start_a - REACH

    message_a, rows_a, rest, sums_a, inverse_a = call(
        lambda *refs: near_a_kernel(plan, *refs),
        "near_a",
        [anywhere],
        [
            array(1, plies, 4 * REACH), array(plies, REACH + 1, 3, tall), array(plies, 3, short), array(plies, tall),
            array(plies, len(plan.inner_a)),
        ],
        scratches=[pltpu.VMEM(view.shape, jnp.float32), pltpu.SemaphoreType.DMA((plies,))],
        vectors=plies * 1000,
    )(view)
    got_a = lax.ppermute(message_a, "tile", swap_a)

    message_b, rows_b, sums_b, inverse_b, bottom, top = call(
        lambda *refs: near_b_kernel(plan, *refs),
        "near_b",
        [whole] * 3,
        [
            array(1, plies, 4 * REACH), array(plies, REACH + 1, 3, short), array(plies, plan.near_a.start - REACH),
            array(plies, len(plan.inner_b)), array(1, 3, cols), array(1, 3, cols),
        ],
        vectors=plies * 800,
    )(rows_a, rest, sums_a)
    got_b = lax.ppermute(message_b, "tile", swap_b)
    above = lax.ppermute(bottom, "ply", [(i + 1, i) for i in range(slabs - 1)])
    below = lax.ppermute(top, "ply", [(i, i + 1) for i in range(slabs - 1)])

    weight, pair = call(
        lambda *refs: weight_kernel(plan, tiles, *refs),
        "weights",
        [],
        [array(plan.wide), array(len(plan.early) + len(plan.late))],
        vectors=600,
    )()

    force, strain = call(
        lambda *refs: early_kernel(plan, tiles, slabs, *refs),
        "early",
        [scalars] * 3 + [whole] * 11,
        [array(plies, 3, cols), array(plies, REACH + 1, plan.wide - 2 * REACH)],
        scratches=[scratch(REACH + 1, 3, REACH), scratch(len(plan.cross_a))],
        vectors=plies * 2000,
    )(
        angle_index, bond_table, interface_stiffness, got_a, rows_a, rows_b, sums_a, sums_b, inverse_a, inverse_b,
        weight, pair, above, below,
    )

    (out,) = call(
        lambda *refs: late_kernel(plan, tiles, *refs),
        "late",
        [scalars] * 2 + [whole] * 10,
        [jax.ShapeDtypeStruct(view.shape, jnp.float32)],
        out_specs=[anywhere],
        scratches=[
            scratch(REACH + 1, 3, REACH), scratch(len(plan.cross_b)), scratch(REACH + 1, 2 * REACH), scratch(3, cols),
            pltpu.VMEM(view.shape, jnp.float32), pltpu.SemaphoreType.DMA((plies,)),
        ],
        vectors=plies * 1700,
    )(
        angle_index, bond_table, got_b, rows_a, rows_b, sums_b, inverse_a, inverse_b, weight, pair, force, strain,
    )
    return (
        out.reshape(comps, plies, subs, cols, LANES)
        .transpose(0, 1, 3, 2, 4)
        .reshape(comps, plies, cols, length)
    )


def solution(mesh):
    placed = (P(None, "ply", "tile", None), P("ply"), P(), P())
    return jax.shard_map(
        local, mesh=mesh, in_specs=placed, out_specs=P(None, "ply", "tile", None), check_vma=False
    )
```

```python
import math

import jax
import jax.numpy as jnp
from jax import lax
from jax.experimental import pallas as pl
from jax.experimental.pallas import tpu as pltpu
from jax.sharding import PartitionSpec as P

bulk_modulus = 40.0
REACH = 3
LANES = 128
VMEM_LIMIT = 24 * 1024 * 1024
EARLY_COST = 2 * 10**9
MIDDLE_COST = 2 * 10**9


def bond_columns():
    halves = []
    for a in range(-REACH, REACH + 1):
        for b in range(-REACH, REACH + 1):
            if 0 < a * a + b * b <= 9 and (a > 0 or (a == 0 and b > 0)):
                halves.append((a, b))
    columns = {}
    for index, (a, b) in enumerate(halves):
        columns[(a, b)] = index
        columns[(-a, -b)] = index
    return columns


COLUMNS = bond_columns()
BONDS = {0: (1, 2, 3), 1: (-2, -1, 0, 1, 2), 2: (-2, -1, 0, 1, 2), 3: (0,)}


def length_of(a, b):
    return math.sqrt(a * a + b * b)


class Plan:
    def __init__(self, cols):
        self.cols = cols
        self.wide = cols + 2 * REACH
        self.own = range(REACH, REACH + cols)
        self.low = range(0, REACH)
        self.high = range(REACH + cols, self.wide)
        self.near_b = range(REACH, 2 * REACH)
        self.near_a = range(cols, cols + REACH)
        every = [
            (b, a, i)
            for b, offsets in BONDS.items()
            for i in range(self.wide)
            for a in offsets
            if 0 <= i + a < self.wide and (i in self.own or i + a in self.own)
        ]
        inner = [k for k in every if k[2] in self.own and k[2] + k[1] in self.own]
        self.inner = inner
        self.inner_a = [k for k in inner if k[2] in self.near_a or k[2] + k[1] in self.near_a]
        self.inner_b = [k for k in inner if k not in self.inner_a]
        self.cross_a = [k for k in every if max(k[2], k[2] + k[1]) in self.high]
        self.cross_b = [k for k in every if min(k[2], k[2] + k[1]) in self.low]
        self.late = [k for k in every if min(k[2], k[2] + k[1]) < 2 * REACH]
        self.early = [k for k in every if k not in self.late]
        self.inner_early = [k for k in self.early if k in inner]
        self.inner_late = [k for k in self.late if k in inner]
        self.inner_start = self.span(self.inner_early).start
        self.start_a = min(min(k[2], k[2] + k[1]) for k in self.inner_a)


    def span(self, keys):
        ends = [x for _, a, i in keys for x in (i, i + a)]
        return range(min(ends), max(ends) + 1)


class Grid:
    def __init__(self, subs):
        self.subs = subs
        self.lane = lax.broadcasted_iota(jnp.int32, (subs, LANES), 1)
        self.y = lax.broadcasted_iota(jnp.int32, (subs, LANES), 0) * LANES + self.lane
        self.total = subs * LANES
        self.exists = {b: self.y < self.total - b for b in range(1, REACH + 1)}

    def ahead(self, row):
        after = pltpu.roll(row, self.subs - 1, axis=0)
        return {
            b: pltpu.roll(jnp.where(self.lane < b, after, row), LANES - b, axis=1) for b in range(1, REACH + 1)
        }

    def back(self, rows):
        total = None
        for b, row in rows.items():
            before = pltpu.roll(row, 1, axis=0)
            moved = pltpu.roll(jnp.where(self.lane >= LANES - b, before, row), b, axis=1)
            total = moved if total is None else total + moved
        return total

    def ring(self, a):
        total = None
        for b in range(-REACH, REACH + 1):
            if 0 < a * a + b * b <= 9:
                exists = (self.y + b >= 0) & (self.y + b < self.total)
                term = jnp.where(exists, length_of(a, b), 0.0)
                total = term if total is None else total + term
        return total


class Store:
    def __init__(self, *parts):
        self.parts = parts

    def at(self, column, *lead):
        for ref, first, columns, head in self.parts:
            if column in columns:
                return ref, (*head, *lead, column - first)
        raise KeyError(column)

    def get(self, column, *lead):
        ref, index = self.at(column, *lead)
        return ref[index]

    def put(self, column, value, *lead):
        ref, index = self.at(column, *lead)
        ref[index] = value


def frame():
    odd = lax.axis_index("tile") % 2 == 1
    return odd, jnp.where(odd, -1.0, 1.0).astype(jnp.float32)


def sides(tiles):
    tile = lax.axis_index("tile")
    has_a = (tile % 2 == 1) | (tile + 1 < tiles)
    has_b = jnp.where(tile % 2 == 1, tile + 1 < tiles, tile > 0)
    return has_a, has_b


def keep_row(grid, rows, column, row):
    for c in range(3):
        rows.put(column, row[c], 0, c)
        for b, moved in grid.ahead(row[c]).items():
            rows.put(column, moved + float(b) if c == 1 else moved, b, c)


def separation(rows, b, a, i, here):
    there = [rows.get(i + a, b, c) for c in range(3)]
    here_x = here[0] - float(a) if a else here[0]
    return there[0] - here_x, there[1] - here[1], there[2] - here[2]


def by_row(keys):
    groups = {}
    for b, a, i in keys:
        groups.setdefault((b, i), []).append(a)
    return groups.items()


def extension_sums(grid, rows, keys, mask_of, keep):
    sums = {}
    shifted = {}
    for (b, i), offsets in by_row(keys):
        here = [rows.get(i, 0, c) for c in range(3)]
        for a in offsets:
            sep = separation(rows, b, a, i, here)
            q = sep[0] * sep[0] + sep[1] * sep[1] + sep[2] * sep[2]
            r = lax.rsqrt(q)
            keep((b, a, i), r)
            e = q * r - length_of(a, b)
            mask = mask_of(b)
            if mask is not None:
                e = jnp.where(mask, e, 0.0)
            sums[i] = sums[i] + e if i in sums else e
            if b == 0:
                sums[i + a] = sums[i + a] + e if i + a in sums else e
            else:
                key = (i + a, b)
                shifted[key] = shifted[key] + e if key in shifted else e
    for x in sorted({x for x, _ in shifted}):
        total = grid.back({b: shifted[(x, b)] for b in range(1, REACH + 1) if (x, b) in shifted})
        sums[x] = sums[x] + total if x in sums else total
    return sums


def chunk_of(plies, most):
    return max(n for n in range(1, most + 1) if plies % n == 0)


def for_plies(plies, most, body):
    count = chunk_of(plies, most)

    def step(n, carry):
        for k in range(count):
            body(n * count + k)
        return carry

    lax.fori_loop(0, plies // count, step, 0)


def pack_kernel(plan, u_ref, rows_ref, message):
    comps, plies, depth, _ = u_ref.shape
    odd, sign = frame()
    for p in range(plies):
        for x in range(plan.cols):
            at = jnp.where(odd, plan.cols - 1 - x, x)
            for c in range(comps):
                row = u_ref[c, p, pl.ds(at, depth // plan.cols, stride=plan.cols), :]
                row = row * sign if c == 0 else row
                rows_ref[p, c, x] = row
                if x + REACH in plan.near_a:
                    message[0, p, c * REACH + x + REACH - plan.near_a.start] = row


def near_a_kernel(plan, base_ref, thin, rows_ref, sums_ref, inverse_ref, first_ref, second_ref):
    plies = base_ref.shape[0]
    grid = Grid(base_ref.shape[-2])
    slots = {key: n for n, key in enumerate(plan.inner_a)}

    def ply(p):
        rows = Store((rows_ref, plan.start_a, range(plan.start_a, plan.own.stop), (p,)))
        for x in rows.parts[0][2]:
            keep_row(grid, rows, x, [base_ref[p, c, x - REACH] for c in range(3)])

        def keep(key, r):
            inverse_ref[p, slots[key]] = r

        sums = extension_sums(grid, rows, plan.inner_a, grid.exists.get, keep)
        for x in rows.parts[0][2]:
            sums_ref[p, x - plan.start_a] = sums[x]
            if x in plan.near_a:
                thin[0, p, x - plan.near_a.start] = sums[x]

    for_plies(plies, 2, ply)
    upper = lax.axis_index("ply") % 2 == 1
    for c in range(3):
        for x in range(plan.cols):
            low, high = base_ref[0, c, x], base_ref[plies - 1, c, x]
            first_ref[0, c, x] = jnp.where(upper, low, high)
            second_ref[0, c, x] = jnp.where(upper, high, low)


def near_b_kernel(
    plan, base_ref, rows_a_ref, sums_a_ref, rows_ref, sums_ref, inverse_ref
):
    plies = rows_a_ref.shape[0]
    grid = Grid(rows_a_ref.shape[-2])
    slots = {key: n for n, key in enumerate(plan.inner_b)}
    fresh = range(REACH, plan.start_a)
    tall = range(plan.start_a, plan.own.stop)

    def ply(p):
        rows = Store((rows_ref, REACH, fresh, (p,)), (rows_a_ref, plan.start_a, tall, (p,)))
        for x in fresh:
            keep_row(grid, rows, x, [base_ref[p, c, x - REACH] for c in range(3)])

        def keep(key, r):
            inverse_ref[p, slots[key]] = r

        sums = extension_sums(grid, rows, plan.inner_b, grid.exists.get, keep)
        for x in range(REACH, plan.near_a.start):
            total = sums[x] + sums_a_ref[p, x - plan.start_a] if x >= plan.start_a else sums[x]
            sums_ref[p, x - REACH] = total

    for_plies(plies, 2, ply)


def weight_kernel(plan, tiles, weight_ref, pair_ref):
    grid = Grid(weight_ref.shape[-2])
    ones = jnp.ones((grid.subs, LANES), jnp.int32)
    has_a, has_b = (ones * side.astype(jnp.int32) > 0 for side in sides(tiles))
    ring = {a: grid.ring(a) for a in range(REACH + 1)}
    weight = {}
    for x in range(plan.wide):
        mass = ring[0]
        for a in range(-REACH, REACH + 1):
            term = ring[abs(a)]
            if x in plan.own and x + a in plan.low:
                term = jnp.where(has_b, term, 0.0)
            if x in plan.own and x + a in plan.high:
                term = jnp.where(has_a, term, 0.0)
            if a:
                mass = mass + term
        weight[x] = 1.0 / mass
        weight_ref[x] = weight[x]
    moved = {x: {0: weight[x], **grid.ahead(weight[x])} for x in range(plan.wide)}
    for n, (b, a, i) in enumerate(plan.early + plan.late):
        pair_ref[n] = weight[i] + moved[i + a][b]


def constants(odd, table_ref, angle):
    found = {}

    def of(a, b):
        if (a, b) not in found:
            column = COLUMNS[(a, b)]
            mirrored = COLUMNS[(-a, b)]
            at = column if column == mirrored else jnp.where(odd, mirrored, column)
            shear = table_ref[angle, at]
            found[(a, b)] = 3.0 * bulk_modulus - 5.0 * shear, 15.0 / length_of(a, b) * shear
        return found[(a, b)]

    return of


def collect(plan, grid, keys, push_of, force):
    held = {}
    last = {}
    for b, a, i in keys:
        last[(i + a, b)] = i
    for (b, i), offsets in by_row(keys):
        mine = None
        for a in offsets:
            j = i + a
            push = push_of((b, a, i))
            if i in plan.own:
                mine = push if mine is None else [mine[c] + push[c] for c in range(3)]
            if j in plan.own:
                held[(j, b)] = [held[(j, b)][c] + push[c] for c in range(3)] if (j, b) in held else push
        if mine is not None:
            force(i, mine)
        for j, _ in [k for k in held if k[1] == b and last[k] == i]:
            total = held.pop((j, b))
            force(j, [-(grid.back({b: total[c]}) if b else total[c]) for c in range(3)])
    assert not held


def whole_push(rows, strains, factors, inverse, pair, mask_of, key):
    b, a, i = key
    alpha, beta = factors(a, b)
    sep = separation(rows, b, a, i, [rows.get(i, 0, c) for c in range(3)])
    r = inverse(key)
    f = (alpha * r) * (strains.get(i, 0) + strains.get(i + a, b)) + (beta * pair(key)) * (1.0 - length_of(a, b) * r)
    mask = mask_of(b)
    if mask is not None:
        f = jnp.where(mask, f, 0.0)
    return [f * sep[c] for c in range(3)]


def inner_kernel(
    plan, keys, angle_ref, table_ref, after_ref, rows_a_ref, rows_b_ref, inverse_a_ref, inverse_b_ref, pair_ref,
    vector_ref, force_ref,
):
    plies = rows_a_ref.shape[0]
    grid = Grid(rows_a_ref.shape[-2])
    odd, _ = frame()
    in_a = {key: n for n, key in enumerate(plan.inner_a)}
    in_b = {key: n for n, key in enumerate(plan.inner_b)}
    in_pair = {key: n for n, key in enumerate(plan.early + plan.late)}
    in_vector = {key: n for n, key in enumerate(keys)}

    def ply(p):
        rows = Store(
            (rows_b_ref, REACH, range(REACH, plan.start_a), (p,)),
            (rows_a_ref, plan.start_a, range(plan.start_a, plan.own.stop), (p,)),
        )
        factors = constants(odd, table_ref, angle_ref[p])
        span = plan.span(keys)
        started = set()
        def push_of(key):
            b, a, i = key
            alpha, beta = factors(a, b)
            sep = separation(rows, b, a, i, [rows.get(i, 0, c) for c in range(3)])
            r = inverse_a_ref[p, in_a[key]] if key in in_a else inverse_b_ref[p, in_b[key]]
            scale = alpha * r
            f = (beta * pair_ref[in_pair[key]]) * (1.0 - length_of(a, b) * r)
            if b:
                scale = jnp.where(grid.exists[b], scale, 0.0)
                f = jnp.where(grid.exists[b], f, 0.0)
            for c in range(3):
                vector_ref[p, in_vector[key], c] = scale * sep[c]
            return [f * sep[c] for c in range(3)]

        def force(x, values):
            for c in range(3):
                at = (p, c, x - span.start)
                force_ref[at] = force_ref[at] + values[c] if x in started else values[c]
            started.add(x)

        collect(plan, grid, keys, push_of, force)
        assert started == set(span)

    for_plies(plies, 2, ply)


def send_kernel(plan, after_ref, inner_ref, base_ref, message):
    for p in range(base_ref.shape[0]):
        for x in range(REACH):
            for c in range(3):
                message[0, p, c * REACH + x] = base_ref[p, c, x]


def early_kernel(
    plan, tiles, slabs, angle_ref, table_ref, stiff_ref, got_ref, thin_ref, rows_a_ref, rows_b_ref, sums_a_ref,
    sums_b_ref, weight_ref, pair_ref, vector_ref, inner_ref, first_ref, second_ref,
    force_ref, strain_ref, thin, halo_ref, cross_ref,
):
    slab = lax.axis_index("ply")
    upper = slab % 2 == 1
    plies = rows_a_ref.shape[0]
    grid = Grid(rows_a_ref.shape[-2])
    odd, _ = frame()
    in_cross = {key: n for n, key in enumerate(plan.cross_a)}
    in_pair = {key: n for n, key in enumerate(plan.early + plan.late)}
    in_vector = {key: n for n, key in enumerate(plan.inner_early)}
    start = 2 * REACH
    has_a = None
    if tiles % 2:
        has_a = jnp.ones((grid.subs, LANES), jnp.int32) * sides(tiles)[0].astype(jnp.int32) > 0

    def cross_mask(b):
        mask = grid.exists.get(b)
        if has_a is None:
            return mask
        return has_a if mask is None else mask & has_a

    def ply(p):
        rows = Store(
            (rows_b_ref, REACH, range(REACH, plan.start_a), (p,)),
            (rows_a_ref, plan.start_a, range(plan.start_a, plan.own.stop), (p,)),
            (halo_ref, plan.high.start, plan.high, ()),
        )
        strains = Store((strain_ref, start, range(start, plan.wide), (p,)))
        factors = constants(odd, table_ref, angle_ref[p])
        for j in range(REACH):
            row = [got_ref[0, p, c * REACH + j] for c in range(3)]
            keep_row(grid, rows, plan.wide - 1 - j, [-row[0], row[1], row[2]])

        def keep(key, r):
            cross_ref[in_cross[key]] = r

        sums = extension_sums(grid, rows, plan.cross_a, cross_mask, keep)
        for x in range(start, plan.wide):
            if x in plan.high:
                total = thin_ref[0, p, plan.wide - 1 - x]
            elif x >= plan.near_a.start:
                total = sums_a_ref[p, x - plan.start_a]
            else:
                total = sums_b_ref[p, x - REACH]
            if x in sums:
                total = total + sums[x]
            strain = 3.0 * total * (weight_ref[x] * weight_ref[x])
            strains.put(x, strain, 0)
            for b, moved in grid.ahead(strain).items():
                strains.put(x, moved, b)

        layers = slabs * plies
        layer = slab * plies + p
        up = jnp.where(layer < layers - 1, stiff_ref[jnp.minimum(layer, layers - 2)], 0.0)
        down = jnp.where(layer > 0, stiff_ref[jnp.maximum(layer - 1, 0)], 0.0)
        over = Store(*((r, s, cs, (jnp.minimum(p + 1, plies - 1),)) for r, s, cs, _ in rows.parts[:2]))
        under = Store(*((r, s, cs, (jnp.maximum(p - 1, 0),)) for r, s, cs, _ in rows.parts[:2]))
        for x in plan.own:
            for c in range(3):
                here = rows.get(x, 0, c)
                first, second = first_ref[0, c, x - REACH], second_ref[0, c, x - REACH]
                above = jnp.where(p == plies - 1, jnp.where(upper, second, first), over.get(x, 0, c))
                below = jnp.where(p == 0, jnp.where(upper, first, second), under.get(x, 0, c))
                spring = up * (above - here) + down * (below - here)
                start_at = plan.inner_start
                force_ref[p, c, x - REACH] = inner_ref[p, c, x - start_at] + spring if x >= start_at else spring

        def push_of(key):
            if key in in_cross:
                return whole_push(
                    rows, strains, factors, lambda k: cross_ref[in_cross[k]], lambda k: pair_ref[in_pair[k]],
                    cross_mask, key,
                )
            b, a, i = key
            total = strains.get(i, 0) + strains.get(i + a, b)
            return [vector_ref[p, in_vector[key], c] * total for c in range(3)]

        def force(x, values):
            for c in range(3):
                force_ref[p, c, x - REACH] = force_ref[p, c, x - REACH] + values[c]

        collect(plan, grid, plan.early, push_of, force)
        for x in range(REACH):
            thin[0, p, x] = sums_b_ref[p, x]

    for_plies(plies, 2, ply)


def middle_kernel(
    plan, tiles, angle_ref, table_ref, got_ref, rows_a_ref, rows_b_ref, sums_b_ref,
    weight_ref, pair_ref, vector_ref, inner_ref, force_in_ref, strain_a_ref,
    force_ref, cross_ref, sums_ref, halo_ref, inverse_ref, strain_ref,
):
    plies = rows_a_ref.shape[0]
    grid = Grid(rows_a_ref.shape[-2])
    odd, _ = frame()
    in_cross = {key: n for n, key in enumerate(plan.cross_b)}
    in_pair = {key: n for n, key in enumerate(plan.early + plan.late)}
    in_vector = {key: n for n, key in enumerate(plan.inner_late)}
    start = 2 * REACH
    has_b = jnp.ones((grid.subs, LANES), jnp.int32) * sides(tiles)[1].astype(jnp.int32) > 0
    cross_masks = {b: grid.exists[b] & has_b if b else has_b for b in range(REACH + 1)}
    late = plan.span(plan.inner_late)

    def ply(p):
        rows = Store(
            (halo_ref, 0, plan.low, ()),
            (rows_b_ref, REACH, range(REACH, plan.start_a), (p,)),
            (rows_a_ref, plan.start_a, range(plan.start_a, plan.own.stop), (p,)),
        )
        strains = Store(
            (strain_ref, REACH, plan.near_b, ()), (strain_a_ref, start, range(start, plan.wide), (p,))
        )
        factors = constants(odd, table_ref, angle_ref[p])
        for j in range(REACH):
            row = [got_ref[0, p, c * REACH + j] for c in range(3)]
            keep_row(grid, rows, REACH - 1 - j, [-row[0], row[1], row[2]])

        def keep(key, r):
            inverse_ref[in_cross[key]] = r

        sums = extension_sums(grid, rows, plan.cross_b, cross_masks.get, keep)
        for x in plan.low:
            sums_ref[p, x] = sums[x]
        for x in plan.near_b:
            strain = 3.0 * (sums_b_ref[p, x - REACH] + sums[x]) * (weight_ref[x] * weight_ref[x])
            strains.put(x, strain, 0)
            for b, moved in grid.ahead(strain).items():
                strains.put(x, moved, b)
        for c in range(3):
            for x in plan.own:
                value = force_in_ref[p, c, x - REACH]
                force_ref[p, c, x - REACH] = value + inner_ref[p, c, x - REACH] if x in late else value

        def push_of(key):
            b, a, i = key
            if key not in in_cross:
                total = strains.get(i, 0) + strains.get(i + a, b)
                return [vector_ref[p, in_vector[key], c] * total for c in range(3)]
            alpha, beta = factors(a, b)
            sep = separation(rows, b, a, i, [rows.get(i, 0, c) for c in range(3)])
            r = inverse_ref[in_cross[key]]
            scale = jnp.where(cross_masks[b], alpha * r, 0.0)
            rest = (beta * pair_ref[in_pair[key]]) * (1.0 - length_of(a, b) * r)
            known = strains.get(i, 0) if i in plan.own else strains.get(i + a, b)
            f = scale * known + jnp.where(cross_masks[b], rest, 0.0)
            for c in range(3):
                cross_ref[p, in_cross[key], c] = scale * sep[c]
            return [f * sep[c] for c in range(3)]

        def force(x, values):
            for c in range(3):
                force_ref[p, c, x - REACH] = force_ref[p, c, x - REACH] + values[c]

        collect(plan, grid, plan.late, push_of, force)

    for_plies(plies, 2, ply)


def last_kernel(plan, thin_ref, sums_ref, weight_ref, cross_ref, force_in_ref, out_hbm, out_ref, sems):
    plies = force_in_ref.shape[0]
    grid = Grid(force_in_ref.shape[-2])
    odd, sign = frame()
    in_cross = {key: n for n, key in enumerate(plan.cross_b)}

    def copy_out(p):
        return pltpu.make_async_copy(out_ref.at[:, pl.ds(p, 1)], out_hbm.at[:, pl.ds(p, 1)], sems.at[p])

    def ply(p):
        strains = {}
        for x in plan.low:
            strain = 3.0 * (thin_ref[0, p, REACH - 1 - x] + sums_ref[p, x]) * (weight_ref[x] * weight_ref[x])
            strains[x] = {0: strain, **grid.ahead(strain)}
        found = {x: [force_in_ref[p, c, x - REACH] for c in range(3)] for x in plan.own}

        def push_of(key):
            b, a, i = key
            strain = strains[i][0] if i in plan.low else strains[i + a][b]
            return [cross_ref[p, in_cross[key], c] * strain for c in range(3)]

        def force(x, values):
            found[x] = [found[x][c] + values[c] for c in range(3)]

        collect(plan, grid, plan.cross_b, push_of, force)
        for x in plan.own:
            at = jnp.where(odd, plan.cols - 1 - (x - REACH), x - REACH)
            for c in range(3):
                value = found[x][c] * sign if c == 0 else found[x][c]
                out_ref[c, p, pl.ds(at, grid.subs, stride=plan.cols), :] = value

    count = chunk_of(plies, 2)

    def step(n, carry):
        for k in range(count):
            ply(n * count + k)
        for k in range(count):
            copy_out(n * count + k).start()
        return carry

    lax.fori_loop(0, plies // count, step, 0)
    for p in range(plies):
        copy_out(p).wait()


def local(displacement, angle_index, bond_table, interface_stiffness):
    comps, plies, cols, length = displacement.shape
    subs = length // LANES
    tiles = lax.axis_size("tile")
    slabs = lax.axis_size("ply")
    assert length % LANES == 0 and cols >= 2 * REACH
    plan = Plan(cols)
    view = (
        displacement.reshape(comps, plies, cols, subs, LANES)
        .transpose(0, 1, 3, 2, 4)
        .reshape(comps, plies, subs * cols, LANES)
    )
    whole = pl.BlockSpec(memory_space=pltpu.VMEM)
    scalars = pl.BlockSpec(memory_space=pltpu.SMEM)

    def array(*shape):
        return jax.ShapeDtypeStruct((*shape, subs, LANES), jnp.float32)

    def scratch(*shape):
        return pltpu.VMEM((*shape, subs, LANES), jnp.float32)

    def call(body, name, ins, outs, out_specs=None, scratches=(), cost=1):
        return pl.pallas_call(
            body,
            out_shape=outs,
            in_specs=ins,
            out_specs=out_specs or [whole] * len(outs),
            scratch_shapes=list(scratches),
            compiler_params=pltpu.CompilerParams(vmem_limit_bytes=VMEM_LIMIT),
            cost_estimate=pl.CostEstimate(flops=cost, bytes_accessed=1, transcendentals=0),
            name=name,
        )

    swap_a = [(i, i ^ 1) for i in range(tiles) if (i ^ 1) < tiles]
    swap_b = []
    for slab in range(slabs):
        for tile in range(tiles):
            other = tile + 1 if tile % 2 else tile - 1
            if 0 <= other < tiles:
                swap_b.append((slab * tiles + tile, slab * tiles + other))
            elif (slab ^ 1) < slabs:
                swap_b.append((slab * tiles + tile, (slab ^ 1) * tiles + tile))
    swap_first = [(i, i ^ 1) for i in range(slabs) if (i ^ 1) < slabs]
    swap_second = [(i, j) for k in range(1, slabs - 1, 2) for i, j in ((k, k + 1), (k + 1, k))]
    if slabs % 2 == 0:
        swap_second += [(0, slabs - 1), (slabs - 1, 0)]
    tall = plan.own.stop - plan.start_a
    short = plan.start_a - REACH

    base, message_a = call(
        lambda *refs: pack_kernel(plan, *refs),
        "pack",
        [whole],
        [array(plies, 3, cols), array(1, plies, 3 * REACH)],
    )(view)
    got_a = lax.ppermute(message_a, "tile", swap_a)

    thin_a, rows_a, sums_a, inverse_a, first, second = call(
        lambda *refs: near_a_kernel(plan, *refs),
        "near_a",
        [whole],
        [
            array(1, plies, REACH), array(plies, REACH + 1, 3, tall), array(plies, tall),
            array(plies, len(plan.inner_a)), array(1, 3, cols), array(1, 3, cols),
        ],
    )(base)
    got_thin_a = lax.ppermute(thin_a, "tile", swap_a)
    got_first = lax.ppermute(first, "ply", swap_first)
    got_second = lax.ppermute(second, "ply", swap_second)

    rows_b, sums_b, inverse_b = call(
        lambda *refs: near_b_kernel(plan, *refs),
        "near_b",
        [whole] * 3,
        [
            array(plies, REACH + 1, 3, short), array(plies, plan.near_a.start - REACH),
            array(plies, len(plan.inner_b)),
        ],
    )(base, rows_a, sums_a)

    weight, pair = call(
        lambda *refs: weight_kernel(plan, tiles, *refs),
        "weights",
        [],
        [array(plan.wide), array(len(plan.early) + len(plan.late))],
    )()

    def inner_part(keys, name, after):
        return call(
            lambda *refs: inner_kernel(plan, keys, *refs),
            name,
            [scalars] * 2 + [whole] * 6,
            [array(plies, len(keys), 3), array(plies, 3, len(plan.span(keys)))],
        )(angle_index, bond_table, after, rows_a, rows_b, inverse_a, inverse_b, pair)

    vector_late, inner_late = inner_part(plan.inner_late, "inner_late", got_first)
    (message_b,) = call(
        lambda *refs: send_kernel(plan, *refs),
        "send",
        [whole] * 3,
        [array(1, plies, 3 * REACH)],
    )(got_a, inner_late, base)
    got_b = lax.ppermute(message_b, ("ply", "tile"), swap_b)
    vector_early, inner_early = inner_part(plan.inner_early, "inner_early", message_b)

    force, strain, thin_b = call(
        lambda *refs: early_kernel(plan, tiles, slabs, *refs),
        "early",
        [scalars] * 3 + [whole] * 12,
        [array(plies, 3, cols), array(plies, REACH + 1, plan.wide - 2 * REACH), array(1, plies, REACH)],
        cost=EARLY_COST,
        scratches=[scratch(REACH + 1, 3, REACH), scratch(len(plan.cross_a))],
    )(
        angle_index, bond_table, interface_stiffness, got_a, got_thin_a, rows_a, rows_b, sums_a, sums_b,
        weight, pair, vector_early, inner_early, got_first, got_second,
    )
    got_thin_b = lax.ppermute(thin_b, ("ply", "tile"), swap_b)

    force, cross, sums_low = call(
        lambda *refs: middle_kernel(plan, tiles, *refs),
        "middle",
        [scalars] * 2 + [whole] * 10,
        [array(plies, 3, cols), array(plies, len(plan.cross_b), 3), array(plies, REACH)],
        cost=MIDDLE_COST,
        scratches=[scratch(REACH + 1, 3, REACH), scratch(len(plan.cross_b)), scratch(REACH + 1, REACH)],
    )(angle_index, bond_table, got_b, rows_a, rows_b, sums_b, weight, pair, vector_late, inner_late, force, strain)

    (out,) = call(
        lambda *refs: last_kernel(plan, *refs),
        "last",
        [whole] * 5,
        [jax.ShapeDtypeStruct(view.shape, jnp.float32)],
        out_specs=[pl.BlockSpec(memory_space=pltpu.HBM)],
        scratches=[pltpu.VMEM(view.shape, jnp.float32), pltpu.SemaphoreType.DMA((plies,))],
    )(got_thin_b, sums_low, weight, cross, force)
    return (
        out.reshape(comps, plies, subs, cols, LANES)
        .transpose(0, 1, 3, 2, 4)
        .reshape(comps, plies, cols, length)
    )


def solution(mesh):
    placed = (P(None, "ply", "tile", None), P("ply"), P(), P())
    return jax.shard_map(
        local, mesh=mesh, in_specs=placed, out_specs=P(None, "ply", "tile", None), check_vma=False
    )
```

```python
import math

import jax
import jax.numpy as jnp
from jax import lax
from jax.experimental import pallas as pl
from jax.experimental.pallas import tpu as pltpu
from jax.sharding import PartitionSpec as P

bulk_modulus = 40.0
REACH = 3
LANES = 128
VMEM_LIMIT = 24 * 1024 * 1024
EARLY_COST = 2 * 10**9
LATE_COST = 2 * 10**9


def bond_columns():
    halves = []
    for a in range(-REACH, REACH + 1):
        for b in range(-REACH, REACH + 1):
            if 0 < a * a + b * b <= 9 and (a > 0 or (a == 0 and b > 0)):
                halves.append((a, b))
    columns = {}
    for index, (a, b) in enumerate(halves):
        columns[(a, b)] = index
        columns[(-a, -b)] = index
    return columns


COLUMNS = bond_columns()
BONDS = {0: (1, 2, 3), 1: (-2, -1, 0, 1, 2), 2: (-2, -1, 0, 1, 2), 3: (0,)}


OFFSETS = [(a, b) for b, offsets in BONDS.items() for a in offsets]


def length_of(a, b):
    return math.sqrt(a * a + b * b)


class Plan:
    def __init__(self, cols):
        self.cols = cols
        self.wide = cols + 2 * REACH
        self.own = range(REACH, REACH + cols)
        self.low = range(0, REACH)
        self.high = range(REACH + cols, self.wide)
        self.near_b = range(REACH, 2 * REACH)
        self.near_a = range(cols, cols + REACH)
        every = [
            (b, a, i)
            for b, offsets in BONDS.items()
            for i in range(self.wide)
            for a in offsets
            if 0 <= i + a < self.wide and (i in self.own or i + a in self.own)
        ]
        inner = [k for k in every if k[2] in self.own and k[2] + k[1] in self.own]
        self.inner = inner
        self.inner_a = [k for k in inner if k[2] in self.near_a or k[2] + k[1] in self.near_a]
        self.inner_b = [k for k in inner if k not in self.inner_a]
        self.cross_a = [k for k in every if max(k[2], k[2] + k[1]) in self.high]
        self.cross_b = [k for k in every if min(k[2], k[2] + k[1]) in self.low]
        self.late = [k for k in every if min(k[2], k[2] + k[1]) < 2 * REACH]
        self.early = [k for k in every if k not in self.late]
        self.inner_early = [k for k in self.early if k in inner]
        self.inner_late = [k for k in self.late if k in inner]
        self.inner_start = self.span(self.inner_early).start
        self.start_a = min(min(k[2], k[2] + k[1]) for k in self.inner_a)


    def span(self, keys):
        ends = [x for _, a, i in keys for x in (i, i + a)]
        return range(min(ends), max(ends) + 1)


class Grid:
    def __init__(self, subs):
        self.subs = subs
        self.lane = lax.broadcasted_iota(jnp.int32, (subs, LANES), 1)
        self.y = lax.broadcasted_iota(jnp.int32, (subs, LANES), 0) * LANES + self.lane
        self.total = subs * LANES
        self.exists = {b: self.y < self.total - b for b in range(1, REACH + 1)}

    def ahead(self, row):
        after = pltpu.roll(row, self.subs - 1, axis=0)
        return {
            b: pltpu.roll(jnp.where(self.lane < b, after, row), LANES - b, axis=1) for b in range(1, REACH + 1)
        }

    def back(self, rows):
        total = None
        for b, row in rows.items():
            before = pltpu.roll(row, 1, axis=0)
            moved = pltpu.roll(jnp.where(self.lane >= LANES - b, before, row), b, axis=1)
            total = moved if total is None else total + moved
        return total

    def ring(self, a):
        total = None
        for b in range(-REACH, REACH + 1):
            if 0 < a * a + b * b <= 9:
                exists = (self.y + b >= 0) & (self.y + b < self.total)
                term = jnp.where(exists, length_of(a, b), 0.0)
                total = term if total is None else total + term
        return total


class Store:
    def __init__(self, *parts):
        self.parts = parts

    def at(self, column, *lead):
        for ref, first, columns, head in self.parts:
            if column in columns:
                return ref, (*head, *lead, column - first)
        raise KeyError(column)

    def get(self, column, *lead):
        ref, index = self.at(column, *lead)
        return ref[index]

    def put(self, column, value, *lead):
        ref, index = self.at(column, *lead)
        ref[index] = value


def frame():
    odd = lax.axis_index("tile") % 2 == 1
    return odd, jnp.where(odd, -1.0, 1.0).astype(jnp.float32)


def sides(tiles):
    tile = lax.axis_index("tile")
    has_a = (tile % 2 == 1) | (tile + 1 < tiles)
    has_b = jnp.where(tile % 2 == 1, tile + 1 < tiles, tile > 0)
    return has_a, has_b


def keep_row(grid, rows, column, row):
    for c in range(3):
        rows.put(column, row[c], 0, c)
        for b, moved in grid.ahead(row[c]).items():
            rows.put(column, moved + float(b) if c == 1 else moved, b, c)


def separation(rows, b, a, i, here):
    there = [rows.get(i + a, b, c) for c in range(3)]
    here_x = here[0] - float(a) if a else here[0]
    return there[0] - here_x, there[1] - here[1], there[2] - here[2]


def by_row(keys):
    groups = {}
    for b, a, i in keys:
        groups.setdefault((b, i), []).append(a)
    return groups.items()


def extension_sums(grid, rows, keys, mask_of, keep):
    sums = {}
    shifted = {}
    for (b, i), offsets in by_row(keys):
        here = [rows.get(i, 0, c) for c in range(3)]
        for a in offsets:
            sep = separation(rows, b, a, i, here)
            q = sep[0] * sep[0] + sep[1] * sep[1] + sep[2] * sep[2]
            r = lax.rsqrt(q)
            keep((b, a, i), r)
            e = q * r - length_of(a, b)
            mask = mask_of(b)
            if mask is not None:
                e = jnp.where(mask, e, 0.0)
            sums[i] = sums[i] + e if i in sums else e
            if b == 0:
                sums[i + a] = sums[i + a] + e if i + a in sums else e
            else:
                key = (i + a, b)
                shifted[key] = shifted[key] + e if key in shifted else e
    for x in sorted({x for x, _ in shifted}):
        total = grid.back({b: shifted[(x, b)] for b in range(1, REACH + 1) if (x, b) in shifted})
        sums[x] = sums[x] + total if x in sums else total
    return sums


def chunk_of(plies, most):
    return max(n for n in range(1, most + 1) if plies % n == 0)


def for_plies(plies, most, body):
    count = chunk_of(plies, most)

    def step(n, carry):
        for k in range(count):
            body(n * count + k)
        return carry

    lax.fori_loop(0, plies // count, step, 0)


def pack_kernel(plan, u_ref, rows_ref, message):
    comps, plies, depth, _ = u_ref.shape
    odd, sign = frame()
    for p in range(plies):
        for x in range(plan.cols):
            at = jnp.where(odd, plan.cols - 1 - x, x)
            for c in range(comps):
                row = u_ref[c, p, pl.ds(at, depth // plan.cols, stride=plan.cols), :]
                row = row * sign if c == 0 else row
                rows_ref[p, c, x] = row
                if x + REACH in plan.near_a and c < 2:
                    message[0, p, c * REACH + x + REACH - plan.near_a.start] = row


def near_a_kernel(plan, base_ref, message, rows_ref, sums_ref, inverse_ref, first_ref, second_ref):
    plies = base_ref.shape[0]
    grid = Grid(base_ref.shape[-2])
    slots = {key: n for n, key in enumerate(plan.inner_a)}

    def ply(p):
        rows = Store((rows_ref, plan.start_a, range(plan.start_a, plan.own.stop), (p,)))
        for x in rows.parts[0][2]:
            keep_row(grid, rows, x, [base_ref[p, c, x - REACH] for c in range(3)])

        def keep(key, r):
            inverse_ref[p, slots[key]] = r

        sums = extension_sums(grid, rows, plan.inner_a, grid.exists.get, keep)
        for x in rows.parts[0][2]:
            sums_ref[p, x - plan.start_a] = sums[x]
            if x in plan.near_a:
                message[0, p, x - plan.near_a.start] = base_ref[p, 2, x - REACH]
                message[0, p, REACH + x - plan.near_a.start] = sums[x]

    for_plies(plies, 2, ply)
    upper = lax.axis_index("ply") % 2 == 1
    for c in range(3):
        for x in range(plan.cols):
            low, high = base_ref[0, c, x], base_ref[plies - 1, c, x]
            first_ref[0, c, x] = jnp.where(upper, low, high)
            second_ref[0, c, x] = jnp.where(upper, high, low)


def near_b_kernel(
    plan, base_ref, rows_a_ref, sums_a_ref, rows_ref, sums_ref, inverse_ref
):
    plies = rows_a_ref.shape[0]
    grid = Grid(rows_a_ref.shape[-2])
    slots = {key: n for n, key in enumerate(plan.inner_b)}
    fresh = range(REACH, plan.start_a)
    tall = range(plan.start_a, plan.own.stop)

    def ply(p):
        rows = Store((rows_ref, REACH, fresh, (p,)), (rows_a_ref, plan.start_a, tall, (p,)))
        for x in fresh:
            keep_row(grid, rows, x, [base_ref[p, c, x - REACH] for c in range(3)])

        def keep(key, r):
            inverse_ref[p, slots[key]] = r

        sums = extension_sums(grid, rows, plan.inner_b, grid.exists.get, keep)
        for x in range(REACH, plan.near_a.start):
            total = sums[x] + sums_a_ref[p, x - plan.start_a] if x >= plan.start_a else sums[x]
            sums_ref[p, x - REACH] = total

    for_plies(plies, 2, ply)


def weight_kernel(
    plan, tiles, slabs, angle_ref, table_ref, stiff_ref, after_ref, weight_ref, pair_ref, factor_ref, spring_ref
):
    plies = factor_ref.shape[0]
    odd, _ = frame()
    slab = lax.axis_index("ply")
    layers = slabs * plies

    def fill(ref, at, value):
        ref[at] = jnp.full(ref.shape[-2:], value, jnp.float32)

    for p in range(plies):
        for n, (a, b) in enumerate(OFFSETS):
            column = COLUMNS[(a, b)]
            mirrored = COLUMNS[(-a, b)]
            shear = table_ref[angle_ref[p], column if column == mirrored else jnp.where(odd, mirrored, column)]
            fill(factor_ref, (p, 2 * n), 3.0 * bulk_modulus - 5.0 * shear)
            fill(factor_ref, (p, 2 * n + 1), 15.0 / length_of(a, b) * shear)
        layer = slab * plies + p
        up = jnp.where(layer < layers - 1, stiff_ref[jnp.minimum(layer, layers - 2)], 0.0)
        down = jnp.where(layer > 0, stiff_ref[jnp.maximum(layer - 1, 0)], 0.0)
        fill(spring_ref, (p, 0), up)
        fill(spring_ref, (p, 1), down)
        fill(spring_ref, (p, 2), up if p < plies - 1 else 0.0)
        fill(spring_ref, (p, 3), down if p > 0 else 0.0)
    grid = Grid(weight_ref.shape[-2])
    ones = jnp.ones((grid.subs, LANES), jnp.int32)
    has_a, has_b = (ones * side.astype(jnp.int32) > 0 for side in sides(tiles))
    ring = {a: grid.ring(a) for a in range(REACH + 1)}
    weight = {}
    for x in range(plan.wide):
        mass = ring[0]
        for a in range(-REACH, REACH + 1):
            term = ring[abs(a)]
            if x in plan.own and x + a in plan.low:
                term = jnp.where(has_b, term, 0.0)
            if x in plan.own and x + a in plan.high:
                term = jnp.where(has_a, term, 0.0)
            if a:
                mass = mass + term
        weight[x] = 1.0 / mass
        weight_ref[x] = weight[x]
    moved = {x: {0: weight[x], **grid.ahead(weight[x])} for x in range(plan.wide)}
    for n, (b, a, i) in enumerate(plan.early + plan.late):
        pair_ref[n] = weight[i] + moved[i + a][b]


def factors_of(factor_ref, p):
    def of(a, b):
        n = OFFSETS.index((a, b))
        return factor_ref[p, 2 * n], factor_ref[p, 2 * n + 1]

    return of


def collect(plan, grid, keys, push_of, force):
    held = {}
    last = {}
    for b, a, i in keys:
        last[(i + a, b)] = i
    for (b, i), offsets in by_row(keys):
        mine = None
        for a in offsets:
            j = i + a
            push = push_of((b, a, i))
            if i in plan.own:
                mine = push if mine is None else [mine[c] + push[c] for c in range(3)]
            if j in plan.own:
                held[(j, b)] = [held[(j, b)][c] + push[c] for c in range(3)] if (j, b) in held else push
        if mine is not None:
            force(i, mine)
        for j, _ in [k for k in held if k[1] == b and last[k] == i]:
            total = held.pop((j, b))
            force(j, [-(grid.back({b: total[c]}) if b else total[c]) for c in range(3)])
    assert not held


def whole_push(rows, strains, factors, inverse, pair, mask_of, key):
    b, a, i = key
    alpha, beta = factors(a, b)
    sep = separation(rows, b, a, i, [rows.get(i, 0, c) for c in range(3)])
    r = inverse(key)
    f = (alpha * r) * (strains.get(i, 0) + strains.get(i + a, b)) + (beta * pair(key)) * (1.0 - length_of(a, b) * r)
    mask = mask_of(b)
    if mask is not None:
        f = jnp.where(mask, f, 0.0)
    return [f * sep[c] for c in range(3)]


def inner_kernel(
    plan, after_ref, factor_ref, rows_a_ref, rows_b_ref, inverse_a_ref, inverse_b_ref, pair_ref, vector_ref, force_ref
):
    keys = plan.inner_late
    plies = rows_a_ref.shape[0]
    grid = Grid(rows_a_ref.shape[-2])
    in_a = {key: n for n, key in enumerate(plan.inner_a)}
    in_b = {key: n for n, key in enumerate(plan.inner_b)}
    in_pair = {key: n for n, key in enumerate(plan.early + plan.late)}
    in_vector = {key: n for n, key in enumerate(keys)}

    def ply(p):
        rows = Store(
            (rows_b_ref, REACH, range(REACH, plan.start_a), (p,)),
            (rows_a_ref, plan.start_a, range(plan.start_a, plan.own.stop), (p,)),
        )
        factors = factors_of(factor_ref, p)
        span = plan.span(keys)
        started = set()
        def push_of(key):
            b, a, i = key
            alpha, beta = factors(a, b)
            sep = separation(rows, b, a, i, [rows.get(i, 0, c) for c in range(3)])
            r = inverse_a_ref[p, in_a[key]] if key in in_a else inverse_b_ref[p, in_b[key]]
            scale = alpha * r
            f = (beta * pair_ref[in_pair[key]]) * (1.0 - length_of(a, b) * r)
            if b:
                scale = jnp.where(grid.exists[b], scale, 0.0)
                f = jnp.where(grid.exists[b], f, 0.0)
            for c in range(3):
                vector_ref[p, in_vector[key], c] = scale * sep[c]
            return [f * sep[c] for c in range(3)]

        def force(x, values):
            for c in range(3):
                at = (p, c, x - span.start)
                force_ref[at] = force_ref[at] + values[c] if x in started else values[c]
            started.add(x)

        collect(plan, grid, keys, push_of, force)
        assert started == set(span)

    for_plies(plies, 2, ply)


def send_kernel(plan, part, after_ref, base_ref, sums_b_ref, message):
    for p in part:
        for x in range(REACH):
            message[0, p - part.start, 3 * REACH + x] = sums_b_ref[p, x]
            for c in range(3):
                message[0, p - part.start, c * REACH + x] = base_ref[p, c, x]


def strain_kernel(
    plan, tiles, after_ref, got_ref, got_more_ref, rows_a_ref, rows_b_ref, sums_a_ref, sums_b_ref, weight_ref,
    halo_ref, strain_ref, inverse_ref,
):
    plies = rows_a_ref.shape[0]
    grid = Grid(rows_a_ref.shape[-2])
    in_cross = {key: n for n, key in enumerate(plan.cross_a)}
    start = 2 * REACH
    mask_of = cross_mask_a(grid, tiles)

    def ply(p):
        rows = Store(
            (rows_b_ref, REACH, range(REACH, plan.start_a), (p,)),
            (rows_a_ref, plan.start_a, range(plan.start_a, plan.own.stop), (p,)),
            (halo_ref, plan.high.start, plan.high, (p,)),
        )
        strains = Store((strain_ref, start, range(start, plan.wide), (p,)))
        for j in range(REACH):
            row = [got_ref[0, p, j], got_ref[0, p, REACH + j], got_more_ref[0, p, j]]
            keep_row(grid, rows, plan.wide - 1 - j, [-row[0], row[1], row[2]])

        def keep(key, r):
            inverse_ref[p, in_cross[key]] = r

        sums = extension_sums(grid, rows, plan.cross_a, mask_of, keep)
        for x in range(start, plan.wide):
            if x in plan.high:
                total = got_more_ref[0, p, REACH + plan.wide - 1 - x]
            elif x >= plan.near_a.start:
                total = sums_a_ref[p, x - plan.start_a]
            else:
                total = sums_b_ref[p, x - REACH]
            if x in sums:
                total = total + sums[x]
            strain = 3.0 * total * (weight_ref[x] * weight_ref[x])
            strains.put(x, strain, 0)
            for b, moved in grid.ahead(strain).items():
                strains.put(x, moved, b)

    for_plies(plies, 2, ply)


def cross_mask_a(grid, tiles):
    if tiles % 2 == 0:
        return grid.exists.get
    has_a = jnp.ones((grid.subs, LANES), jnp.int32) * sides(tiles)[0].astype(jnp.int32) > 0
    return {b: grid.exists[b] & has_a if b else has_a for b in range(REACH + 1)}.get


def early_kernel(
    plan, tiles, rows_a_ref, rows_b_ref, halo_ref, strain_ref, inverse_ref, inverse_a_ref, inverse_b_ref, pair_ref,
    factor_ref, spring_ref, force_ref,
):
    plies = rows_a_ref.shape[0]
    grid = Grid(rows_a_ref.shape[-2])
    in_a = {key: n for n, key in enumerate(plan.inner_a)}
    in_b = {key: n for n, key in enumerate(plan.inner_b)}
    in_cross = {key: n for n, key in enumerate(plan.cross_a)}
    in_pair = {key: n for n, key in enumerate(plan.early + plan.late)}
    start = 2 * REACH
    cross_mask = cross_mask_a(grid, tiles)

    def ply(p):
        def rows_of(q, *more):
            return Store(
                (rows_b_ref, REACH, range(REACH, plan.start_a), (q,)),
                (rows_a_ref, plan.start_a, range(plan.start_a, plan.own.stop), (q,)),
                *more,
            )

        rows = rows_of(p, (halo_ref, plan.high.start, plan.high, (p,)))
        strains = Store((strain_ref, start, range(start, plan.wide), (p,)))
        factors = factors_of(factor_ref, p)
        up, down = spring_ref[p, 2], spring_ref[p, 3]
        over, under = rows_of(jnp.minimum(p + 1, plies - 1)), rows_of(jnp.maximum(p - 1, 0))
        for x in plan.own:
            for c in range(3):
                here = rows.get(x, 0, c)
                spring = up * (over.get(x, 0, c) - here) + down * (under.get(x, 0, c) - here)
                force_ref[p, c, x - REACH] = spring

        def inverse(key):
            if key in in_cross:
                return inverse_ref[p, in_cross[key]]
            return inverse_a_ref[p, in_a[key]] if key in in_a else inverse_b_ref[p, in_b[key]]

        def push_of(key):
            mask_of = cross_mask if key in in_cross else grid.exists.get
            return whole_push(rows, strains, factors, inverse, lambda k: pair_ref[in_pair[k]], mask_of, key)

        def force(x, values):
            for c in range(3):
                force_ref[p, c, x - REACH] = force_ref[p, c, x - REACH] + values[c]

        collect(plan, grid, plan.early, push_of, force)

    for_plies(plies, 2, ply)


def late_kernel(
    plan, tiles, part, final, first_ref, second_ref, got_ref, rows_a_ref, rows_b_ref, sums_b_ref, weight_ref, pair_ref,
    factor_ref, spring_ref, vector_ref, inner_ref, force_in_ref, strain_a_ref, *rest,
):
    if final:
        before_ref, out_hbm, halo_ref, cross_ref, strain_ref, force_ref, out_ref, sems, before_sem = rest
        copy_before = pltpu.make_async_copy(before_ref, out_hbm.at[:, pl.ds(0, part.start)], before_sem)
        copy_before.start()
    else:
        out_ref, halo_ref, cross_ref, strain_ref, force_ref = rest
    plies = rows_a_ref.shape[0]
    grid = Grid(rows_a_ref.shape[-2])
    odd, sign = frame()
    upper = lax.axis_index("ply") % 2 == 1
    in_cross = {key: n for n, key in enumerate(plan.cross_b)}
    in_pair = {key: n for n, key in enumerate(plan.early + plan.late)}
    in_vector = {key: n for n, key in enumerate(plan.inner_late)}
    start = 2 * REACH
    has_b = jnp.ones((grid.subs, LANES), jnp.int32) * sides(tiles)[1].astype(jnp.int32) > 0
    cross_masks = {b: grid.exists[b] & has_b if b else has_b for b in range(REACH + 1)}
    late = plan.span(plan.inner_late)

    def copy_out(p):
        return pltpu.make_async_copy(
            out_ref.at[:, pl.ds(p - part.start, 1)], out_hbm.at[:, pl.ds(p, 1)], sems.at[p - part.start]
        )

    def ply(p):
        n = p - part.start
        rows = Store(
            (halo_ref, 0, plan.low, (n,)),
            (rows_b_ref, REACH, range(REACH, plan.start_a), (p,)),
            (rows_a_ref, plan.start_a, range(plan.start_a, plan.own.stop), (p,)),
        )
        strains = Store(
            (strain_ref, 0, range(start), (n,)), (strain_a_ref, start, range(start, plan.wide), (p,))
        )
        factors = factors_of(factor_ref, p)
        for j in range(REACH):
            row = [got_ref[0, n, c * REACH + j] for c in range(3)]
            keep_row(grid, rows, REACH - 1 - j, [-row[0], row[1], row[2]])

        def keep(key, r):
            cross_ref[n, in_cross[key]] = r

        sums = extension_sums(grid, rows, plan.cross_b, cross_masks.get, keep)
        for x in range(start):
            total = got_ref[0, n, 3 * REACH + REACH - 1 - x] if x in plan.low else sums_b_ref[p, x - REACH]
            strain = 3.0 * (total + sums[x]) * (weight_ref[x] * weight_ref[x])
            strains.put(x, strain, 0)
            for b, moved in grid.ahead(strain).items():
                strains.put(x, moved, b)
        faces = []
        if p == plies - 1:
            faces.append((spring_ref[p, 0], second_ref, first_ref))
        if p == 0:
            faces.append((spring_ref[p, 1], first_ref, second_ref))
        for c in range(3):
            for x in plan.own:
                value = force_in_ref[p, c, x - REACH]
                if x in late:
                    value = value + inner_ref[p, c, x - REACH]
                for factor, one, two in faces:
                    beyond = jnp.where(upper, one[0, c, x - REACH], two[0, c, x - REACH])
                    value = value + factor * (beyond - rows.get(x, 0, c))
                force_ref[n, c, x - REACH] = value

        def push_of(key):
            if key in in_cross:
                return whole_push(
                    rows, strains, factors, lambda k: cross_ref[n, in_cross[k]], lambda k: pair_ref[in_pair[k]],
                    cross_masks.get, key,
                )
            b, a, i = key
            total = strains.get(i, 0) + strains.get(i + a, b)
            return [vector_ref[p, in_vector[key], c] * total for c in range(3)]

        def force(x, values):
            for c in range(3):
                force_ref[n, c, x - REACH] = force_ref[n, c, x - REACH] + values[c]

        collect(plan, grid, plan.late, push_of, force)
        for x in plan.own:
            at = jnp.where(odd, plan.cols - 1 - (x - REACH), x - REACH)
            for c in range(3):
                value = force_ref[n, c, x - REACH]
                out_ref[c, n, pl.ds(at, grid.subs, stride=plan.cols), :] = value * sign if c == 0 else value

    for first in range(part.start, part.stop, 2):
        group = range(first, min(first + 2, part.stop))
        for p in group:
            ply(p)
        if final:
            for p in group:
                copy_out(p).start()
    if final:
        copy_before.wait()
        for p in part:
            copy_out(p).wait()


def local(displacement, angle_index, bond_table, interface_stiffness):
    comps, plies, cols, length = displacement.shape
    subs = length // LANES
    tiles = lax.axis_size("tile")
    slabs = lax.axis_size("ply")
    assert length % LANES == 0 and cols >= 2 * REACH
    plan = Plan(cols)
    view = (
        displacement.reshape(comps, plies, cols, subs, LANES)
        .transpose(0, 1, 3, 2, 4)
        .reshape(comps, plies, subs * cols, LANES)
    )
    whole = pl.BlockSpec(memory_space=pltpu.VMEM)
    scalars = pl.BlockSpec(memory_space=pltpu.SMEM)

    def array(*shape):
        return jax.ShapeDtypeStruct((*shape, subs, LANES), jnp.float32)

    def scratch(*shape):
        return pltpu.VMEM((*shape, subs, LANES), jnp.float32)

    def call(body, name, ins, outs, out_specs=None, scratches=(), cost=1):
        return pl.pallas_call(
            body,
            out_shape=outs,
            in_specs=ins,
            out_specs=out_specs or [whole] * len(outs),
            scratch_shapes=list(scratches),
            compiler_params=pltpu.CompilerParams(vmem_limit_bytes=VMEM_LIMIT),
            cost_estimate=pl.CostEstimate(flops=cost, bytes_accessed=1, transcendentals=0),
            name=name,
        )

    swap_a = [(i, i ^ 1) for i in range(tiles) if (i ^ 1) < tiles]
    swap_b = []
    for slab in range(slabs):
        for tile in range(tiles):
            other = tile + 1 if tile % 2 else tile - 1
            if 0 <= other < tiles:
                swap_b.append((slab * tiles + tile, slab * tiles + other))
            elif (slab ^ 1) < slabs:
                swap_b.append((slab * tiles + tile, (slab ^ 1) * tiles + tile))
    swap_first = [(i, i ^ 1) for i in range(slabs) if (i ^ 1) < slabs]
    swap_second = [(i, j) for k in range(1, slabs - 1, 2) for i, j in ((k, k + 1), (k + 1, k))]
    if slabs % 2 == 0:
        swap_second += [(0, slabs - 1), (slabs - 1, 0)]
    tall = plan.own.stop - plan.start_a
    short = plan.start_a - REACH

    base, message_a = call(
        lambda *refs: pack_kernel(plan, *refs),
        "pack",
        [whole],
        [array(plies, 3, cols), array(1, plies, 2 * REACH)],
    )(view)
    got_a = lax.ppermute(message_a, "tile", swap_a)

    more_a, rows_a, sums_a, inverse_a, first, second = call(
        lambda *refs: near_a_kernel(plan, *refs),
        "near_a",
        [whole],
        [
            array(1, plies, 2 * REACH), array(plies, REACH + 1, 3, tall), array(plies, tall),
            array(plies, len(plan.inner_a)), array(1, 3, cols), array(1, 3, cols),
        ],
    )(base)
    got_more_a = lax.ppermute(more_a, "tile", swap_a)
    got_second = lax.ppermute(second, "ply", swap_second)
    got_first = lax.ppermute(first, "ply", swap_first)

    rows_b, sums_b, inverse_b = call(
        lambda *refs: near_b_kernel(plan, *refs),
        "near_b",
        [whole] * 3,
        [
            array(plies, REACH + 1, 3, short), array(plies, plan.near_a.start - REACH),
            array(plies, len(plan.inner_b)),
        ],
    )(base, rows_a, sums_a)

    weight, pair, factor, spring = call(
        lambda *refs: weight_kernel(plan, tiles, slabs, *refs),
        "weights",
        [scalars] * 3 + [whole],
        [
            array(plan.wide), array(len(plan.early) + len(plan.late)), array(plies, 2 * len(OFFSETS)),
            array(plies, 4),
        ],
    )(angle_index, bond_table, interface_stiffness, got_first)

    vector_late, inner_late = call(
        lambda *refs: inner_kernel(plan, *refs),
        "inner",
        [whole] * 7,
        [array(plies, len(plan.inner_late), 3), array(plies, 3, len(plan.span(plan.inner_late)))],
    )(got_second, factor, rows_a, rows_b, inverse_a, inverse_b, pair)

    count = plies - plies // 3
    parts = [range(count), range(count, plies)]
    def send_part(part, name, after):
        (message,) = call(
            lambda *refs: send_kernel(plan, part, *refs), name, [whole] * 3, [array(1, len(part), 4 * REACH)]
        )(after, base, sums_b)
        return message, lax.ppermute(message, ("ply", "tile"), swap_b)

    message_b, got = send_part(parts[0], "send", got_a)
    got_b = [got]
    message_b, got = send_part(parts[1], "send_rest", inner_late)
    got_b.append(got)

    halo_a, strain, inverse_cross = call(
        lambda *refs: strain_kernel(plan, tiles, *refs),
        "strain",
        [whole] * 8,
        [
            array(plies, REACH + 1, 3, REACH), array(plies, REACH + 1, plan.wide - 2 * REACH),
            array(plies, len(plan.cross_a)),
        ],
    )(message_b, got_a, got_more_a, rows_a, rows_b, sums_a, sums_b, weight)

    (force,) = call(
        lambda *refs: early_kernel(plan, tiles, *refs),
        "early",
        [whole] * 10,
        [array(plies, 3, cols)],
        cost=EARLY_COST,
    )(rows_a, rows_b, halo_a, strain, inverse_cross, inverse_a, inverse_b, pair, factor, spring)

    out = []
    for part, got in zip(parts, got_b):
        final = part.stop == plies
        result = jax.ShapeDtypeStruct((comps, len(part), *view.shape[2:]), jnp.float32)
        scratches = [
            scratch(len(part), REACH + 1, 3, REACH), scratch(len(part), len(plan.cross_b)),
            scratch(len(part), REACH + 1, 2 * REACH), scratch(len(part), 3, cols),
        ]
        if final:
            scratches += [
                pltpu.VMEM(result.shape, jnp.float32), pltpu.SemaphoreType.DMA((len(part),)), pltpu.SemaphoreType.DMA,
            ]
        out = call(
            lambda *refs: late_kernel(plan, tiles, part, final, *refs),
            "late_rest" if final else "late",
            [whole] * (14 + len(out)),
            [jax.ShapeDtypeStruct(view.shape, jnp.float32) if final else result],
            out_specs=[pl.BlockSpec(memory_space=pltpu.HBM)] if final else None,
            scratches=scratches,
            cost=LATE_COST,
        )(
            got_first, got_second, got, rows_a, rows_b, sums_b, weight, pair, factor, spring, vector_late, inner_late,
            force, strain, *out,
        )
    (out,) = out
    return (
        out.reshape(comps, plies, subs, cols, LANES)
        .transpose(0, 1, 3, 2, 4)
        .reshape(comps, plies, cols, length)
    )


def solution(mesh):
    placed = (P(None, "ply", "tile", None), P("ply"), P(), P())
    return jax.shard_map(
        local, mesh=mesh, in_specs=placed, out_specs=P(None, "ply", "tile", None), check_vma=False
    )
```

```python
import math

import jax
import jax.numpy as jnp
from jax import lax
from jax.experimental import pallas as pl
from jax.experimental.pallas import tpu as pltpu
from jax.sharding import PartitionSpec as P

bulk_modulus = 40.0
REACH = 3
LANES = 128
VMEM_LIMIT = 24 * 1024 * 1024
EARLY_COST = 2 * 10**9
LATE_COST = 2 * 10**9


def bond_columns():
    halves = []
    for a in range(-REACH, REACH + 1):
        for b in range(-REACH, REACH + 1):
            if 0 < a * a + b * b <= 9 and (a > 0 or (a == 0 and b > 0)):
                halves.append((a, b))
    columns = {}
    for index, (a, b) in enumerate(halves):
        columns[(a, b)] = index
        columns[(-a, -b)] = index
    return columns


COLUMNS = bond_columns()
BONDS = {0: (1, 2, 3), 1: (-2, -1, 0, 1, 2), 2: (-2, -1, 0, 1, 2), 3: (0,)}


OFFSETS = [(a, b) for b, offsets in BONDS.items() for a in offsets]


def length_of(a, b):
    return math.sqrt(a * a + b * b)


class Plan:
    def __init__(self, cols):
        self.cols = cols
        self.wide = cols + 2 * REACH
        self.own = range(REACH, REACH + cols)
        self.low = range(0, REACH)
        self.high = range(REACH + cols, self.wide)
        self.near_b = range(REACH, 2 * REACH)
        self.near_a = range(cols, cols + REACH)
        every = [
            (b, a, i)
            for b, offsets in BONDS.items()
            for i in range(self.wide)
            for a in offsets
            if 0 <= i + a < self.wide and (i in self.own or i + a in self.own)
        ]
        inner = [k for k in every if k[2] in self.own and k[2] + k[1] in self.own]
        self.inner = inner
        self.inner_a = [k for k in inner if k[2] in self.near_a or k[2] + k[1] in self.near_a]
        self.inner_b = [k for k in inner if k not in self.inner_a]
        self.cross_a = [k for k in every if max(k[2], k[2] + k[1]) in self.high]
        self.cross_b = [k for k in every if min(k[2], k[2] + k[1]) in self.low]
        self.late = [k for k in every if min(k[2], k[2] + k[1]) < 2 * REACH]
        self.early = [k for k in every if k not in self.late]
        self.inner_early = [k for k in self.early if k in inner]
        self.inner_late = [k for k in self.late if k in inner]
        self.inner_start = self.span(self.inner_early).start
        self.start_a = min(min(k[2], k[2] + k[1]) for k in self.inner_a)


    def span(self, keys):
        ends = [x for _, a, i in keys for x in (i, i + a)]
        return range(min(ends), max(ends) + 1)


class Grid:
    def __init__(self, subs):
        self.subs = subs
        self.lane = lax.broadcasted_iota(jnp.int32, (subs, LANES), 1)
        self.y = lax.broadcasted_iota(jnp.int32, (subs, LANES), 0) * LANES + self.lane
        self.total = subs * LANES
        self.exists = {b: self.y < self.total - b for b in range(1, REACH + 1)}

    def ahead(self, row):
        after = pltpu.roll(row, self.subs - 1, axis=0)
        return {
            b: pltpu.roll(jnp.where(self.lane < b, after, row), LANES - b, axis=1) for b in range(1, REACH + 1)
        }

    def back(self, rows):
        total = None
        for b, row in rows.items():
            before = pltpu.roll(row, 1, axis=0)
            moved = pltpu.roll(jnp.where(self.lane >= LANES - b, before, row), b, axis=1)
            total = moved if total is None else total + moved
        return total

    def ring(self, a):
        total = None
        for b in range(-REACH, REACH + 1):
            if 0 < a * a + b * b <= 9:
                exists = (self.y + b >= 0) & (self.y + b < self.total)
                term = jnp.where(exists, length_of(a, b), 0.0)
                total = term if total is None else total + term
        return total


class Store:
    def __init__(self, *parts):
        self.parts = parts

    def at(self, column, *lead):
        for ref, first, columns, head in self.parts:
            if column in columns:
                return ref, (*head, *lead, column - first)
        raise KeyError(column)

    def get(self, column, *lead):
        ref, index = self.at(column, *lead)
        return ref[index]

    def put(self, column, value, *lead):
        ref, index = self.at(column, *lead)
        ref[index] = value


def frame():
    odd = lax.axis_index("tile") % 2 == 1
    return odd, jnp.where(odd, -1.0, 1.0).astype(jnp.float32)


def sides(tiles):
    tile = lax.axis_index("tile")
    has_a = (tile % 2 == 1) | (tile + 1 < tiles)
    has_b = jnp.where(tile % 2 == 1, tile + 1 < tiles, tile > 0)
    return has_a, has_b


def keep_row(grid, rows, column, row):
    for c in range(3):
        rows.put(column, row[c], 0, c)
        for b, moved in grid.ahead(row[c]).items():
            rows.put(column, moved + float(b) if c == 1 else moved, b, c)


def separation(rows, b, a, i, here):
    there = [rows.get(i + a, b, c) for c in range(3)]
    here_x = here[0] - float(a) if a else here[0]
    return there[0] - here_x, there[1] - here[1], there[2] - here[2]


def by_row(keys):
    groups = {}
    for b, a, i in keys:
        groups.setdefault((b, i), []).append(a)
    return groups.items()


def extension_sums(grid, rows, keys, mask_of, keep):
    sums = {}
    shifted = {}
    for (b, i), offsets in by_row(keys):
        here = [rows.get(i, 0, c) for c in range(3)]
        for a in offsets:
            sep = separation(rows, b, a, i, here)
            q = sep[0] * sep[0] + sep[1] * sep[1] + sep[2] * sep[2]
            r = lax.rsqrt(q)
            keep((b, a, i), r)
            e = q * r - length_of(a, b)
            mask = mask_of(b)
            if mask is not None:
                e = jnp.where(mask, e, 0.0)
            sums[i] = sums[i] + e if i in sums else e
            if b == 0:
                sums[i + a] = sums[i + a] + e if i + a in sums else e
            else:
                key = (i + a, b)
                shifted[key] = shifted[key] + e if key in shifted else e
    for x in sorted({x for x, _ in shifted}):
        total = grid.back({b: shifted[(x, b)] for b in range(1, REACH + 1) if (x, b) in shifted})
        sums[x] = sums[x] + total if x in sums else total
    return sums


def chunk_of(plies, most):
    return max(n for n in range(1, most + 1) if plies % n == 0)


def for_plies(plies, most, body):
    count = chunk_of(plies, most)

    def step(n, carry):
        for k in range(count):
            body(n * count + k)
        return carry

    lax.fori_loop(0, plies // count, step, 0)


def own_row(plan, u_ref, odd, sign, p, c, column):
    x = column - REACH
    at = jnp.where(odd, plan.cols - 1 - x, x)
    row = u_ref[c, p, pl.ds(at, u_ref.shape[2] // plan.cols, stride=plan.cols), :]
    return row * sign if c == 0 else row


def pack_kernel(plan, u_ref, message):
    odd, sign = frame()
    for p in range(u_ref.shape[1]):
        for c in range(2):
            for n, column in enumerate(plan.near_a):
                message[0, p, c * REACH + n] = own_row(plan, u_ref, odd, sign, p, c, column)


def near_a_kernel(plan, after_ref, u_ref, message, base_ref, rows_ref, sums_ref, inverse_ref, first_ref, second_ref):
    plies = base_ref.shape[0]
    odd, sign = frame()
    grid = Grid(base_ref.shape[-2])
    slots = {key: n for n, key in enumerate(plan.inner_a)}

    def ply(p):
        rows = Store((rows_ref, plan.start_a, range(plan.start_a, plan.own.stop), (p,)))
        for x in plan.own:
            row = [own_row(plan, u_ref, odd, sign, p, c, x) for c in range(3)]
            for c in range(3):
                base_ref[p, c, x - REACH] = row[c]
            if x >= plan.start_a:
                keep_row(grid, rows, x, row)

        def keep(key, r):
            inverse_ref[p, slots[key]] = r

        sums = extension_sums(grid, rows, plan.inner_a, grid.exists.get, keep)
        for x in rows.parts[0][2]:
            sums_ref[p, x - plan.start_a] = sums[x]
            if x in plan.near_a:
                message[0, p, x - plan.near_a.start] = base_ref[p, 2, x - REACH]
                message[0, p, REACH + x - plan.near_a.start] = sums[x]

    for_plies(plies, 2, ply)
    upper = lax.axis_index("ply") % 2 == 1
    for c in range(3):
        for x in range(plan.cols):
            low, high = base_ref[0, c, x], base_ref[plies - 1, c, x]
            first_ref[0, c, x] = jnp.where(upper, low, high)
            second_ref[0, c, x] = jnp.where(upper, high, low)


def near_b_kernel(
    plan, base_ref, rows_a_ref, sums_a_ref, rows_ref, sums_ref, inverse_ref
):
    plies = rows_a_ref.shape[0]
    grid = Grid(rows_a_ref.shape[-2])
    slots = {key: n for n, key in enumerate(plan.inner_b)}
    fresh = range(REACH, plan.start_a)
    tall = range(plan.start_a, plan.own.stop)

    def ply(p):
        rows = Store((rows_ref, REACH, fresh, (p,)), (rows_a_ref, plan.start_a, tall, (p,)))
        for x in fresh:
            keep_row(grid, rows, x, [base_ref[p, c, x - REACH] for c in range(3)])

        def keep(key, r):
            inverse_ref[p, slots[key]] = r

        sums = extension_sums(grid, rows, plan.inner_b, grid.exists.get, keep)
        for x in range(REACH, plan.near_a.start):
            total = sums[x] + sums_a_ref[p, x - plan.start_a] if x >= plan.start_a else sums[x]
            sums_ref[p, x - REACH] = total

    for_plies(plies, 2, ply)


def weight_kernel(
    plan, tiles, slabs, angle_ref, table_ref, stiff_ref, after_ref, weight_ref, pair_ref, factor_ref, spring_ref
):
    plies = factor_ref.shape[0]
    odd, _ = frame()
    slab = lax.axis_index("ply")
    layers = slabs * plies

    def fill(ref, at, value):
        ref[at] = jnp.full(ref.shape[-2:], value, jnp.float32)

    for p in range(plies):
        for n, (a, b) in enumerate(OFFSETS):
            column = COLUMNS[(a, b)]
            mirrored = COLUMNS[(-a, b)]
            shear = table_ref[angle_ref[p], column if column == mirrored else jnp.where(odd, mirrored, column)]
            fill(factor_ref, (p, 2 * n), 3.0 * bulk_modulus - 5.0 * shear)
            fill(factor_ref, (p, 2 * n + 1), 15.0 / length_of(a, b) * shear)
        layer = slab * plies + p
        up = jnp.where(layer < layers - 1, stiff_ref[jnp.minimum(layer, layers - 2)], 0.0)
        down = jnp.where(layer > 0, stiff_ref[jnp.maximum(layer - 1, 0)], 0.0)
        fill(spring_ref, (p, 0), up)
        fill(spring_ref, (p, 1), down)
        fill(spring_ref, (p, 2), up if p < plies - 1 else 0.0)
        fill(spring_ref, (p, 3), down if p > 0 else 0.0)
    grid = Grid(weight_ref.shape[-2])
    ones = jnp.ones((grid.subs, LANES), jnp.int32)
    has_a, has_b = (ones * side.astype(jnp.int32) > 0 for side in sides(tiles))
    ring = {a: grid.ring(a) for a in range(REACH + 1)}
    weight = {}
    for x in range(plan.wide):
        mass = ring[0]
        for a in range(-REACH, REACH + 1):
            term = ring[abs(a)]
            if x in plan.own and x + a in plan.low:
                term = jnp.where(has_b, term, 0.0)
            if x in plan.own and x + a in plan.high:
                term = jnp.where(has_a, term, 0.0)
            if a:
                mass = mass + term
        weight[x] = 1.0 / mass
        weight_ref[x] = weight[x]
    moved = {x: {0: weight[x], **grid.ahead(weight[x])} for x in range(plan.wide)}
    for n, (b, a, i) in enumerate(plan.early + plan.late):
        pair_ref[n] = weight[i] + moved[i + a][b]


def factors_of(factor_ref, p):
    def of(a, b):
        n = OFFSETS.index((a, b))
        return factor_ref[p, 2 * n], factor_ref[p, 2 * n + 1]

    return of


def collect(plan, grid, keys, push_of, force):
    held = {}
    last = {}
    for b, a, i in keys:
        last[(i + a, b)] = i
    for (b, i), offsets in by_row(keys):
        mine = None
        for a in offsets:
            j = i + a
            push = push_of((b, a, i))
            if i in plan.own:
                mine = push if mine is None else [mine[c] + push[c] for c in range(3)]
            if j in plan.own:
                held[(j, b)] = [held[(j, b)][c] + push[c] for c in range(3)] if (j, b) in held else push
        if mine is not None:
            force(i, mine)
        for j, _ in [k for k in held if k[1] == b and last[k] == i]:
            total = held.pop((j, b))
            force(j, [-(grid.back({b: total[c]}) if b else total[c]) for c in range(3)])
    assert not held


def whole_push(rows, strains, factors, inverse, pair, mask_of, key):
    b, a, i = key
    alpha, beta = factors(a, b)
    sep = separation(rows, b, a, i, [rows.get(i, 0, c) for c in range(3)])
    r = inverse(key)
    f = (alpha * r) * (strains.get(i, 0) + strains.get(i + a, b)) + (beta * pair(key)) * (1.0 - length_of(a, b) * r)
    mask = mask_of(b)
    if mask is not None:
        f = jnp.where(mask, f, 0.0)
    return [f * sep[c] for c in range(3)]


def inner_kernel(
    plan, after_ref, factor_ref, rows_a_ref, rows_b_ref, inverse_a_ref, inverse_b_ref, pair_ref, vector_ref, force_ref
):
    keys = plan.inner_late
    plies = rows_a_ref.shape[0]
    grid = Grid(rows_a_ref.shape[-2])
    in_a = {key: n for n, key in enumerate(plan.inner_a)}
    in_b = {key: n for n, key in enumerate(plan.inner_b)}
    in_pair = {key: n for n, key in enumerate(plan.early + plan.late)}
    in_vector = {key: n for n, key in enumerate(keys)}

    def ply(p):
        rows = Store(
            (rows_b_ref, REACH, range(REACH, plan.start_a), (p,)),
            (rows_a_ref, plan.start_a, range(plan.start_a, plan.own.stop), (p,)),
        )
        factors = factors_of(factor_ref, p)
        span = plan.span(keys)
        started = set()
        def push_of(key):
            b, a, i = key
            alpha, beta = factors(a, b)
            sep = separation(rows, b, a, i, [rows.get(i, 0, c) for c in range(3)])
            r = inverse_a_ref[p, in_a[key]] if key in in_a else inverse_b_ref[p, in_b[key]]
            scale = alpha * r
            f = (beta * pair_ref[in_pair[key]]) * (1.0 - length_of(a, b) * r)
            if b:
                scale = jnp.where(grid.exists[b], scale, 0.0)
                f = jnp.where(grid.exists[b], f, 0.0)
            for c in range(3):
                vector_ref[p, in_vector[key], c] = scale * sep[c]
            return [f * sep[c] for c in range(3)]

        def force(x, values):
            for c in range(3):
                at = (p, c, x - span.start)
                force_ref[at] = force_ref[at] + values[c] if x in started else values[c]
            started.add(x)

        collect(plan, grid, keys, push_of, force)
        assert started == set(span)

    for_plies(plies, 2, ply)


def send_kernel(plan, part, after_ref, base_ref, sums_b_ref, message):
    for p in part:
        for x in range(REACH):
            message[0, p - part.start, 3 * REACH + x] = sums_b_ref[p, x]
            for c in range(3):
                message[0, p - part.start, c * REACH + x] = base_ref[p, c, x]


def strain_kernel(
    plan, tiles, after_ref, got_ref, got_more_ref, rows_a_ref, rows_b_ref, sums_a_ref, sums_b_ref, weight_ref,
    halo_ref, strain_ref, inverse_ref,
):
    plies = rows_a_ref.shape[0]
    grid = Grid(rows_a_ref.shape[-2])
    in_cross = {key: n for n, key in enumerate(plan.cross_a)}
    start = 2 * REACH
    mask_of = cross_mask_a(grid, tiles)

    def ply(p):
        rows = Store(
            (rows_b_ref, REACH, range(REACH, plan.start_a), (p,)),
            (rows_a_ref, plan.start_a, range(plan.start_a, plan.own.stop), (p,)),
            (halo_ref, plan.high.start, plan.high, (p,)),
        )
        strains = Store((strain_ref, start, range(start, plan.wide), (p,)))
        for j in range(REACH):
            row = [got_ref[0, p, j], got_ref[0, p, REACH + j], got_more_ref[0, p, j]]
            keep_row(grid, rows, plan.wide - 1 - j, [-row[0], row[1], row[2]])

        def keep(key, r):
            inverse_ref[p, in_cross[key]] = r

        sums = extension_sums(grid, rows, plan.cross_a, mask_of, keep)
        for x in range(start, plan.wide):
            if x in plan.high:
                total = got_more_ref[0, p, REACH + plan.wide - 1 - x]
            elif x >= plan.near_a.start:
                total = sums_a_ref[p, x - plan.start_a]
            else:
                total = sums_b_ref[p, x - REACH]
            if x in sums:
                total = total + sums[x]
            strain = 3.0 * total * (weight_ref[x] * weight_ref[x])
            strains.put(x, strain, 0)
            for b, moved in grid.ahead(strain).items():
                strains.put(x, moved, b)

    for_plies(plies, 2, ply)


def cross_mask_a(grid, tiles):
    if tiles % 2 == 0:
        return grid.exists.get
    has_a = jnp.ones((grid.subs, LANES), jnp.int32) * sides(tiles)[0].astype(jnp.int32) > 0
    return {b: grid.exists[b] & has_a if b else has_a for b in range(REACH + 1)}.get


def early_kernel(
    plan, tiles, rows_a_ref, rows_b_ref, halo_ref, strain_ref, inverse_ref, inverse_a_ref, inverse_b_ref, pair_ref,
    factor_ref, spring_ref, force_ref,
):
    plies = rows_a_ref.shape[0]
    grid = Grid(rows_a_ref.shape[-2])
    in_a = {key: n for n, key in enumerate(plan.inner_a)}
    in_b = {key: n for n, key in enumerate(plan.inner_b)}
    in_cross = {key: n for n, key in enumerate(plan.cross_a)}
    in_pair = {key: n for n, key in enumerate(plan.early + plan.late)}
    start = 2 * REACH
    cross_mask = cross_mask_a(grid, tiles)

    def ply(p):
        def rows_of(q, *more):
            return Store(
                (rows_b_ref, REACH, range(REACH, plan.start_a), (q,)),
                (rows_a_ref, plan.start_a, range(plan.start_a, plan.own.stop), (q,)),
                *more,
            )

        rows = rows_of(p, (halo_ref, plan.high.start, plan.high, (p,)))
        strains = Store((strain_ref, start, range(start, plan.wide), (p,)))
        factors = factors_of(factor_ref, p)
        up, down = spring_ref[p, 2], spring_ref[p, 3]
        over, under = rows_of(jnp.minimum(p + 1, plies - 1)), rows_of(jnp.maximum(p - 1, 0))
        for x in plan.own:
            for c in range(3):
                here = rows.get(x, 0, c)
                spring = up * (over.get(x, 0, c) - here) + down * (under.get(x, 0, c) - here)
                force_ref[p, c, x - REACH] = spring

        def inverse(key):
            if key in in_cross:
                return inverse_ref[p, in_cross[key]]
            return inverse_a_ref[p, in_a[key]] if key in in_a else inverse_b_ref[p, in_b[key]]

        def push_of(key):
            mask_of = cross_mask if key in in_cross else grid.exists.get
            return whole_push(rows, strains, factors, inverse, lambda k: pair_ref[in_pair[k]], mask_of, key)

        def force(x, values):
            for c in range(3):
                force_ref[p, c, x - REACH] = force_ref[p, c, x - REACH] + values[c]

        collect(plan, grid, plan.early, push_of, force)

    for_plies(plies, 2, ply)


def late_kernel(
    plan, tiles, part, final, first_ref, second_ref, got_ref, rows_a_ref, rows_b_ref, sums_b_ref, weight_ref, pair_ref,
    factor_ref, spring_ref, vector_ref, inner_ref, force_in_ref, strain_a_ref, *rest,
):
    if final:
        before_ref, out_hbm, halo_ref, cross_ref, strain_ref, force_ref, out_ref, sems, before_sem = rest
        copy_before = pltpu.make_async_copy(before_ref, out_hbm.at[:, pl.ds(0, part.start)], before_sem)
        copy_before.start()
    else:
        out_ref, halo_ref, cross_ref, strain_ref, force_ref = rest
    plies = rows_a_ref.shape[0]
    grid = Grid(rows_a_ref.shape[-2])
    odd, sign = frame()
    upper = lax.axis_index("ply") % 2 == 1
    in_cross = {key: n for n, key in enumerate(plan.cross_b)}
    in_pair = {key: n for n, key in enumerate(plan.early + plan.late)}
    in_vector = {key: n for n, key in enumerate(plan.inner_late)}
    start = 2 * REACH
    has_b = jnp.ones((grid.subs, LANES), jnp.int32) * sides(tiles)[1].astype(jnp.int32) > 0
    cross_masks = {b: grid.exists[b] & has_b if b else has_b for b in range(REACH + 1)}
    late = plan.span(plan.inner_late)

    def copy_out(p):
        return pltpu.make_async_copy(
            out_ref.at[:, pl.ds(p - part.start, 1)], out_hbm.at[:, pl.ds(p, 1)], sems.at[p - part.start]
        )

    def ply(p):
        n = p - part.start
        rows = Store(
            (halo_ref, 0, plan.low, (n,)),
            (rows_b_ref, REACH, range(REACH, plan.start_a), (p,)),
            (rows_a_ref, plan.start_a, range(plan.start_a, plan.own.stop), (p,)),
        )
        strains = Store(
            (strain_ref, 0, range(start), (n,)), (strain_a_ref, start, range(start, plan.wide), (p,))
        )
        factors = factors_of(factor_ref, p)
        for j in range(REACH):
            row = [got_ref[0, n, c * REACH + j] for c in range(3)]
            keep_row(grid, rows, REACH - 1 - j, [-row[0], row[1], row[2]])

        def keep(key, r):
            cross_ref[n, in_cross[key]] = r

        sums = extension_sums(grid, rows, plan.cross_b, cross_masks.get, keep)
        for x in range(start):
            total = got_ref[0, n, 3 * REACH + REACH - 1 - x] if x in plan.low else sums_b_ref[p, x - REACH]
            strain = 3.0 * (total + sums[x]) * (weight_ref[x] * weight_ref[x])
            strains.put(x, strain, 0)
            for b, moved in grid.ahead(strain).items():
                strains.put(x, moved, b)
        faces = []
        if p == plies - 1:
            faces.append((spring_ref[p, 0], second_ref, first_ref))
        if p == 0:
            faces.append((spring_ref[p, 1], first_ref, second_ref))
        for c in range(3):
            for x in plan.own:
                value = force_in_ref[p, c, x - REACH]
                if x in late:
                    value = value + inner_ref[p, c, x - REACH]
                for factor, one, two in faces:
                    beyond = jnp.where(upper, one[0, c, x - REACH], two[0, c, x - REACH])
                    value = value + factor * (beyond - rows.get(x, 0, c))
                force_ref[n, c, x - REACH] = value

        def push_of(key):
            if key in in_cross:
                return whole_push(
                    rows, strains, factors, lambda k: cross_ref[n, in_cross[k]], lambda k: pair_ref[in_pair[k]],
                    cross_masks.get, key,
                )
            b, a, i = key
            total = strains.get(i, 0) + strains.get(i + a, b)
            return [vector_ref[p, in_vector[key], c] * total for c in range(3)]

        def force(x, values):
            for c in range(3):
                force_ref[n, c, x - REACH] = force_ref[n, c, x - REACH] + values[c]

        collect(plan, grid, plan.late, push_of, force)
        for x in plan.own:
            at = jnp.where(odd, plan.cols - 1 - (x - REACH), x - REACH)
            for c in range(3):
                value = force_ref[n, c, x - REACH]
                out_ref[c, n, pl.ds(at, grid.subs, stride=plan.cols), :] = value * sign if c == 0 else value

    for first in range(part.start, part.stop, 2):
        group = range(first, min(first + 2, part.stop))
        for p in group:
            ply(p)
        if final:
            for p in group:
                copy_out(p).start()
    if final:
        copy_before.wait()
        for p in part:
            copy_out(p).wait()


def local(displacement, angle_index, bond_table, interface_stiffness):
    comps, plies, cols, length = displacement.shape
    subs = length // LANES
    tiles = lax.axis_size("tile")
    slabs = lax.axis_size("ply")
    assert length % LANES == 0 and cols >= 2 * REACH
    plan = Plan(cols)
    view = (
        displacement.reshape(comps, plies, cols, subs, LANES)
        .transpose(0, 1, 3, 2, 4)
        .reshape(comps, plies, subs * cols, LANES)
    )
    whole = pl.BlockSpec(memory_space=pltpu.VMEM)
    scalars = pl.BlockSpec(memory_space=pltpu.SMEM)

    def array(*shape):
        return jax.ShapeDtypeStruct((*shape, subs, LANES), jnp.float32)

    def scratch(*shape):
        return pltpu.VMEM((*shape, subs, LANES), jnp.float32)

    def call(body, name, ins, outs, out_specs=None, scratches=(), cost=1):
        return pl.pallas_call(
            body,
            out_shape=outs,
            in_specs=ins,
            out_specs=out_specs or [whole] * len(outs),
            scratch_shapes=list(scratches),
            compiler_params=pltpu.CompilerParams(vmem_limit_bytes=VMEM_LIMIT),
            cost_estimate=pl.CostEstimate(flops=cost, bytes_accessed=1, transcendentals=0),
            name=name,
        )

    swap_a = [(i, i ^ 1) for i in range(tiles) if (i ^ 1) < tiles]
    swap_b = []
    for slab in range(slabs):
        for tile in range(tiles):
            other = tile + 1 if tile % 2 else tile - 1
            if 0 <= other < tiles:
                swap_b.append((slab * tiles + tile, slab * tiles + other))
            elif (slab ^ 1) < slabs:
                swap_b.append((slab * tiles + tile, (slab ^ 1) * tiles + tile))
    swap_first = [(i, i ^ 1) for i in range(slabs) if (i ^ 1) < slabs]
    swap_second = [(i, j) for k in range(1, slabs - 1, 2) for i, j in ((k, k + 1), (k + 1, k))]
    if slabs % 2 == 0:
        swap_second += [(0, slabs - 1), (slabs - 1, 0)]
    tall = plan.own.stop - plan.start_a
    short = plan.start_a - REACH

    (message_a,) = call(
        lambda *refs: pack_kernel(plan, *refs),
        "pack",
        [whole],
        [array(1, plies, 2 * REACH)],
    )(view)
    got_a = lax.ppermute(message_a, "tile", swap_a)

    more_a, base, rows_a, sums_a, inverse_a, first, second = call(
        lambda *refs: near_a_kernel(plan, *refs),
        "near_a",
        [whole] * 2,
        [
            array(1, plies, 2 * REACH), array(plies, 3, cols), array(plies, REACH + 1, 3, tall), array(plies, tall),
            array(plies, len(plan.inner_a)), array(1, 3, cols), array(1, 3, cols),
        ],
    )(message_a, view)
    got_more_a = lax.ppermute(more_a, "tile", swap_a)
    got_second = lax.ppermute(second, "ply", swap_second)
    got_first = lax.ppermute(first, "ply", swap_first)

    rows_b, sums_b, inverse_b = call(
        lambda *refs: near_b_kernel(plan, *refs),
        "near_b",
        [whole] * 3,
        [
            array(plies, REACH + 1, 3, short), array(plies, plan.near_a.start - REACH),
            array(plies, len(plan.inner_b)),
        ],
    )(base, rows_a, sums_a)

    weight, pair, factor, spring = call(
        lambda *refs: weight_kernel(plan, tiles, slabs, *refs),
        "weights",
        [scalars] * 3 + [whole],
        [
            array(plan.wide), array(len(plan.early) + len(plan.late)), array(plies, 2 * len(OFFSETS)),
            array(plies, 4),
        ],
    )(angle_index, bond_table, interface_stiffness, got_first)

    vector_late, inner_late = call(
        lambda *refs: inner_kernel(plan, *refs),
        "inner",
        [whole] * 7,
        [array(plies, len(plan.inner_late), 3), array(plies, 3, len(plan.span(plan.inner_late)))],
    )(got_second, factor, rows_a, rows_b, inverse_a, inverse_b, pair)

    count = plies - plies // 3
    parts = [range(count), range(count, plies)]
    def send_part(part, name, after):
        (message,) = call(
            lambda *refs: send_kernel(plan, part, *refs), name, [whole] * 3, [array(1, len(part), 4 * REACH)]
        )(after, base, sums_b)
        return message, lax.ppermute(message, ("ply", "tile"), swap_b)

    message_b, got = send_part(parts[0], "send", got_a)
    got_b = [got]
    message_b, got = send_part(parts[1], "send_rest", inner_late)
    got_b.append(got)

    halo_a, strain, inverse_cross = call(
        lambda *refs: strain_kernel(plan, tiles, *refs),
        "strain",
        [whole] * 8,
        [
            array(plies, REACH + 1, 3, REACH), array(plies, REACH + 1, plan.wide - 2 * REACH),
            array(plies, len(plan.cross_a)),
        ],
    )(message_b, got_a, got_more_a, rows_a, rows_b, sums_a, sums_b, weight)

    (force,) = call(
        lambda *refs: early_kernel(plan, tiles, *refs),
        "early",
        [whole] * 10,
        [array(plies, 3, cols)],
        cost=EARLY_COST,
    )(rows_a, rows_b, halo_a, strain, inverse_cross, inverse_a, inverse_b, pair, factor, spring)

    out = []
    for part, got in zip(parts, got_b):
        final = part.stop == plies
        result = jax.ShapeDtypeStruct((comps, len(part), *view.shape[2:]), jnp.float32)
        scratches = [
            scratch(len(part), REACH + 1, 3, REACH), scratch(len(part), len(plan.cross_b)),
            scratch(len(part), REACH + 1, 2 * REACH), scratch(len(part), 3, cols),
        ]
        if final:
            scratches += [
                pltpu.VMEM(result.shape, jnp.float32), pltpu.SemaphoreType.DMA((len(part),)), pltpu.SemaphoreType.DMA,
            ]
        out = call(
            lambda *refs: late_kernel(plan, tiles, part, final, *refs),
            "late_rest" if final else "late",
            [whole] * (14 + len(out)),
            [jax.ShapeDtypeStruct(view.shape, jnp.float32) if final else result],
            out_specs=[pl.BlockSpec(memory_space=pltpu.HBM)] if final else None,
            scratches=scratches,
            cost=LATE_COST,
        )(
            got_first, got_second, got, rows_a, rows_b, sums_b, weight, pair, factor, spring, vector_late, inner_late,
            force, strain, *out,
        )
    (out,) = out
    return (
        out.reshape(comps, plies, subs, cols, LANES)
        .transpose(0, 1, 3, 2, 4)
        .reshape(comps, plies, cols, length)
    )


def solution(mesh):
    placed = (P(None, "ply", "tile", None), P("ply"), P(), P())
    return jax.shard_map(
        local, mesh=mesh, in_specs=placed, out_specs=P(None, "ply", "tile", None), check_vma=False
    )
```

```python
import math

import jax
import jax.numpy as jnp
from jax import lax
from jax.experimental import pallas as pl
from jax.experimental.pallas import tpu as pltpu
from jax.sharding import PartitionSpec as P

bulk_modulus = 40.0
REACH = 3
LANES = 128
VMEM_LIMIT = 24 * 1024 * 1024
EARLY_COST = 2 * 10**9
LATE_COST = 2 * 10**9


def bond_columns():
    halves = []
    for a in range(-REACH, REACH + 1):
        for b in range(-REACH, REACH + 1):
            if 0 < a * a + b * b <= 9 and (a > 0 or (a == 0 and b > 0)):
                halves.append((a, b))
    columns = {}
    for index, (a, b) in enumerate(halves):
        columns[(a, b)] = index
        columns[(-a, -b)] = index
    return columns


COLUMNS = bond_columns()
BONDS = {0: (1, 2, 3), 1: (-2, -1, 0, 1, 2), 2: (-2, -1, 0, 1, 2), 3: (0,)}
OFFSETS = [(a, b) for b, offsets in BONDS.items() for a in offsets]


def length_of(a, b):
    return math.sqrt(a * a + b * b)


class Plan:
    def __init__(self, cols):
        self.cols = cols
        self.wide = cols + 2 * REACH
        self.own = range(REACH, REACH + cols)
        self.low = range(0, REACH)
        self.high = range(REACH + cols, self.wide)
        self.near_b = range(REACH, 2 * REACH)
        self.near_a = range(cols, cols + REACH)
        every = [
            (b, a, i)
            for b, offsets in BONDS.items()
            for i in range(self.wide)
            for a in offsets
            if 0 <= i + a < self.wide and (i in self.own or i + a in self.own)
        ]
        inner = [k for k in every if k[2] in self.own and k[2] + k[1] in self.own]
        self.inner = inner
        self.inner_a = [k for k in inner if k[2] in self.near_a or k[2] + k[1] in self.near_a]
        self.inner_b = [k for k in inner if k not in self.inner_a]
        self.cross_a = [k for k in every if max(k[2], k[2] + k[1]) in self.high]
        self.cross_b = [k for k in every if min(k[2], k[2] + k[1]) in self.low]
        self.late = [k for k in every if min(k[2], k[2] + k[1]) < 2 * REACH]
        self.early = [k for k in every if k not in self.late]
        self.inner_early = [k for k in self.early if k in inner]
        self.inner_late = [k for k in self.late if k in inner]
        self.inner_start = self.span(self.inner_early).start
        self.start_a = min(min(k[2], k[2] + k[1]) for k in self.inner_a)


    def span(self, keys):
        ends = [x for _, a, i in keys for x in (i, i + a)]
        return range(min(ends), max(ends) + 1)


class Grid:
    def __init__(self, subs):
        self.subs = subs
        self.lane = lax.broadcasted_iota(jnp.int32, (subs, LANES), 1)
        self.y = lax.broadcasted_iota(jnp.int32, (subs, LANES), 0) * LANES + self.lane
        self.total = subs * LANES
        self.exists = {b: self.y < self.total - b for b in range(1, REACH + 1)}

    def ahead(self, row):
        after = pltpu.roll(row, self.subs - 1, axis=0)
        return {
            b: pltpu.roll(jnp.where(self.lane < b, after, row), LANES - b, axis=1) for b in range(1, REACH + 1)
        }

    def back(self, rows):
        total = None
        for b, row in rows.items():
            before = pltpu.roll(row, 1, axis=0)
            moved = pltpu.roll(jnp.where(self.lane >= LANES - b, before, row), b, axis=1)
            total = moved if total is None else total + moved
        return total

    def ring(self, a):
        total = None
        for b in range(-REACH, REACH + 1):
            if 0 < a * a + b * b <= 9:
                exists = (self.y + b >= 0) & (self.y + b < self.total)
                term = jnp.where(exists, length_of(a, b), 0.0)
                total = term if total is None else total + term
        return total


class Store:
    def __init__(self, *parts):
        self.parts = parts

    def at(self, column, *lead):
        for ref, first, columns, head in self.parts:
            if column in columns:
                return ref, (*head, *lead, column - first)
        raise KeyError(column)

    def get(self, column, *lead):
        ref, index = self.at(column, *lead)
        return ref[index]

    def put(self, column, value, *lead):
        ref, index = self.at(column, *lead)
        ref[index] = value


def frame():
    odd = lax.axis_index("tile") % 2 == 1
    return odd, jnp.where(odd, -1.0, 1.0).astype(jnp.float32)


def sides(tiles):
    tile = lax.axis_index("tile")
    has_a = (tile % 2 == 1) | (tile + 1 < tiles)
    has_b = jnp.where(tile % 2 == 1, tile + 1 < tiles, tile > 0)
    return has_a, has_b


def keep_row(grid, rows, column, row):
    for c in range(3):
        rows.put(column, row[c], 0, c)
        for b, moved in grid.ahead(row[c]).items():
            rows.put(column, moved + float(b) if c == 1 else moved, b, c)


def separation(rows, b, a, i, here):
    there = [rows.get(i + a, b, c) for c in range(3)]
    here_x = here[0] - float(a) if a else here[0]
    return there[0] - here_x, there[1] - here[1], there[2] - here[2]


def by_row(keys):
    groups = {}
    for b, a, i in keys:
        groups.setdefault((b, i), []).append(a)
    return groups.items()


def extension_sums(grid, rows, keys, mask_of, keep):
    sums = {}
    shifted = {}
    for (b, i), offsets in by_row(keys):
        here = [rows.get(i, 0, c) for c in range(3)]
        for a in offsets:
            sep = separation(rows, b, a, i, here)
            q = sep[0] * sep[0] + sep[1] * sep[1] + sep[2] * sep[2]
            r = lax.rsqrt(q)
            keep((b, a, i), r)
            e = q * r - length_of(a, b)
            mask = mask_of(b)
            if mask is not None:
                e = jnp.where(mask, e, 0.0)
            sums[i] = sums[i] + e if i in sums else e
            if b == 0:
                sums[i + a] = sums[i + a] + e if i + a in sums else e
            else:
                key = (i + a, b)
                shifted[key] = shifted[key] + e if key in shifted else e
    for x in sorted({x for x, _ in shifted}):
        total = grid.back({b: shifted[(x, b)] for b in range(1, REACH + 1) if (x, b) in shifted})
        sums[x] = sums[x] + total if x in sums else total
    return sums


def chunk_of(plies, most):
    return max(n for n in range(1, most + 1) if plies % n == 0)


def for_plies(plies, most, body):
    count = chunk_of(plies, most)

    def step(n, carry):
        for k in range(count):
            body(n * count + k)
        return carry

    lax.fori_loop(0, plies // count, step, 0)


def own_row(plan, u_ref, odd, sign, p, c, column):
    x = column - REACH
    at = jnp.where(odd, plan.cols - 1 - x, x)
    row = u_ref[c, p, pl.ds(at, u_ref.shape[2] // plan.cols, stride=plan.cols), :]
    return row * sign if c == 0 else row


def pack_kernel(plan, u_ref, message):
    odd, sign = frame()
    for p in range(u_ref.shape[1]):
        for c in range(2):
            for n, column in enumerate(plan.near_a):
                message[0, p, c * REACH + n] = own_row(plan, u_ref, odd, sign, p, c, column)


def near_a_kernel(plan, after_ref, u_ref, message, base_ref, rows_ref, sums_ref, inverse_ref, first_ref, second_ref):
    plies = base_ref.shape[0]
    odd, sign = frame()
    grid = Grid(base_ref.shape[-2])
    slots = {key: n for n, key in enumerate(plan.inner_a)}

    def ply(p):
        rows = Store((rows_ref, plan.start_a, range(plan.start_a, plan.own.stop), (p,)))
        for x in plan.own:
            row = [own_row(plan, u_ref, odd, sign, p, c, x) for c in range(3)]
            for c in range(3):
                base_ref[p, c, x - REACH] = row[c]
            if x >= plan.start_a:
                keep_row(grid, rows, x, row)

        def keep(key, r):
            inverse_ref[p, slots[key]] = r

        sums = extension_sums(grid, rows, plan.inner_a, grid.exists.get, keep)
        for x in rows.parts[0][2]:
            sums_ref[p, x - plan.start_a] = sums[x]
            if x in plan.near_a:
                message[0, p, x - plan.near_a.start] = base_ref[p, 2, x - REACH]
                message[0, p, REACH + x - plan.near_a.start] = sums[x]

    for_plies(plies, 3, ply)
    upper = lax.axis_index("ply") % 2 == 1
    for c in range(3):
        for x in range(plan.cols):
            low, high = base_ref[0, c, x], base_ref[plies - 1, c, x]
            first_ref[0, c, x] = jnp.where(upper, low, high)
            second_ref[0, c, x] = jnp.where(upper, high, low)


def near_b_kernel(
    plan, base_ref, rows_a_ref, sums_a_ref, rows_ref, sums_ref, inverse_ref
):
    plies = rows_a_ref.shape[0]
    grid = Grid(rows_a_ref.shape[-2])
    slots = {key: n for n, key in enumerate(plan.inner_b)}
    fresh = range(REACH, plan.start_a)
    tall = range(plan.start_a, plan.own.stop)

    def ply(p):
        rows = Store((rows_ref, REACH, fresh, (p,)), (rows_a_ref, plan.start_a, tall, (p,)))
        for x in fresh:
            keep_row(grid, rows, x, [base_ref[p, c, x - REACH] for c in range(3)])

        def keep(key, r):
            inverse_ref[p, slots[key]] = r

        sums = extension_sums(grid, rows, plan.inner_b, grid.exists.get, keep)
        for x in range(REACH, plan.near_a.start):
            total = sums[x] + sums_a_ref[p, x - plan.start_a] if x >= plan.start_a else sums[x]
            sums_ref[p, x - REACH] = total

    for_plies(plies, 2, ply)


def weight_kernel(
    plan, tiles, slabs, angle_ref, table_ref, stiff_ref, after_ref, weight_ref, pair_ref, factor_ref, spring_ref
):
    plies = factor_ref.shape[0]
    odd, _ = frame()
    slab = lax.axis_index("ply")
    layers = slabs * plies

    def fill(ref, at, value):
        ref[at] = jnp.full(ref.shape[-2:], value, jnp.float32)

    for p in range(plies):
        for n, (a, b) in enumerate(OFFSETS):
            column = COLUMNS[(a, b)]
            mirrored = COLUMNS[(-a, b)]
            shear = table_ref[angle_ref[p], column if column == mirrored else jnp.where(odd, mirrored, column)]
            fill(factor_ref, (p, 2 * n), 3.0 * bulk_modulus - 5.0 * shear)
            fill(factor_ref, (p, 2 * n + 1), 15.0 / length_of(a, b) * shear)
        layer = slab * plies + p
        up = jnp.where(layer < layers - 1, stiff_ref[jnp.minimum(layer, layers - 2)], 0.0)
        down = jnp.where(layer > 0, stiff_ref[jnp.maximum(layer - 1, 0)], 0.0)
        fill(spring_ref, (p, 0), up)
        fill(spring_ref, (p, 1), down)
        fill(spring_ref, (p, 2), up if p < plies - 1 else 0.0)
        fill(spring_ref, (p, 3), down if p > 0 else 0.0)
    grid = Grid(weight_ref.shape[-2])
    ones = jnp.ones((grid.subs, LANES), jnp.int32)
    has_a, has_b = (ones * side.astype(jnp.int32) > 0 for side in sides(tiles))
    ring = {a: grid.ring(a) for a in range(REACH + 1)}
    weight = {}
    for x in range(plan.wide):
        mass = ring[0]
        for a in range(-REACH, REACH + 1):
            term = ring[abs(a)]
            if x in plan.own and x + a in plan.low:
                term = jnp.where(has_b, term, 0.0)
            if x in plan.own and x + a in plan.high:
                term = jnp.where(has_a, term, 0.0)
            if a:
                mass = mass + term
        weight[x] = 1.0 / mass
        weight_ref[x] = weight[x]
    moved = {x: {0: weight[x], **grid.ahead(weight[x])} for x in range(plan.wide)}
    for n, (b, a, i) in enumerate(plan.early + plan.late):
        pair_ref[n] = weight[i] + moved[i + a][b]


def factors_of(factor_ref, p):
    def of(a, b):
        n = OFFSETS.index((a, b))
        return factor_ref[p, 2 * n], factor_ref[p, 2 * n + 1]

    return of


def collect(plan, grid, keys, push_of, force):
    held = {}
    last = {}
    for b, a, i in keys:
        last[(i + a, b)] = i
    for (b, i), offsets in by_row(keys):
        mine = None
        for a in offsets:
            j = i + a
            push = push_of((b, a, i))
            if i in plan.own:
                mine = push if mine is None else [mine[c] + push[c] for c in range(3)]
            if j in plan.own:
                held[(j, b)] = [held[(j, b)][c] + push[c] for c in range(3)] if (j, b) in held else push
        if mine is not None:
            force(i, mine)
        for j, _ in [k for k in held if k[1] == b and last[k] == i]:
            total = held.pop((j, b))
            force(j, [-(grid.back({b: total[c]}) if b else total[c]) for c in range(3)])
    assert not held


def whole_push(rows, strains, factors, inverse, pair, mask_of, key):
    b, a, i = key
    alpha, beta = factors(a, b)
    sep = separation(rows, b, a, i, [rows.get(i, 0, c) for c in range(3)])
    r = inverse(key)
    f = (alpha * r) * (strains.get(i, 0) + strains.get(i + a, b)) + (beta * pair(key)) * (1.0 - length_of(a, b) * r)
    mask = mask_of(b)
    if mask is not None:
        f = jnp.where(mask, f, 0.0)
    return [f * sep[c] for c in range(3)]


def inner_kernel(
    plan, after_ref, factor_ref, rows_a_ref, rows_b_ref, inverse_a_ref, inverse_b_ref, pair_ref, vector_ref, force_ref
):
    keys = plan.inner_late
    plies = rows_a_ref.shape[0]
    grid = Grid(rows_a_ref.shape[-2])
    in_a = {key: n for n, key in enumerate(plan.inner_a)}
    in_b = {key: n for n, key in enumerate(plan.inner_b)}
    in_pair = {key: n for n, key in enumerate(plan.early + plan.late)}
    in_vector = {key: n for n, key in enumerate(keys)}

    def ply(p):
        rows = Store(
            (rows_b_ref, REACH, range(REACH, plan.start_a), (p,)),
            (rows_a_ref, plan.start_a, range(plan.start_a, plan.own.stop), (p,)),
        )
        factors = factors_of(factor_ref, p)
        span = plan.span(keys)
        started = set()
        def push_of(key):
            b, a, i = key
            alpha, beta = factors(a, b)
            sep = separation(rows, b, a, i, [rows.get(i, 0, c) for c in range(3)])
            r = inverse_a_ref[p, in_a[key]] if key in in_a else inverse_b_ref[p, in_b[key]]
            scale = alpha * r
            f = (beta * pair_ref[in_pair[key]]) * (1.0 - length_of(a, b) * r)
            if b:
                scale = jnp.where(grid.exists[b], scale, 0.0)
                f = jnp.where(grid.exists[b], f, 0.0)
            for c in range(3):
                vector_ref[p, in_vector[key], c] = scale * sep[c]
            return [f * sep[c] for c in range(3)]

        def force(x, values):
            for c in range(3):
                at = (p, c, x - span.start)
                force_ref[at] = force_ref[at] + values[c] if x in started else values[c]
            started.add(x)

        collect(plan, grid, keys, push_of, force)
        assert started == set(span)

    for_plies(plies, 2, ply)


def send_kernel(plan, part, after_ref, base_ref, sums_b_ref, message):
    for p in part:
        for x in range(REACH):
            message[0, p - part.start, 3 * REACH + x] = sums_b_ref[p, x]
            for c in range(3):
                message[0, p - part.start, c * REACH + x] = base_ref[p, c, x]


def strain_kernel(
    plan, tiles, after_ref, got_ref, got_more_ref, rows_a_ref, rows_b_ref, sums_a_ref, sums_b_ref, weight_ref,
    halo_ref, strain_ref, inverse_ref,
):
    plies = rows_a_ref.shape[0]
    grid = Grid(rows_a_ref.shape[-2])
    in_cross = {key: n for n, key in enumerate(plan.cross_a)}
    start = 2 * REACH
    mask_of = cross_mask_a(grid, tiles)

    def ply(p):
        rows = Store(
            (rows_b_ref, REACH, range(REACH, plan.start_a), (p,)),
            (rows_a_ref, plan.start_a, range(plan.start_a, plan.own.stop), (p,)),
            (halo_ref, plan.high.start, plan.high, (p,)),
        )
        strains = Store((strain_ref, start, range(start, plan.wide), (p,)))
        for j in range(REACH):
            row = [got_ref[0, p, j], got_ref[0, p, REACH + j], got_more_ref[0, p, j]]
            keep_row(grid, rows, plan.wide - 1 - j, [-row[0], row[1], row[2]])

        def keep(key, r):
            inverse_ref[p, in_cross[key]] = r

        sums = extension_sums(grid, rows, plan.cross_a, mask_of, keep)
        for x in range(start, plan.wide):
            if x in plan.high:
                total = got_more_ref[0, p, REACH + plan.wide - 1 - x]
            elif x >= plan.near_a.start:
                total = sums_a_ref[p, x - plan.start_a]
            else:
                total = sums_b_ref[p, x - REACH]
            if x in sums:
                total = total + sums[x]
            strain = 3.0 * total * (weight_ref[x] * weight_ref[x])
            strains.put(x, strain, 0)
            for b, moved in grid.ahead(strain).items():
                strains.put(x, moved, b)

    for_plies(plies, 3, ply)


def cross_mask_a(grid, tiles):
    if tiles % 2 == 0:
        return grid.exists.get
    has_a = jnp.ones((grid.subs, LANES), jnp.int32) * sides(tiles)[0].astype(jnp.int32) > 0
    return {b: grid.exists[b] & has_a if b else has_a for b in range(REACH + 1)}.get


def early_kernel(
    plan, tiles, rows_a_ref, rows_b_ref, halo_ref, strain_ref, inverse_ref, inverse_a_ref, inverse_b_ref, pair_ref,
    factor_ref, spring_ref, force_ref,
):
    plies = rows_a_ref.shape[0]
    grid = Grid(rows_a_ref.shape[-2])
    in_a = {key: n for n, key in enumerate(plan.inner_a)}
    in_b = {key: n for n, key in enumerate(plan.inner_b)}
    in_cross = {key: n for n, key in enumerate(plan.cross_a)}
    in_pair = {key: n for n, key in enumerate(plan.early + plan.late)}
    start = 2 * REACH
    cross_mask = cross_mask_a(grid, tiles)

    def ply(p):
        def rows_of(q, *more):
            return Store(
                (rows_b_ref, REACH, range(REACH, plan.start_a), (q,)),
                (rows_a_ref, plan.start_a, range(plan.start_a, plan.own.stop), (q,)),
                *more,
            )

        rows = rows_of(p, (halo_ref, plan.high.start, plan.high, (p,)))
        strains = Store((strain_ref, start, range(start, plan.wide), (p,)))
        factors = factors_of(factor_ref, p)
        up, down = spring_ref[p, 2], spring_ref[p, 3]
        over, under = rows_of(jnp.minimum(p + 1, plies - 1)), rows_of(jnp.maximum(p - 1, 0))
        for x in plan.own:
            for c in range(3):
                here = rows.get(x, 0, c)
                spring = up * (over.get(x, 0, c) - here) + down * (under.get(x, 0, c) - here)
                force_ref[p, c, x - REACH] = spring

        def inverse(key):
            if key in in_cross:
                return inverse_ref[p, in_cross[key]]
            return inverse_a_ref[p, in_a[key]] if key in in_a else inverse_b_ref[p, in_b[key]]

        def push_of(key):
            mask_of = cross_mask if key in in_cross else grid.exists.get
            return whole_push(rows, strains, factors, inverse, lambda k: pair_ref[in_pair[k]], mask_of, key)

        def force(x, values):
            for c in range(3):
                force_ref[p, c, x - REACH] = force_ref[p, c, x - REACH] + values[c]

        collect(plan, grid, plan.early, push_of, force)

    for_plies(plies, 2, ply)


def late_kernel(
    plan, tiles, part, final, first_ref, second_ref, got_ref, rows_a_ref, rows_b_ref, sums_b_ref, weight_ref, pair_ref,
    factor_ref, spring_ref, vector_ref, inner_ref, force_in_ref, strain_a_ref, *rest,
):
    if final:
        before_ref, out_hbm, halo_ref, cross_ref, strain_ref, force_ref, out_ref, sems, before_sem = rest
        copy_before = pltpu.make_async_copy(before_ref, out_hbm.at[:, pl.ds(0, part.start)], before_sem)
        copy_before.start()
    else:
        out_ref, halo_ref, cross_ref, strain_ref, force_ref = rest
    plies = rows_a_ref.shape[0]
    grid = Grid(rows_a_ref.shape[-2])
    odd, sign = frame()
    upper = lax.axis_index("ply") % 2 == 1
    in_cross = {key: n for n, key in enumerate(plan.cross_b)}
    in_pair = {key: n for n, key in enumerate(plan.early + plan.late)}
    in_vector = {key: n for n, key in enumerate(plan.inner_late)}
    start = 2 * REACH
    has_b = jnp.ones((grid.subs, LANES), jnp.int32) * sides(tiles)[1].astype(jnp.int32) > 0
    cross_masks = {b: grid.exists[b] & has_b if b else has_b for b in range(REACH + 1)}
    late = plan.span(plan.inner_late)

    def copy_out(p):
        return pltpu.make_async_copy(
            out_ref.at[:, pl.ds(p - part.start, 1)], out_hbm.at[:, pl.ds(p, 1)], sems.at[p - part.start]
        )

    def ply(p):
        n = p - part.start
        rows = Store(
            (halo_ref, 0, plan.low, (n,)),
            (rows_b_ref, REACH, range(REACH, plan.start_a), (p,)),
            (rows_a_ref, plan.start_a, range(plan.start_a, plan.own.stop), (p,)),
        )
        strains = Store(
            (strain_ref, 0, range(start), (n,)), (strain_a_ref, start, range(start, plan.wide), (p,))
        )
        factors = factors_of(factor_ref, p)
        for j in range(REACH):
            row = [got_ref[0, n, c * REACH + j] for c in range(3)]
            keep_row(grid, rows, REACH - 1 - j, [-row[0], row[1], row[2]])

        def keep(key, r):
            cross_ref[n, in_cross[key]] = r

        sums = extension_sums(grid, rows, plan.cross_b, cross_masks.get, keep)
        for x in range(start):
            total = got_ref[0, n, 3 * REACH + REACH - 1 - x] if x in plan.low else sums_b_ref[p, x - REACH]
            strain = 3.0 * (total + sums[x]) * (weight_ref[x] * weight_ref[x])
            strains.put(x, strain, 0)
            for b, moved in grid.ahead(strain).items():
                strains.put(x, moved, b)
        faces = []
        if p == plies - 1:
            faces.append((spring_ref[p, 0], second_ref, first_ref))
        if p == 0:
            faces.append((spring_ref[p, 1], first_ref, second_ref))
        for c in range(3):
            for x in plan.own:
                value = force_in_ref[p, c, x - REACH]
                if x in late:
                    value = value + inner_ref[p, c, x - REACH]
                for factor, one, two in faces:
                    beyond = jnp.where(upper, one[0, c, x - REACH], two[0, c, x - REACH])
                    value = value + factor * (beyond - rows.get(x, 0, c))
                force_ref[n, c, x - REACH] = value

        def push_of(key):
            if key in in_cross:
                return whole_push(
                    rows, strains, factors, lambda k: cross_ref[n, in_cross[k]], lambda k: pair_ref[in_pair[k]],
                    cross_masks.get, key,
                )
            b, a, i = key
            total = strains.get(i, 0) + strains.get(i + a, b)
            return [vector_ref[p, in_vector[key], c] * total for c in range(3)]

        def force(x, values):
            for c in range(3):
                force_ref[n, c, x - REACH] = force_ref[n, c, x - REACH] + values[c]

        collect(plan, grid, plan.late, push_of, force)
        for x in plan.own:
            at = jnp.where(odd, plan.cols - 1 - (x - REACH), x - REACH)
            for c in range(3):
                value = force_ref[n, c, x - REACH]
                out_ref[c, n, pl.ds(at, grid.subs, stride=plan.cols), :] = value * sign if c == 0 else value

    for first in range(part.start, part.stop, 2):
        group = range(first, min(first + 2, part.stop))
        for p in group:
            ply(p)
        if final:
            for p in group:
                copy_out(p).start()
    if final:
        copy_before.wait()
        for p in part:
            copy_out(p).wait()


def local(displacement, angle_index, bond_table, interface_stiffness):
    comps, plies, cols, length = displacement.shape
    subs = length // LANES
    tiles = lax.axis_size("tile")
    slabs = lax.axis_size("ply")
    assert length % LANES == 0 and cols >= 2 * REACH
    plan = Plan(cols)
    view = (
        displacement.reshape(comps, plies, cols, subs, LANES)
        .transpose(0, 1, 3, 2, 4)
        .reshape(comps, plies, subs * cols, LANES)
    )
    whole = pl.BlockSpec(memory_space=pltpu.VMEM)
    scalars = pl.BlockSpec(memory_space=pltpu.SMEM)

    def array(*shape):
        return jax.ShapeDtypeStruct((*shape, subs, LANES), jnp.float32)

    def scratch(*shape):
        return pltpu.VMEM((*shape, subs, LANES), jnp.float32)

    def call(body, name, ins, outs, out_specs=None, scratches=(), cost=1):
        return pl.pallas_call(
            body,
            out_shape=outs,
            in_specs=ins,
            out_specs=out_specs or [whole] * len(outs),
            scratch_shapes=list(scratches),
            compiler_params=pltpu.CompilerParams(vmem_limit_bytes=VMEM_LIMIT),
            cost_estimate=pl.CostEstimate(flops=cost, bytes_accessed=1, transcendentals=0),
            name=name,
        )

    swap_a = [(i, i ^ 1) for i in range(tiles) if (i ^ 1) < tiles]
    swap_b = []
    for slab in range(slabs):
        for tile in range(tiles):
            other = tile + 1 if tile % 2 else tile - 1
            if 0 <= other < tiles:
                swap_b.append((slab * tiles + tile, slab * tiles + other))
            elif (slab ^ 1) < slabs:
                swap_b.append((slab * tiles + tile, (slab ^ 1) * tiles + tile))
    swap_first = [(i, i ^ 1) for i in range(slabs) if (i ^ 1) < slabs]
    swap_second = [(i, j) for k in range(1, slabs - 1, 2) for i, j in ((k, k + 1), (k + 1, k))]
    if slabs % 2 == 0:
        swap_second += [(0, slabs - 1), (slabs - 1, 0)]
    tall = plan.own.stop - plan.start_a
    short = plan.start_a - REACH

    (message_a,) = call(
        lambda *refs: pack_kernel(plan, *refs),
        "pack",
        [whole],
        [array(1, plies, 2 * REACH)],
    )(view)
    got_a = lax.ppermute(message_a, "tile", swap_a)

    more_a, base, rows_a, sums_a, inverse_a, first, second = call(
        lambda *refs: near_a_kernel(plan, *refs),
        "near_a",
        [whole] * 2,
        [
            array(1, plies, 2 * REACH), array(plies, 3, cols), array(plies, REACH + 1, 3, tall), array(plies, tall),
            array(plies, len(plan.inner_a)), array(1, 3, cols), array(1, 3, cols),
        ],
    )(message_a, view)
    got_more_a = lax.ppermute(more_a, "tile", swap_a)
    got_second = lax.ppermute(second, "ply", swap_second)
    got_first = lax.ppermute(first, "ply", swap_first)

    rows_b, sums_b, inverse_b = call(
        lambda *refs: near_b_kernel(plan, *refs),
        "near_b",
        [whole] * 3,
        [
            array(plies, REACH + 1, 3, short), array(plies, plan.near_a.start - REACH),
            array(plies, len(plan.inner_b)),
        ],
    )(base, rows_a, sums_a)

    weight, pair, factor, spring = call(
        lambda *refs: weight_kernel(plan, tiles, slabs, *refs),
        "weights",
        [scalars] * 3 + [whole],
        [
            array(plan.wide), array(len(plan.early) + len(plan.late)), array(plies, 2 * len(OFFSETS)),
            array(plies, 4),
        ],
    )(angle_index, bond_table, interface_stiffness, got_first)

    vector_late, inner_late = call(
        lambda *refs: inner_kernel(plan, *refs),
        "inner",
        [whole] * 7,
        [array(plies, len(plan.inner_late), 3), array(plies, 3, len(plan.span(plan.inner_late)))],
    )(got_second, factor, rows_a, rows_b, inverse_a, inverse_b, pair)

    count = plies - plies // 3
    parts = [range(count), range(count, plies)]
    def send_part(part, name, after):
        (message,) = call(
            lambda *refs: send_kernel(plan, part, *refs), name, [whole] * 3, [array(1, len(part), 4 * REACH)]
        )(after, base, sums_b)
        return message, lax.ppermute(message, ("ply", "tile"), swap_b)

    message_b, got = send_part(parts[0], "send", got_a)
    got_b = [got]
    message_b, got = send_part(parts[1], "send_rest", inner_late)
    got_b.append(got)

    halo_a, strain, inverse_cross = call(
        lambda *refs: strain_kernel(plan, tiles, *refs),
        "strain",
        [whole] * 8,
        [
            array(plies, REACH + 1, 3, REACH), array(plies, REACH + 1, plan.wide - 2 * REACH),
            array(plies, len(plan.cross_a)),
        ],
    )(message_b, got_a, got_more_a, rows_a, rows_b, sums_a, sums_b, weight)

    (force,) = call(
        lambda *refs: early_kernel(plan, tiles, *refs),
        "early",
        [whole] * 10,
        [array(plies, 3, cols)],
        cost=EARLY_COST,
    )(rows_a, rows_b, halo_a, strain, inverse_cross, inverse_a, inverse_b, pair, factor, spring)

    out = []
    for part, got in zip(parts, got_b):
        final = part.stop == plies
        result = jax.ShapeDtypeStruct((comps, len(part), *view.shape[2:]), jnp.float32)
        scratches = [
            scratch(len(part), REACH + 1, 3, REACH), scratch(len(part), len(plan.cross_b)),
            scratch(len(part), REACH + 1, 2 * REACH), scratch(len(part), 3, cols),
        ]
        if final:
            scratches += [
                pltpu.VMEM(result.shape, jnp.float32), pltpu.SemaphoreType.DMA((len(part),)), pltpu.SemaphoreType.DMA,
            ]
        out = call(
            lambda *refs: late_kernel(plan, tiles, part, final, *refs),
            "late_rest" if final else "late",
            [whole] * (14 + len(out)),
            [jax.ShapeDtypeStruct(view.shape, jnp.float32) if final else result],
            out_specs=[pl.BlockSpec(memory_space=pltpu.HBM)] if final else None,
            scratches=scratches,
            cost=LATE_COST,
        )(
            got_first, got_second, got, rows_a, rows_b, sums_b, weight, pair, factor, spring, vector_late, inner_late,
            force, strain, *out,
        )
    (out,) = out
    return (
        out.reshape(comps, plies, subs, cols, LANES)
        .transpose(0, 1, 3, 2, 4)
        .reshape(comps, plies, cols, length)
    )


def solution(mesh):
    placed = (P(None, "ply", "tile", None), P("ply"), P(), P())
    return jax.shard_map(
        local, mesh=mesh, in_specs=placed, out_specs=P(None, "ply", "tile", None), check_vma=False
    )
```

```python
import math

import jax
import jax.numpy as jnp
from jax import lax
from jax.experimental import pallas as pl
from jax.experimental.pallas import tpu as pltpu
from jax.sharding import PartitionSpec as P

bulk_modulus = 40.0
REACH = 3
LANES = 128
VMEM_LIMIT = 24 * 1024 * 1024
EARLY_COST = 2 * 10**9
LATE_COST = 2 * 10**9


def bond_columns():
    halves = []
    for a in range(-REACH, REACH + 1):
        for b in range(-REACH, REACH + 1):
            if 0 < a * a + b * b <= 9 and (a > 0 or (a == 0 and b > 0)):
                halves.append((a, b))
    columns = {}
    for index, (a, b) in enumerate(halves):
        columns[(a, b)] = index
        columns[(-a, -b)] = index
    return columns


COLUMNS = bond_columns()
BONDS = {0: (1, 2, 3), 1: (-2, -1, 0, 1, 2), 2: (-2, -1, 0, 1, 2), 3: (0,)}
OFFSETS = [(a, b) for b, offsets in BONDS.items() for a in offsets]


def length_of(a, b):
    return math.sqrt(a * a + b * b)


class Plan:
    def __init__(self, cols):
        self.cols = cols
        self.wide = cols + 2 * REACH
        self.own = range(REACH, REACH + cols)
        self.low = range(0, REACH)
        self.high = range(REACH + cols, self.wide)
        self.near_b = range(REACH, 2 * REACH)
        self.near_a = range(cols, cols + REACH)
        every = [
            (b, a, i)
            for b, offsets in BONDS.items()
            for i in range(self.wide)
            for a in offsets
            if 0 <= i + a < self.wide and (i in self.own or i + a in self.own)
        ]
        inner = [k for k in every if k[2] in self.own and k[2] + k[1] in self.own]
        self.inner = inner
        self.inner_a = [k for k in inner if k[2] in self.near_a or k[2] + k[1] in self.near_a]
        self.inner_b = [k for k in inner if k not in self.inner_a]
        self.cross_a = [k for k in every if max(k[2], k[2] + k[1]) in self.high]
        self.cross_b = [k for k in every if min(k[2], k[2] + k[1]) in self.low]
        self.late = [k for k in every if min(k[2], k[2] + k[1]) < 2 * REACH]
        self.early = [k for k in every if k not in self.late]
        self.inner_early = [k for k in self.early if k in inner]
        self.inner_late = [k for k in self.late if k in inner]
        self.inner_start = self.span(self.inner_early).start
        self.start_a = min(min(k[2], k[2] + k[1]) for k in self.inner_a)


    def span(self, keys):
        ends = [x for _, a, i in keys for x in (i, i + a)]
        return range(min(ends), max(ends) + 1)


class Grid:
    def __init__(self, subs):
        self.subs = subs
        self.lane = lax.broadcasted_iota(jnp.int32, (subs, LANES), 1)
        self.y = lax.broadcasted_iota(jnp.int32, (subs, LANES), 0) * LANES + self.lane
        self.total = subs * LANES
        self.exists = {b: self.y < self.total - b for b in range(1, REACH + 1)}

    def ahead(self, row):
        after = pltpu.roll(row, self.subs - 1, axis=0)
        return {
            b: pltpu.roll(jnp.where(self.lane < b, after, row), LANES - b, axis=1) for b in range(1, REACH + 1)
        }

    def back(self, rows):
        total = None
        for b, row in rows.items():
            before = pltpu.roll(row, 1, axis=0)
            moved = pltpu.roll(jnp.where(self.lane >= LANES - b, before, row), b, axis=1)
            total = moved if total is None else total + moved
        return total

    def ring(self, a):
        total = None
        for b in range(-REACH, REACH + 1):
            if 0 < a * a + b * b <= 9:
                exists = (self.y + b >= 0) & (self.y + b < self.total)
                term = jnp.where(exists, length_of(a, b), 0.0)
                total = term if total is None else total + term
        return total


class Store:
    def __init__(self, *parts):
        self.parts = parts

    def at(self, column, *lead):
        for ref, first, columns, head in self.parts:
            if column in columns:
                return ref, (*head, *lead, column - first)
        raise KeyError(column)

    def get(self, column, *lead):
        ref, index = self.at(column, *lead)
        return ref[index]

    def put(self, column, value, *lead):
        ref, index = self.at(column, *lead)
        ref[index] = value


def frame():
    odd = lax.axis_index("tile") % 2 == 1
    return odd, jnp.where(odd, -1.0, 1.0).astype(jnp.float32)


def sides(tiles):
    tile = lax.axis_index("tile")
    has_a = (tile % 2 == 1) | (tile + 1 < tiles)
    has_b = jnp.where(tile % 2 == 1, tile + 1 < tiles, tile > 0)
    return has_a, has_b


def keep_row(grid, rows, column, row):
    for c in range(3):
        rows.put(column, row[c], 0, c)
        for b, moved in grid.ahead(row[c]).items():
            rows.put(column, moved + float(b) if c == 1 else moved, b, c)


def separation(rows, b, a, i, here):
    there = [rows.get(i + a, b, c) for c in range(3)]
    here_x = here[0] - float(a) if a else here[0]
    return there[0] - here_x, there[1] - here[1], there[2] - here[2]


def by_row(keys):
    groups = {}
    for b, a, i in keys:
        groups.setdefault((b, i), []).append(a)
    return groups.items()


def extension_sums(grid, rows, keys, mask_of, keep):
    sums = {}
    shifted = {}
    for (b, i), offsets in by_row(keys):
        here = [rows.get(i, 0, c) for c in range(3)]
        for a in offsets:
            sep = separation(rows, b, a, i, here)
            q = sep[0] * sep[0] + sep[1] * sep[1] + sep[2] * sep[2]
            r = lax.rsqrt(q)
            keep((b, a, i), r, sep)
            e = q * r - length_of(a, b)
            mask = mask_of(b)
            if mask is not None:
                e = jnp.where(mask, e, 0.0)
            sums[i] = sums[i] + e if i in sums else e
            if b == 0:
                sums[i + a] = sums[i + a] + e if i + a in sums else e
            else:
                key = (i + a, b)
                shifted[key] = shifted[key] + e if key in shifted else e
    for x in sorted({x for x, _ in shifted}):
        total = grid.back({b: shifted[(x, b)] for b in range(1, REACH + 1) if (x, b) in shifted})
        sums[x] = sums[x] + total if x in sums else total
    return sums


def chunk_of(plies, most):
    return max(n for n in range(1, most + 1) if plies % n == 0)


def for_plies(plies, most, body):
    count = chunk_of(plies, most)

    def step(n, carry):
        for k in range(count):
            body(n * count + k)
        return carry

    lax.fori_loop(0, plies // count, step, 0)


def own_row(plan, u_ref, odd, sign, p, c, column):
    x = column - REACH
    at = jnp.where(odd, plan.cols - 1 - x, x)
    row = u_ref[c, p, pl.ds(at, u_ref.shape[2] // plan.cols, stride=plan.cols), :]
    return row * sign if c == 0 else row


def pack_kernel(plan, u_ref, message):
    odd, sign = frame()
    for p in range(u_ref.shape[1]):
        for c in range(2):
            for n, column in enumerate(plan.near_a):
                message[0, p, c * REACH + n] = own_row(plan, u_ref, odd, sign, p, c, column)


def near_a_kernel(plan, after_ref, u_ref, message, base_ref, rows_ref, sums_ref, inverse_ref, first_ref, second_ref):
    plies = base_ref.shape[0]
    odd, sign = frame()
    grid = Grid(base_ref.shape[-2])
    slots = {key: n for n, key in enumerate(plan.inner_a)}

    def ply(p):
        rows = Store((rows_ref, plan.start_a, range(plan.start_a, plan.own.stop), (p,)))
        for x in plan.own:
            row = [own_row(plan, u_ref, odd, sign, p, c, x) for c in range(3)]
            for c in range(3):
                base_ref[p, c, x - REACH] = row[c]
            if x >= plan.start_a:
                keep_row(grid, rows, x, row)

        def keep(key, r, sep):
            inverse_ref[p, slots[key]] = r

        sums = extension_sums(grid, rows, plan.inner_a, grid.exists.get, keep)
        for x in rows.parts[0][2]:
            sums_ref[p, x - plan.start_a] = sums[x]
            if x in plan.near_a:
                message[0, p, x - plan.near_a.start] = base_ref[p, 2, x - REACH]
                message[0, p, REACH + x - plan.near_a.start] = sums[x]

    for_plies(plies, 3, ply)
    upper = lax.axis_index("ply") % 2 == 1
    for c in range(3):
        for x in range(plan.cols):
            low, high = base_ref[0, c, x], base_ref[plies - 1, c, x]
            first_ref[0, c, x] = jnp.where(upper, low, high)
            second_ref[0, c, x] = jnp.where(upper, high, low)


def near_b_kernel(
    plan, base_ref, rows_a_ref, sums_a_ref, rows_ref, sums_ref, inverse_ref
):
    plies = rows_a_ref.shape[0]
    grid = Grid(rows_a_ref.shape[-2])
    slots = {key: n for n, key in enumerate(plan.inner_b)}
    fresh = range(REACH, plan.start_a)
    tall = range(plan.start_a, plan.own.stop)

    def ply(p):
        rows = Store((rows_ref, REACH, fresh, (p,)), (rows_a_ref, plan.start_a, tall, (p,)))
        for x in fresh:
            keep_row(grid, rows, x, [base_ref[p, c, x - REACH] for c in range(3)])

        def keep(key, r, sep):
            inverse_ref[p, slots[key]] = r

        sums = extension_sums(grid, rows, plan.inner_b, grid.exists.get, keep)
        for x in range(REACH, plan.near_a.start):
            total = sums[x] + sums_a_ref[p, x - plan.start_a] if x >= plan.start_a else sums[x]
            sums_ref[p, x - REACH] = total

    for_plies(plies, 2, ply)


def weight_kernel(
    plan, tiles, slabs, angle_ref, table_ref, stiff_ref, after_ref, weight_ref, pair_ref, factor_ref, spring_ref
):
    plies = factor_ref.shape[0]
    odd, _ = frame()
    slab = lax.axis_index("ply")
    layers = slabs * plies

    def fill(ref, at, value):
        ref[at] = jnp.full(ref.shape[-2:], value, jnp.float32)

    for p in range(plies):
        for n, (a, b) in enumerate(OFFSETS):
            column = COLUMNS[(a, b)]
            mirrored = COLUMNS[(-a, b)]
            shear = table_ref[angle_ref[p], column if column == mirrored else jnp.where(odd, mirrored, column)]
            fill(factor_ref, (p, 2 * n), 3.0 * bulk_modulus - 5.0 * shear)
            fill(factor_ref, (p, 2 * n + 1), 15.0 / length_of(a, b) * shear)
        layer = slab * plies + p
        up = jnp.where(layer < layers - 1, stiff_ref[jnp.minimum(layer, layers - 2)], 0.0)
        down = jnp.where(layer > 0, stiff_ref[jnp.maximum(layer - 1, 0)], 0.0)
        fill(spring_ref, (p, 0), up)
        fill(spring_ref, (p, 1), down)
        fill(spring_ref, (p, 2), up if p < plies - 1 else 0.0)
        fill(spring_ref, (p, 3), down if p > 0 else 0.0)
    grid = Grid(weight_ref.shape[-2])
    ones = jnp.ones((grid.subs, LANES), jnp.int32)
    has_a, has_b = (ones * side.astype(jnp.int32) > 0 for side in sides(tiles))
    ring = {a: grid.ring(a) for a in range(REACH + 1)}
    weight = {}
    for x in range(plan.wide):
        mass = ring[0]
        for a in range(-REACH, REACH + 1):
            term = ring[abs(a)]
            if x in plan.own and x + a in plan.low:
                term = jnp.where(has_b, term, 0.0)
            if x in plan.own and x + a in plan.high:
                term = jnp.where(has_a, term, 0.0)
            if a:
                mass = mass + term
        weight[x] = 1.0 / mass
        weight_ref[x] = weight[x]
    moved = {x: {0: weight[x], **grid.ahead(weight[x])} for x in range(plan.wide)}
    for n, (b, a, i) in enumerate(plan.early + plan.late):
        pair_ref[n] = weight[i] + moved[i + a][b]


def factors_of(factor_ref, p):
    def of(a, b):
        n = OFFSETS.index((a, b))
        return factor_ref[p, 2 * n], factor_ref[p, 2 * n + 1]

    return of


def collect(plan, grid, keys, push_of, force):
    held = {}
    last = {}
    for b, a, i in keys:
        last[(i + a, b)] = i
    for (b, i), offsets in by_row(keys):
        mine = None
        for a in offsets:
            j = i + a
            push = push_of((b, a, i))
            if i in plan.own:
                mine = push if mine is None else [mine[c] + push[c] for c in range(3)]
            if j in plan.own:
                held[(j, b)] = [held[(j, b)][c] + push[c] for c in range(3)] if (j, b) in held else push
        if mine is not None:
            force(i, mine)
        for j, _ in [k for k in held if k[1] == b and last[k] == i]:
            total = held.pop((j, b))
            force(j, [-(grid.back({b: total[c]}) if b else total[c]) for c in range(3)])
    assert not held


def whole_push(rows, strains, factors, inverse, pair, mask_of, key):
    b, a, i = key
    sep = separation(rows, b, a, i, [rows.get(i, 0, c) for c in range(3)])
    return push_from(strains, factors, inverse(key), sep, pair, mask_of, key)


def push_from(strains, factors, r, sep, pair, mask_of, key):
    b, a, i = key
    alpha, beta = factors(a, b)
    f = (alpha * r) * (strains.get(i, 0) + strains.get(i + a, b)) + (beta * pair(key)) * (1.0 - length_of(a, b) * r)
    mask = mask_of(b)
    if mask is not None:
        f = jnp.where(mask, f, 0.0)
    return [f * sep[c] for c in range(3)]


def inner_kernel(
    plan, after_ref, factor_ref, rows_a_ref, rows_b_ref, inverse_a_ref, inverse_b_ref, pair_ref, vector_ref, force_ref
):
    keys = plan.inner_late
    plies = rows_a_ref.shape[0]
    grid = Grid(rows_a_ref.shape[-2])
    in_a = {key: n for n, key in enumerate(plan.inner_a)}
    in_b = {key: n for n, key in enumerate(plan.inner_b)}
    in_pair = {key: n for n, key in enumerate(plan.early + plan.late)}
    in_vector = {key: n for n, key in enumerate(keys)}

    def ply(p):
        rows = Store(
            (rows_b_ref, REACH, range(REACH, plan.start_a), (p,)),
            (rows_a_ref, plan.start_a, range(plan.start_a, plan.own.stop), (p,)),
        )
        factors = factors_of(factor_ref, p)
        span = plan.span(keys)
        started = set()
        def push_of(key):
            b, a, i = key
            alpha, beta = factors(a, b)
            sep = separation(rows, b, a, i, [rows.get(i, 0, c) for c in range(3)])
            r = inverse_a_ref[p, in_a[key]] if key in in_a else inverse_b_ref[p, in_b[key]]
            scale = alpha * r
            f = (beta * pair_ref[in_pair[key]]) * (1.0 - length_of(a, b) * r)
            if b:
                scale = jnp.where(grid.exists[b], scale, 0.0)
                f = jnp.where(grid.exists[b], f, 0.0)
            for c in range(3):
                vector_ref[p, in_vector[key], c] = scale * sep[c]
            return [f * sep[c] for c in range(3)]

        def force(x, values):
            for c in range(3):
                at = (p, c, x - span.start)
                force_ref[at] = force_ref[at] + values[c] if x in started else values[c]
            started.add(x)

        collect(plan, grid, keys, push_of, force)
        assert started == set(span)

    for_plies(plies, 2, ply)


def send_kernel(plan, part, after_ref, base_ref, sums_b_ref, message):
    for p in part:
        for x in range(REACH):
            message[0, p - part.start, 3 * REACH + x] = sums_b_ref[p, x]
            for c in range(3):
                message[0, p - part.start, c * REACH + x] = base_ref[p, c, x]


def strain_kernel(
    plan, tiles, after_ref, got_ref, got_more_ref, rows_a_ref, rows_b_ref, sums_a_ref, sums_b_ref, weight_ref,
    halo_ref, strain_ref, inverse_ref,
):
    plies = rows_a_ref.shape[0]
    grid = Grid(rows_a_ref.shape[-2])
    in_cross = {key: n for n, key in enumerate(plan.cross_a)}
    start = 2 * REACH
    mask_of = cross_mask_a(grid, tiles)

    def ply(p):
        rows = Store(
            (rows_b_ref, REACH, range(REACH, plan.start_a), (p,)),
            (rows_a_ref, plan.start_a, range(plan.start_a, plan.own.stop), (p,)),
            (halo_ref, plan.high.start, plan.high, (p,)),
        )
        strains = Store((strain_ref, start, range(start, plan.wide), (p,)))
        for j in range(REACH):
            row = [got_ref[0, p, j], got_ref[0, p, REACH + j], got_more_ref[0, p, j]]
            keep_row(grid, rows, plan.wide - 1 - j, [-row[0], row[1], row[2]])

        def keep(key, r, sep):
            inverse_ref[p, in_cross[key]] = r

        sums = extension_sums(grid, rows, plan.cross_a, mask_of, keep)
        for x in range(start, plan.wide):
            if x in plan.high:
                total = got_more_ref[0, p, REACH + plan.wide - 1 - x]
            elif x >= plan.near_a.start:
                total = sums_a_ref[p, x - plan.start_a]
            else:
                total = sums_b_ref[p, x - REACH]
            if x in sums:
                total = total + sums[x]
            strain = 3.0 * total * (weight_ref[x] * weight_ref[x])
            strains.put(x, strain, 0)
            for b, moved in grid.ahead(strain).items():
                strains.put(x, moved, b)

    for_plies(plies, 3, ply)


def cross_mask_a(grid, tiles):
    if tiles % 2 == 0:
        return grid.exists.get
    has_a = jnp.ones((grid.subs, LANES), jnp.int32) * sides(tiles)[0].astype(jnp.int32) > 0
    return {b: grid.exists[b] & has_a if b else has_a for b in range(REACH + 1)}.get


def early_kernel(
    plan, tiles, rows_a_ref, rows_b_ref, halo_ref, strain_ref, inverse_ref, inverse_a_ref, inverse_b_ref, pair_ref,
    factor_ref, spring_ref, inner_ref, first_ref, second_ref, force_ref,
):
    plies = rows_a_ref.shape[0]
    grid = Grid(rows_a_ref.shape[-2])
    in_a = {key: n for n, key in enumerate(plan.inner_a)}
    in_b = {key: n for n, key in enumerate(plan.inner_b)}
    in_cross = {key: n for n, key in enumerate(plan.cross_a)}
    in_pair = {key: n for n, key in enumerate(plan.early + plan.late)}
    start = 2 * REACH
    cross_mask = cross_mask_a(grid, tiles)
    late = plan.span(plan.inner_late)

    def ply(p):
        def rows_of(q, *more):
            return Store(
                (rows_b_ref, REACH, range(REACH, plan.start_a), (q,)),
                (rows_a_ref, plan.start_a, range(plan.start_a, plan.own.stop), (q,)),
                *more,
            )

        rows = rows_of(p, (halo_ref, plan.high.start, plan.high, (p,)))
        strains = Store((strain_ref, start, range(start, plan.wide), (p,)))
        factors = factors_of(factor_ref, p)
        up, down = spring_ref[p, 2], spring_ref[p, 3]
        over, under = rows_of(jnp.minimum(p + 1, plies - 1)), rows_of(jnp.maximum(p - 1, 0))
        for x in plan.own:
            for c in range(3):
                here = rows.get(x, 0, c)
                spring = up * (over.get(x, 0, c) - here) + down * (under.get(x, 0, c) - here)
                if x in late:
                    spring = spring + inner_ref[p, c, x - REACH]
                force_ref[p, c, x - REACH] = spring

        def inverse(key):
            if key in in_cross:
                return inverse_ref[p, in_cross[key]]
            return inverse_a_ref[p, in_a[key]] if key in in_a else inverse_b_ref[p, in_b[key]]

        def push_of(key):
            mask_of = cross_mask if key in in_cross else grid.exists.get
            return whole_push(rows, strains, factors, inverse, lambda k: pair_ref[in_pair[k]], mask_of, key)

        def force(x, values):
            for c in range(3):
                force_ref[p, c, x - REACH] = force_ref[p, c, x - REACH] + values[c]

        collect(plan, grid, plan.early, push_of, force)

    for_plies(plies, 2, ply)
    upper = lax.axis_index("ply") % 2 == 1
    for p, n, one, two in ((plies - 1, 0, second_ref, first_ref), (0, 1, first_ref, second_ref)):
        rows = Store(
            (rows_b_ref, REACH, range(REACH, plan.start_a), (p,)),
            (rows_a_ref, plan.start_a, range(plan.start_a, plan.own.stop), (p,)),
        )
        for c in range(3):
            for x in plan.own:
                at = (p, c, x - REACH)
                beyond = jnp.where(upper, one[0, c, x - REACH], two[0, c, x - REACH])
                force_ref[at] = force_ref[at] + spring_ref[p, n] * (beyond - rows.get(x, 0, c))


def late_kernel(
    plan, tiles, part, final, got_ref, rows_a_ref, rows_b_ref, sums_b_ref, weight_ref, pair_ref,
    factor_ref, vector_ref, force_in_ref, strain_a_ref, *rest,
):
    if final:
        before_ref, out_hbm, halo_ref, strain_ref, force_ref, out_ref, out_sem, before_sem = rest
        copy_before = pltpu.make_async_copy(before_ref, out_hbm.at[:, pl.ds(0, part.start)], before_sem)
        copy_before.start()
    else:
        out_ref, halo_ref, strain_ref, force_ref = rest
    plies = rows_a_ref.shape[0]
    grid = Grid(rows_a_ref.shape[-2])
    odd, sign = frame()
    in_pair = {key: n for n, key in enumerate(plan.early + plan.late)}
    in_vector = {key: n for n, key in enumerate(plan.inner_late)}
    start = 2 * REACH
    has_b = jnp.ones((grid.subs, LANES), jnp.int32) * sides(tiles)[1].astype(jnp.int32) > 0
    cross_masks = {b: grid.exists[b] & has_b if b else has_b for b in range(REACH + 1)}

    def ply(p):
        n = p - part.start
        rows = Store(
            (halo_ref, 0, plan.low, (n,)),
            (rows_b_ref, REACH, range(REACH, plan.start_a), (p,)),
            (rows_a_ref, plan.start_a, range(plan.start_a, plan.own.stop), (p,)),
        )
        strains = Store(
            (strain_ref, 0, range(start), (n,)), (strain_a_ref, start, range(start, plan.wide), (p,))
        )
        factors = factors_of(factor_ref, p)
        for j in range(REACH):
            row = [got_ref[0, n, c * REACH + j] for c in range(3)]
            keep_row(grid, rows, REACH - 1 - j, [-row[0], row[1], row[2]])

        crossed = {}

        def keep(key, r, sep):
            crossed[key] = r, sep

        sums = extension_sums(grid, rows, plan.cross_b, cross_masks.get, keep)
        for x in range(start):
            total = got_ref[0, n, 3 * REACH + REACH - 1 - x] if x in plan.low else sums_b_ref[p, x - REACH]
            strain = 3.0 * (total + sums[x]) * (weight_ref[x] * weight_ref[x])
            strains.put(x, strain, 0)
            for b, moved in grid.ahead(strain).items():
                strains.put(x, moved, b)
        for c in range(3):
            for x in plan.own:
                force_ref[n, c, x - REACH] = force_in_ref[p, c, x - REACH]

        def push_of(key):
            if key in crossed:
                r, sep = crossed[key]
                return push_from(strains, factors, r, sep, lambda k: pair_ref[in_pair[k]], cross_masks.get, key)
            b, a, i = key
            total = strains.get(i, 0) + strains.get(i + a, b)
            return [vector_ref[p, in_vector[key], c] * total for c in range(3)]

        def force(x, values):
            for c in range(3):
                force_ref[n, c, x - REACH] = force_ref[n, c, x - REACH] + values[c]

        collect(plan, grid, plan.late, push_of, force)
        for x in plan.own:
            at = jnp.where(odd, plan.cols - 1 - (x - REACH), x - REACH)
            for c in range(3):
                value = force_ref[n, c, x - REACH]
                out_ref[c, n, pl.ds(at, grid.subs, stride=plan.cols), :] = value * sign if c == 0 else value

    for p in part:
        ply(p)
    if final:
        copy_out = pltpu.make_async_copy(out_ref, out_hbm.at[:, pl.ds(part.start, len(part))], out_sem)
        copy_out.start()
        copy_before.wait()
        copy_out.wait()


def local(displacement, angle_index, bond_table, interface_stiffness):
    comps, plies, cols, length = displacement.shape
    subs = length // LANES
    tiles = lax.axis_size("tile")
    slabs = lax.axis_size("ply")
    assert length % LANES == 0 and cols >= 2 * REACH
    plan = Plan(cols)
    view = (
        displacement.reshape(comps, plies, cols, subs, LANES)
        .transpose(0, 1, 3, 2, 4)
        .reshape(comps, plies, subs * cols, LANES)
    )
    whole = pl.BlockSpec(memory_space=pltpu.VMEM)
    scalars = pl.BlockSpec(memory_space=pltpu.SMEM)

    def array(*shape):
        return jax.ShapeDtypeStruct((*shape, subs, LANES), jnp.float32)

    def scratch(*shape):
        return pltpu.VMEM((*shape, subs, LANES), jnp.float32)

    def call(body, name, ins, outs, out_specs=None, scratches=(), cost=1):
        return pl.pallas_call(
            body,
            out_shape=outs,
            in_specs=ins,
            out_specs=out_specs or [whole] * len(outs),
            scratch_shapes=list(scratches),
            compiler_params=pltpu.CompilerParams(vmem_limit_bytes=VMEM_LIMIT),
            cost_estimate=pl.CostEstimate(flops=cost, bytes_accessed=1, transcendentals=0),
            name=name,
        )

    swap_a = [(i, i ^ 1) for i in range(tiles) if (i ^ 1) < tiles]
    swap_b = []
    for slab in range(slabs):
        for tile in range(tiles):
            other = tile + 1 if tile % 2 else tile - 1
            if 0 <= other < tiles:
                swap_b.append((slab * tiles + tile, slab * tiles + other))
            elif (slab ^ 1) < slabs:
                swap_b.append((slab * tiles + tile, (slab ^ 1) * tiles + tile))
    swap_first = [(i, i ^ 1) for i in range(slabs) if (i ^ 1) < slabs]
    swap_second = [(i, j) for k in range(1, slabs - 1, 2) for i, j in ((k, k + 1), (k + 1, k))]
    if slabs % 2 == 0:
        swap_second += [(0, slabs - 1), (slabs - 1, 0)]
    tall = plan.own.stop - plan.start_a
    short = plan.start_a - REACH

    (message_a,) = call(
        lambda *refs: pack_kernel(plan, *refs),
        "pack",
        [whole],
        [array(1, plies, 2 * REACH)],
    )(view)
    got_a = lax.ppermute(message_a, "tile", swap_a)

    more_a, base, rows_a, sums_a, inverse_a, first, second = call(
        lambda *refs: near_a_kernel(plan, *refs),
        "near_a",
        [whole] * 2,
        [
            array(1, plies, 2 * REACH), array(plies, 3, cols), array(plies, REACH + 1, 3, tall), array(plies, tall),
            array(plies, len(plan.inner_a)), array(1, 3, cols), array(1, 3, cols),
        ],
    )(message_a, view)
    got_more_a = lax.ppermute(more_a, "tile", swap_a)
    got_second = lax.ppermute(second, "ply", swap_second)
    got_first = lax.ppermute(first, "ply", swap_first)

    rows_b, sums_b, inverse_b = call(
        lambda *refs: near_b_kernel(plan, *refs),
        "near_b",
        [whole] * 3,
        [
            array(plies, REACH + 1, 3, short), array(plies, plan.near_a.start - REACH),
            array(plies, len(plan.inner_b)),
        ],
    )(base, rows_a, sums_a)

    weight, pair, factor, spring = call(
        lambda *refs: weight_kernel(plan, tiles, slabs, *refs),
        "weights",
        [scalars] * 3 + [whole],
        [
            array(plan.wide), array(len(plan.early) + len(plan.late)), array(plies, 2 * len(OFFSETS)),
            array(plies, 4),
        ],
    )(angle_index, bond_table, interface_stiffness, got_first)

    vector_late, inner_late = call(
        lambda *refs: inner_kernel(plan, *refs),
        "inner",
        [whole] * 7,
        [array(plies, len(plan.inner_late), 3), array(plies, 3, len(plan.span(plan.inner_late)))],
    )(got_second, factor, rows_a, rows_b, inverse_a, inverse_b, pair)

    count = plies - plies // 3
    parts = [range(count), range(count, plies)]
    def send_part(part, name, after):
        (message,) = call(
            lambda *refs: send_kernel(plan, part, *refs), name, [whole] * 3, [array(1, len(part), 4 * REACH)]
        )(after, base, sums_b)
        return message, lax.ppermute(message, ("ply", "tile"), swap_b)

    message_b, got = send_part(parts[0], "send", got_a)
    got_b = [got]
    message_b, got = send_part(parts[1], "send_rest", inner_late)
    got_b.append(got)

    halo_a, strain, inverse_cross = call(
        lambda *refs: strain_kernel(plan, tiles, *refs),
        "strain",
        [whole] * 8,
        [
            array(plies, REACH + 1, 3, REACH), array(plies, REACH + 1, plan.wide - 2 * REACH),
            array(plies, len(plan.cross_a)),
        ],
    )(message_b, got_a, got_more_a, rows_a, rows_b, sums_a, sums_b, weight)

    (force,) = call(
        lambda *refs: early_kernel(plan, tiles, *refs),
        "early",
        [whole] * 13,
        [array(plies, 3, cols)],
        cost=EARLY_COST,
    )(
        rows_a, rows_b, halo_a, strain, inverse_cross, inverse_a, inverse_b, pair, factor, spring, inner_late,
        got_first, got_second,
    )

    out = []
    for part, got in zip(parts, got_b):
        final = part.stop == plies
        result = jax.ShapeDtypeStruct((comps, len(part), *view.shape[2:]), jnp.float32)
        scratches = [
            scratch(len(part), REACH + 1, 3, REACH), scratch(len(part), REACH + 1, 2 * REACH),
            scratch(len(part), 3, cols),
        ]
        if final:
            scratches += [
                pltpu.VMEM(result.shape, jnp.float32), pltpu.SemaphoreType.DMA, pltpu.SemaphoreType.DMA,
            ]
        out = call(
            lambda *refs: late_kernel(plan, tiles, part, final, *refs),
            "late_rest" if final else "late",
            [whole] * (10 + len(out)),
            [jax.ShapeDtypeStruct(view.shape, jnp.float32) if final else result],
            out_specs=[pl.BlockSpec(memory_space=pltpu.HBM)] if final else None,
            scratches=scratches,
            cost=LATE_COST,
        )(
            got, rows_a, rows_b, sums_b, weight, pair, factor, vector_late, force, strain, *out,
        )
    (out,) = out
    return (
        out.reshape(comps, plies, subs, cols, LANES)
        .transpose(0, 1, 3, 2, 4)
        .reshape(comps, plies, cols, length)
    )


def solution(mesh):
    placed = (P(None, "ply", "tile", None), P("ply"), P(), P())
    return jax.shard_map(
        local, mesh=mesh, in_specs=placed, out_specs=P(None, "ply", "tile", None), check_vma=False
    )
```

```python
import math

import jax
import jax.numpy as jnp
from jax import lax
from jax.experimental import pallas as pl
from jax.experimental.pallas import tpu as pltpu
from jax.sharding import PartitionSpec as P

bulk_modulus = 40.0
REACH = 3
LANES = 128
VMEM_LIMIT = 24 * 1024 * 1024
EXTRA = 1
EARLY_COST = 2 * 10**9
LATE_COST = 2 * 10**9


def bond_columns():
    halves = []
    for a in range(-REACH, REACH + 1):
        for b in range(-REACH, REACH + 1):
            if 0 < a * a + b * b <= 9 and (a > 0 or (a == 0 and b > 0)):
                halves.append((a, b))
    columns = {}
    for index, (a, b) in enumerate(halves):
        columns[(a, b)] = index
        columns[(-a, -b)] = index
    return columns


COLUMNS = bond_columns()
BONDS = {0: (1, 2, 3), 1: (-2, -1, 0, 1, 2), 2: (-2, -1, 0, 1, 2), 3: (0,)}
OFFSETS = [(a, b) for b, offsets in BONDS.items() for a in offsets]


def length_of(a, b):
    return math.sqrt(a * a + b * b)


class Plan:
    def __init__(self, cols):
        self.cols = cols
        self.wide = cols + 2 * REACH
        self.own = range(REACH, REACH + cols)
        self.low = range(0, REACH)
        self.high = range(REACH + cols, self.wide)
        self.near_b = range(REACH, 2 * REACH)
        self.near_a = range(cols, cols + REACH)
        every = [
            (b, a, i)
            for b, offsets in BONDS.items()
            for i in range(self.wide)
            for a in offsets
            if 0 <= i + a < self.wide and (i in self.own or i + a in self.own)
        ]
        inner = [k for k in every if k[2] in self.own and k[2] + k[1] in self.own]
        self.inner = inner
        self.inner_a = [k for k in inner if k[2] in self.near_a or k[2] + k[1] in self.near_a]
        self.inner_b = [k for k in inner if k not in self.inner_a]
        self.cross_a = [k for k in every if max(k[2], k[2] + k[1]) in self.high]
        self.cross_b = [k for k in every if min(k[2], k[2] + k[1]) in self.low]
        self.late = [k for k in every if min(k[2], k[2] + k[1]) < 2 * REACH]
        self.early = [k for k in every if k not in self.late]
        self.inner_early = [k for k in self.early if k in inner]
        self.inner_late = [k for k in self.late if k in inner]
        self.inner_start = self.span(self.inner_early).start
        self.start_a = min(min(k[2], k[2] + k[1]) for k in self.inner_a)


    def span(self, keys):
        ends = [x for _, a, i in keys for x in (i, i + a)]
        return range(min(ends), max(ends) + 1)


class Grid:
    def __init__(self, subs):
        self.subs = subs
        self.lane = lax.broadcasted_iota(jnp.int32, (subs, LANES), 1)
        self.y = lax.broadcasted_iota(jnp.int32, (subs, LANES), 0) * LANES + self.lane
        self.total = subs * LANES
        self.exists = {b: self.y < self.total - b for b in range(1, REACH + 1)}

    def ahead(self, row):
        after = pltpu.roll(row, self.subs - 1, axis=0)
        return {
            b: pltpu.roll(jnp.where(self.lane < b, after, row), LANES - b, axis=1) for b in range(1, REACH + 1)
        }

    def back(self, rows):
        total = None
        for b, row in rows.items():
            before = pltpu.roll(row, 1, axis=0)
            moved = pltpu.roll(jnp.where(self.lane >= LANES - b, before, row), b, axis=1)
            total = moved if total is None else total + moved
        return total

    def ring(self, a):
        total = None
        for b in range(-REACH, REACH + 1):
            if 0 < a * a + b * b <= 9:
                exists = (self.y + b >= 0) & (self.y + b < self.total)
                term = jnp.where(exists, length_of(a, b), 0.0)
                total = term if total is None else total + term
        return total


class Store:
    def __init__(self, *parts):
        self.parts = parts

    def at(self, column, *lead):
        for ref, first, columns, head in self.parts:
            if column in columns:
                return ref, (*head, *lead, column - first)
        raise KeyError(column)

    def get(self, column, *lead):
        ref, index = self.at(column, *lead)
        return ref[index]

    def put(self, column, value, *lead):
        ref, index = self.at(column, *lead)
        ref[index] = value


def frame():
    odd = lax.axis_index("tile") % 2 == 1
    return odd, jnp.where(odd, -1.0, 1.0).astype(jnp.float32)


def sides(tiles):
    tile = lax.axis_index("tile")
    has_a = (tile % 2 == 1) | (tile + 1 < tiles)
    has_b = jnp.where(tile % 2 == 1, tile + 1 < tiles, tile > 0)
    return has_a, has_b


def keep_row(grid, rows, column, row):
    for c in range(3):
        rows.put(column, row[c], 0, c)
        for b, moved in grid.ahead(row[c]).items():
            rows.put(column, moved + float(b) if c == 1 else moved, b, c)


def separation(rows, b, a, i, here):
    there = [rows.get(i + a, b, c) for c in range(3)]
    here_x = here[0] - float(a) if a else here[0]
    return there[0] - here_x, there[1] - here[1], there[2] - here[2]


def by_row(keys):
    groups = {}
    for b, a, i in keys:
        groups.setdefault((b, i), []).append(a)
    return groups.items()


def extension_sums(grid, rows, keys, mask_of, keep):
    sums = {}
    shifted = {}
    for (b, i), offsets in by_row(keys):
        here = [rows.get(i, 0, c) for c in range(3)]
        for a in offsets:
            sep = separation(rows, b, a, i, here)
            q = sep[0] * sep[0] + sep[1] * sep[1] + sep[2] * sep[2]
            r = lax.rsqrt(q)
            keep((b, a, i), r, sep)
            e = q * r - length_of(a, b)
            mask = mask_of(b)
            if mask is not None:
                e = jnp.where(mask, e, 0.0)
            sums[i] = sums[i] + e if i in sums else e
            if b == 0:
                sums[i + a] = sums[i + a] + e if i + a in sums else e
            else:
                key = (i + a, b)
                shifted[key] = shifted[key] + e if key in shifted else e
    for x in sorted({x for x, _ in shifted}):
        total = grid.back({b: shifted[(x, b)] for b in range(1, REACH + 1) if (x, b) in shifted})
        sums[x] = sums[x] + total if x in sums else total
    return sums


def chunk_of(plies, most):
    return max(n for n in range(1, most + 1) if plies % n == 0)


def for_plies(plies, most, body):
    count = chunk_of(plies, most)

    def step(n, carry):
        for k in range(count):
            body(n * count + k)
        return carry

    lax.fori_loop(0, plies // count, step, 0)


def own_row(plan, u_ref, odd, sign, p, c, column):
    x = column - REACH
    at = jnp.where(odd, plan.cols - 1 - x, x)
    row = u_ref[c, p, pl.ds(at, u_ref.shape[2] // plan.cols, stride=plan.cols), :]
    return row * sign if c == 0 else row


def pack_kernel(plan, u_ref, message):
    odd, sign = frame()
    for p in range(u_ref.shape[1]):
        for c in range(2):
            for n, column in enumerate(plan.near_a):
                message[0, p, c * REACH + n] = own_row(plan, u_ref, odd, sign, p, c, column)


def near_a_kernel(plan, after_ref, u_ref, message, base_ref, rows_ref, sums_ref, inverse_ref, first_ref, second_ref):
    plies = base_ref.shape[0]
    odd, sign = frame()
    grid = Grid(base_ref.shape[-2])
    slots = {key: n for n, key in enumerate(plan.inner_a)}

    def ply(p):
        rows = Store((rows_ref, plan.start_a, range(plan.start_a, plan.own.stop), (p,)))
        for x in plan.own:
            row = [own_row(plan, u_ref, odd, sign, p, c, x) for c in range(3)]
            for c in range(3):
                base_ref[p, c, x - REACH] = row[c]
            if x >= plan.start_a:
                keep_row(grid, rows, x, row)

        def keep(key, r, sep):
            inverse_ref[p, slots[key]] = r

        sums = extension_sums(grid, rows, plan.inner_a, grid.exists.get, keep)
        for x in rows.parts[0][2]:
            sums_ref[p, x - plan.start_a] = sums[x]
            if x in plan.near_a:
                message[0, p, x - plan.near_a.start] = base_ref[p, 2, x - REACH]
                message[0, p, REACH + x - plan.near_a.start] = sums[x]

    for_plies(plies, 3, ply)
    upper = lax.axis_index("ply") % 2 == 1
    for c in range(3):
        for x in range(plan.cols):
            low, high = base_ref[0, c, x], base_ref[plies - 1, c, x]
            first_ref[0, c, x] = jnp.where(upper, low, high)
            second_ref[0, c, x] = jnp.where(upper, high, low)


def near_b_kernel(
    plan, base_ref, rows_a_ref, sums_a_ref, rows_ref, sums_ref, inverse_ref
):
    plies = rows_a_ref.shape[0]
    grid = Grid(rows_a_ref.shape[-2])
    slots = {key: n for n, key in enumerate(plan.inner_b)}
    fresh = range(REACH, plan.start_a)
    tall = range(plan.start_a, plan.own.stop)

    def ply(p):
        rows = Store((rows_ref, REACH, fresh, (p,)), (rows_a_ref, plan.start_a, tall, (p,)))
        for x in fresh:
            keep_row(grid, rows, x, [base_ref[p, c, x - REACH] for c in range(3)])

        def keep(key, r, sep):
            inverse_ref[p, slots[key]] = r

        sums = extension_sums(grid, rows, plan.inner_b, grid.exists.get, keep)
        for x in range(REACH, plan.near_a.start):
            total = sums[x] + sums_a_ref[p, x - plan.start_a] if x >= plan.start_a else sums[x]
            sums_ref[p, x - REACH] = total

    for_plies(plies, 2, ply)


def weight_kernel(
    plan, tiles, slabs, angle_ref, table_ref, stiff_ref, after_ref, weight_ref, pair_ref, factor_ref, spring_ref
):
    plies = factor_ref.shape[0]
    odd, _ = frame()
    slab = lax.axis_index("ply")
    layers = slabs * plies

    def fill(ref, at, value):
        ref[at] = jnp.full(ref.shape[-2:], value, jnp.float32)

    for p in range(plies):
        for n, (a, b) in enumerate(OFFSETS):
            column = COLUMNS[(a, b)]
            mirrored = COLUMNS[(-a, b)]
            shear = table_ref[angle_ref[p], column if column == mirrored else jnp.where(odd, mirrored, column)]
            fill(factor_ref, (p, 2 * n), 3.0 * bulk_modulus - 5.0 * shear)
            fill(factor_ref, (p, 2 * n + 1), 15.0 / length_of(a, b) * shear)
        layer = slab * plies + p
        up = jnp.where(layer < layers - 1, stiff_ref[jnp.minimum(layer, layers - 2)], 0.0)
        down = jnp.where(layer > 0, stiff_ref[jnp.maximum(layer - 1, 0)], 0.0)
        fill(spring_ref, (p, 0), up)
        fill(spring_ref, (p, 1), down)
        fill(spring_ref, (p, 2), up if p < plies - 1 else 0.0)
        fill(spring_ref, (p, 3), down if p > 0 else 0.0)
    grid = Grid(weight_ref.shape[-2])
    ones = jnp.ones((grid.subs, LANES), jnp.int32)
    has_a, has_b = (ones * side.astype(jnp.int32) > 0 for side in sides(tiles))
    ring = {a: grid.ring(a) for a in range(REACH + 1)}
    weight = {}
    for x in range(plan.wide):
        mass = ring[0]
        for a in range(-REACH, REACH + 1):
            term = ring[abs(a)]
            if x in plan.own and x + a in plan.low:
                term = jnp.where(has_b, term, 0.0)
            if x in plan.own and x + a in plan.high:
                term = jnp.where(has_a, term, 0.0)
            if a:
                mass = mass + term
        weight[x] = 1.0 / mass
        weight_ref[x] = weight[x]
    moved = {x: {0: weight[x], **grid.ahead(weight[x])} for x in range(plan.wide)}
    for n, (b, a, i) in enumerate(plan.early + plan.late):
        pair_ref[n] = weight[i] + moved[i + a][b]


def factors_of(factor_ref, p):
    def of(a, b):
        n = OFFSETS.index((a, b))
        return factor_ref[p, 2 * n], factor_ref[p, 2 * n + 1]

    return of


def collect(plan, grid, keys, push_of, force):
    held = {}
    last = {}
    for b, a, i in keys:
        last[(i + a, b)] = i
    for (b, i), offsets in by_row(keys):
        mine = None
        for a in offsets:
            j = i + a
            push = push_of((b, a, i))
            if i in plan.own:
                mine = push if mine is None else [mine[c] + push[c] for c in range(3)]
            if j in plan.own:
                held[(j, b)] = [held[(j, b)][c] + push[c] for c in range(3)] if (j, b) in held else push
        if mine is not None:
            force(i, mine)
        for j, _ in [k for k in held if k[1] == b and last[k] == i]:
            total = held.pop((j, b))
            force(j, [-(grid.back({b: total[c]}) if b else total[c]) for c in range(3)])
    assert not held


def whole_push(rows, strains, factors, inverse, pair, mask_of, key):
    b, a, i = key
    sep = separation(rows, b, a, i, [rows.get(i, 0, c) for c in range(3)])
    return push_from(strains, factors, inverse(key), sep, pair, mask_of, key)


def push_from(strains, factors, r, sep, pair, mask_of, key):
    b, a, i = key
    alpha, beta = factors(a, b)
    f = (alpha * r) * (strains.get(i, 0) + strains.get(i + a, b)) + (beta * pair(key)) * (1.0 - length_of(a, b) * r)
    mask = mask_of(b)
    if mask is not None:
        f = jnp.where(mask, f, 0.0)
    return [f * sep[c] for c in range(3)]


def inner_kernel(
    plan, after_ref, factor_ref, rows_a_ref, rows_b_ref, inverse_a_ref, inverse_b_ref, pair_ref, vector_ref, force_ref
):
    keys = plan.inner_late
    plies = rows_a_ref.shape[0]
    grid = Grid(rows_a_ref.shape[-2])
    in_a = {key: n for n, key in enumerate(plan.inner_a)}
    in_b = {key: n for n, key in enumerate(plan.inner_b)}
    in_pair = {key: n for n, key in enumerate(plan.early + plan.late)}
    in_vector = {key: n for n, key in enumerate(keys)}

    def ply(p):
        rows = Store(
            (rows_b_ref, REACH, range(REACH, plan.start_a), (p,)),
            (rows_a_ref, plan.start_a, range(plan.start_a, plan.own.stop), (p,)),
        )
        factors = factors_of(factor_ref, p)
        span = plan.span(keys)
        started = set()
        def push_of(key):
            b, a, i = key
            alpha, beta = factors(a, b)
            sep = separation(rows, b, a, i, [rows.get(i, 0, c) for c in range(3)])
            r = inverse_a_ref[p, in_a[key]] if key in in_a else inverse_b_ref[p, in_b[key]]
            scale = alpha * r
            f = (beta * pair_ref[in_pair[key]]) * (1.0 - length_of(a, b) * r)
            if b:
                scale = jnp.where(grid.exists[b], scale, 0.0)
                f = jnp.where(grid.exists[b], f, 0.0)
            for c in range(3):
                vector_ref[p, in_vector[key], c] = scale * sep[c]
            return [f * sep[c] for c in range(3)]

        def force(x, values):
            for c in range(3):
                at = (p, c, x - span.start)
                force_ref[at] = force_ref[at] + values[c] if x in started else values[c]
            started.add(x)

        collect(plan, grid, keys, push_of, force)
        assert started == set(span)

    for_plies(plies, 2, ply)


def send_kernel(plan, wanted, after_ref, base_ref, sums_b_ref, message):
    for at, (p, n) in enumerate(wanted):
        x = n % REACH
        message[0, at] = sums_b_ref[p, x] if n >= 3 * REACH else base_ref[p, n // REACH, x]


def strain_kernel(
    plan, tiles, after_ref, got_ref, got_more_ref, rows_a_ref, rows_b_ref, sums_a_ref, sums_b_ref, weight_ref,
    halo_ref, strain_ref, inverse_ref,
):
    plies = rows_a_ref.shape[0]
    grid = Grid(rows_a_ref.shape[-2])
    in_cross = {key: n for n, key in enumerate(plan.cross_a)}
    start = 2 * REACH
    mask_of = cross_mask_a(grid, tiles)

    def ply(p):
        rows = Store(
            (rows_b_ref, REACH, range(REACH, plan.start_a), (p,)),
            (rows_a_ref, plan.start_a, range(plan.start_a, plan.own.stop), (p,)),
            (halo_ref, plan.high.start, plan.high, (p,)),
        )
        strains = Store((strain_ref, start, range(start, plan.wide), (p,)))
        for j in range(REACH):
            row = [got_ref[0, p, j], got_ref[0, p, REACH + j], got_more_ref[0, p, j]]
            keep_row(grid, rows, plan.wide - 1 - j, [-row[0], row[1], row[2]])

        def keep(key, r, sep):
            inverse_ref[p, in_cross[key]] = r

        sums = extension_sums(grid, rows, plan.cross_a, mask_of, keep)
        for x in range(start, plan.wide):
            if x in plan.high:
                total = got_more_ref[0, p, REACH + plan.wide - 1 - x]
            elif x >= plan.near_a.start:
                total = sums_a_ref[p, x - plan.start_a]
            else:
                total = sums_b_ref[p, x - REACH]
            if x in sums:
                total = total + sums[x]
            strain = 3.0 * total * (weight_ref[x] * weight_ref[x])
            strains.put(x, strain, 0)
            for b, moved in grid.ahead(strain).items():
                strains.put(x, moved, b)

    for_plies(plies, 3, ply)


def cross_mask_a(grid, tiles):
    if tiles % 2 == 0:
        return grid.exists.get
    has_a = jnp.ones((grid.subs, LANES), jnp.int32) * sides(tiles)[0].astype(jnp.int32) > 0
    return {b: grid.exists[b] & has_a if b else has_a for b in range(REACH + 1)}.get


def early_kernel(
    plan, tiles, rows_a_ref, rows_b_ref, halo_ref, strain_ref, inverse_ref, inverse_a_ref, inverse_b_ref, pair_ref,
    factor_ref, spring_ref, inner_ref, first_ref, second_ref, force_ref,
):
    plies = rows_a_ref.shape[0]
    grid = Grid(rows_a_ref.shape[-2])
    in_a = {key: n for n, key in enumerate(plan.inner_a)}
    in_b = {key: n for n, key in enumerate(plan.inner_b)}
    in_cross = {key: n for n, key in enumerate(plan.cross_a)}
    in_pair = {key: n for n, key in enumerate(plan.early + plan.late)}
    start = 2 * REACH
    cross_mask = cross_mask_a(grid, tiles)
    late = plan.span(plan.inner_late)

    def ply(p):
        def rows_of(q, *more):
            return Store(
                (rows_b_ref, REACH, range(REACH, plan.start_a), (q,)),
                (rows_a_ref, plan.start_a, range(plan.start_a, plan.own.stop), (q,)),
                *more,
            )

        rows = rows_of(p, (halo_ref, plan.high.start, plan.high, (p,)))
        strains = Store((strain_ref, start, range(start, plan.wide), (p,)))
        factors = factors_of(factor_ref, p)
        up, down = spring_ref[p, 2], spring_ref[p, 3]
        over, under = rows_of(jnp.minimum(p + 1, plies - 1)), rows_of(jnp.maximum(p - 1, 0))
        for x in plan.own:
            for c in range(3):
                here = rows.get(x, 0, c)
                spring = up * (over.get(x, 0, c) - here) + down * (under.get(x, 0, c) - here)
                if x in late:
                    spring = spring + inner_ref[p, c, x - REACH]
                force_ref[p, c, x - REACH] = spring

        def inverse(key):
            if key in in_cross:
                return inverse_ref[p, in_cross[key]]
            return inverse_a_ref[p, in_a[key]] if key in in_a else inverse_b_ref[p, in_b[key]]

        def push_of(key):
            mask_of = cross_mask if key in in_cross else grid.exists.get
            return whole_push(rows, strains, factors, inverse, lambda k: pair_ref[in_pair[k]], mask_of, key)

        def force(x, values):
            for c in range(3):
                force_ref[p, c, x - REACH] = force_ref[p, c, x - REACH] + values[c]

        collect(plan, grid, plan.early, push_of, force)

    for_plies(plies, 2, ply)
    upper = lax.axis_index("ply") % 2 == 1
    for p, n, one, two in ((plies - 1, 0, second_ref, first_ref), (0, 1, first_ref, second_ref)):
        rows = Store(
            (rows_b_ref, REACH, range(REACH, plan.start_a), (p,)),
            (rows_a_ref, plan.start_a, range(plan.start_a, plan.own.stop), (p,)),
        )
        for c in range(3):
            for x in plan.own:
                at = (p, c, x - REACH)
                beyond = jnp.where(upper, one[0, c, x - REACH], two[0, c, x - REACH])
                force_ref[at] = force_ref[at] + spring_ref[p, n] * (beyond - rows.get(x, 0, c))


def late_kernel(
    plan, tiles, part, final, wanted, got_ref, more_ref, rows_a_ref, rows_b_ref, sums_b_ref, weight_ref, pair_ref,
    factor_ref, vector_ref, force_in_ref, strain_a_ref, *rest,
):
    if final:
        before_ref, out_hbm, halo_ref, strain_ref, force_ref, out_ref, out_sem, before_sem = rest
        copy_before = pltpu.make_async_copy(before_ref, out_hbm.at[:, pl.ds(0, part.start)], before_sem)
        copy_before.start()
    else:
        out_ref, halo_ref, strain_ref, force_ref = rest
    plies = rows_a_ref.shape[0]
    grid = Grid(rows_a_ref.shape[-2])
    odd, sign = frame()
    in_pair = {key: n for n, key in enumerate(plan.early + plan.late)}
    in_vector = {key: n for n, key in enumerate(plan.inner_late)}
    start = 2 * REACH
    has_b = jnp.ones((grid.subs, LANES), jnp.int32) * sides(tiles)[1].astype(jnp.int32) > 0
    cross_masks = {b: grid.exists[b] & has_b if b else has_b for b in range(REACH + 1)}

    def got_row(p, n):
        for ref, places in zip((got_ref, more_ref), wanted):
            if (p, n) in places:
                return ref[0, places.index((p, n))]

    def ply(p):
        n = p - part.start
        rows = Store(
            (halo_ref, 0, plan.low, (n,)),
            (rows_b_ref, REACH, range(REACH, plan.start_a), (p,)),
            (rows_a_ref, plan.start_a, range(plan.start_a, plan.own.stop), (p,)),
        )
        strains = Store(
            (strain_ref, 0, range(start), (n,)), (strain_a_ref, start, range(start, plan.wide), (p,))
        )
        factors = factors_of(factor_ref, p)
        for j in range(REACH):
            row = [got_row(p, c * REACH + j) for c in range(3)]
            keep_row(grid, rows, REACH - 1 - j, [-row[0], row[1], row[2]])

        crossed = {}

        def keep(key, r, sep):
            crossed[key] = r, sep

        sums = extension_sums(grid, rows, plan.cross_b, cross_masks.get, keep)
        for x in range(start):
            total = got_row(p, 3 * REACH + REACH - 1 - x) if x in plan.low else sums_b_ref[p, x - REACH]
            strain = 3.0 * (total + sums[x]) * (weight_ref[x] * weight_ref[x])
            strains.put(x, strain, 0)
            for b, moved in grid.ahead(strain).items():
                strains.put(x, moved, b)
        for c in range(3):
            for x in plan.own:
                force_ref[n, c, x - REACH] = force_in_ref[p, c, x - REACH]

        def push_of(key):
            if key in crossed:
                r, sep = crossed[key]
                return push_from(strains, factors, r, sep, lambda k: pair_ref[in_pair[k]], cross_masks.get, key)
            b, a, i = key
            total = strains.get(i, 0) + strains.get(i + a, b)
            return [vector_ref[p, in_vector[key], c] * total for c in range(3)]

        def force(x, values):
            for c in range(3):
                force_ref[n, c, x - REACH] = force_ref[n, c, x - REACH] + values[c]

        collect(plan, grid, plan.late, push_of, force)
        for x in plan.own:
            at = jnp.where(odd, plan.cols - 1 - (x - REACH), x - REACH)
            for c in range(3):
                value = force_ref[n, c, x - REACH]
                out_ref[c, n, pl.ds(at, grid.subs, stride=plan.cols), :] = value * sign if c == 0 else value

    for p in part:
        ply(p)
    if final:
        copy_out = pltpu.make_async_copy(out_ref, out_hbm.at[:, pl.ds(part.start, len(part))], out_sem)
        copy_out.start()
        copy_before.wait()
        copy_out.wait()


def local(displacement, angle_index, bond_table, interface_stiffness):
    comps, plies, cols, length = displacement.shape
    subs = length // LANES
    tiles = lax.axis_size("tile")
    slabs = lax.axis_size("ply")
    assert length % LANES == 0 and cols >= 2 * REACH
    plan = Plan(cols)
    view = (
        displacement.reshape(comps, plies, cols, subs, LANES)
        .transpose(0, 1, 3, 2, 4)
        .reshape(comps, plies, subs * cols, LANES)
    )
    whole = pl.BlockSpec(memory_space=pltpu.VMEM)
    scalars = pl.BlockSpec(memory_space=pltpu.SMEM)

    def array(*shape):
        return jax.ShapeDtypeStruct((*shape, subs, LANES), jnp.float32)

    def scratch(*shape):
        return pltpu.VMEM((*shape, subs, LANES), jnp.float32)

    def call(body, name, ins, outs, out_specs=None, scratches=(), cost=1):
        return pl.pallas_call(
            body,
            out_shape=outs,
            in_specs=ins,
            out_specs=out_specs or [whole] * len(outs),
            scratch_shapes=list(scratches),
            compiler_params=pltpu.CompilerParams(vmem_limit_bytes=VMEM_LIMIT),
            cost_estimate=pl.CostEstimate(flops=cost, bytes_accessed=1, transcendentals=0),
            name=name,
        )

    swap_a = [(i, i ^ 1) for i in range(tiles) if (i ^ 1) < tiles]
    swap_b = []
    for slab in range(slabs):
        for tile in range(tiles):
            other = tile + 1 if tile % 2 else tile - 1
            if 0 <= other < tiles:
                swap_b.append((slab * tiles + tile, slab * tiles + other))
            elif (slab ^ 1) < slabs:
                swap_b.append((slab * tiles + tile, (slab ^ 1) * tiles + tile))
    swap_first = [(i, i ^ 1) for i in range(slabs) if (i ^ 1) < slabs]
    swap_second = [(i, j) for k in range(1, slabs - 1, 2) for i, j in ((k, k + 1), (k + 1, k))]
    if slabs % 2 == 0:
        swap_second += [(0, slabs - 1), (slabs - 1, 0)]
    tall = plan.own.stop - plan.start_a
    short = plan.start_a - REACH

    (message_a,) = call(
        lambda *refs: pack_kernel(plan, *refs),
        "pack",
        [whole],
        [array(1, plies, 2 * REACH)],
    )(view)
    got_a = lax.ppermute(message_a, "tile", swap_a)

    more_a, base, rows_a, sums_a, inverse_a, first, second = call(
        lambda *refs: near_a_kernel(plan, *refs),
        "near_a",
        [whole] * 2,
        [
            array(1, plies, 2 * REACH), array(plies, 3, cols), array(plies, REACH + 1, 3, tall), array(plies, tall),
            array(plies, len(plan.inner_a)), array(1, 3, cols), array(1, 3, cols),
        ],
    )(message_a, view)
    got_more_a = lax.ppermute(more_a, "tile", swap_a)
    got_second = lax.ppermute(second, "ply", swap_second)
    got_first = lax.ppermute(first, "ply", swap_first)

    rows_b, sums_b, inverse_b = call(
        lambda *refs: near_b_kernel(plan, *refs),
        "near_b",
        [whole] * 3,
        [
            array(plies, REACH + 1, 3, short), array(plies, plan.near_a.start - REACH),
            array(plies, len(plan.inner_b)),
        ],
    )(base, rows_a, sums_a)

    weight, pair, factor, spring = call(
        lambda *refs: weight_kernel(plan, tiles, slabs, *refs),
        "weights",
        [scalars] * 3 + [whole],
        [
            array(plan.wide), array(len(plan.early) + len(plan.late)), array(plies, 2 * len(OFFSETS)),
            array(plies, 4),
        ],
    )(angle_index, bond_table, interface_stiffness, got_first)

    vector_late, inner_late = call(
        lambda *refs: inner_kernel(plan, *refs),
        "inner",
        [whole] * 7,
        [array(plies, len(plan.inner_late), 3), array(plies, 3, len(plan.span(plan.inner_late)))],
    )(got_second, factor, rows_a, rows_b, inverse_a, inverse_b, pair)

    count = plies - plies // 3
    parts = [range(count), range(count, plies)]
    width = 4 * REACH
    wanted = [
        [(p, n) for p in parts[0] for n in range(width)] + [(p, n) for p in parts[1] for n in range(EXTRA)],
        [(p, n) for p in parts[1] for n in range(EXTRA, width)],
    ]

    def send_part(places, name, after):
        (message,) = call(
            lambda *refs: send_kernel(plan, places, *refs), name, [whole] * 3, [array(1, len(places))]
        )(after, base, sums_b)
        return message, lax.ppermute(message, ("ply", "tile"), swap_b)

    _, got_b = send_part(wanted[0], "send", got_a)
    message_b, got_rest = send_part(wanted[1], "send_rest", inner_late)

    halo_a, strain, inverse_cross = call(
        lambda *refs: strain_kernel(plan, tiles, *refs),
        "strain",
        [whole] * 8,
        [
            array(plies, REACH + 1, 3, REACH), array(plies, REACH + 1, plan.wide - 2 * REACH),
            array(plies, len(plan.cross_a)),
        ],
    )(message_b, got_a, got_more_a, rows_a, rows_b, sums_a, sums_b, weight)

    (force,) = call(
        lambda *refs: early_kernel(plan, tiles, *refs),
        "early",
        [whole] * 13,
        [array(plies, 3, cols)],
        cost=EARLY_COST,
    )(
        rows_a, rows_b, halo_a, strain, inverse_cross, inverse_a, inverse_b, pair, factor, spring, inner_late,
        got_first, got_second,
    )

    out = []
    for part in parts:
        final = part.stop == plies
        result = jax.ShapeDtypeStruct((comps, len(part), *view.shape[2:]), jnp.float32)
        scratches = [
            scratch(len(part), REACH + 1, 3, REACH), scratch(len(part), REACH + 1, 2 * REACH),
            scratch(len(part), 3, cols),
        ]
        if final:
            scratches += [
                pltpu.VMEM(result.shape, jnp.float32), pltpu.SemaphoreType.DMA, pltpu.SemaphoreType.DMA,
            ]
        out = call(
            lambda *refs: late_kernel(plan, tiles, part, final, wanted, *refs),
            "late_rest" if final else "late",
            [whole] * (11 + len(out)),
            [jax.ShapeDtypeStruct(view.shape, jnp.float32) if final else result],
            out_specs=[pl.BlockSpec(memory_space=pltpu.HBM)] if final else None,
            scratches=scratches,
            cost=LATE_COST,
        )(
            got_b, got_rest if final else got_b, rows_a, rows_b, sums_b, weight, pair, factor, vector_late, force, strain, *out,
        )
    (out,) = out
    return (
        out.reshape(comps, plies, subs, cols, LANES)
        .transpose(0, 1, 3, 2, 4)
        .reshape(comps, plies, cols, length)
    )


def solution(mesh):
    placed = (P(None, "ply", "tile", None), P("ply"), P(), P())
    return jax.shard_map(
        local, mesh=mesh, in_specs=placed, out_specs=P(None, "ply", "tile", None), check_vma=False
    )
```

```python
import math

import jax
import jax.numpy as jnp
from jax import lax
from jax.experimental import pallas as pl
from jax.experimental.pallas import tpu as pltpu
from jax.sharding import PartitionSpec as P

bulk_modulus = 40.0
REACH = 3
LANES = 128
VMEM_LIMIT = 24 * 1024 * 1024
EXTRA = 1
EARLY_COST = 2 * 10**9
LATE_COST = 2 * 10**9


def bond_columns():
    halves = []
    for a in range(-REACH, REACH + 1):
        for b in range(-REACH, REACH + 1):
            if 0 < a * a + b * b <= 9 and (a > 0 or (a == 0 and b > 0)):
                halves.append((a, b))
    columns = {}
    for index, (a, b) in enumerate(halves):
        columns[(a, b)] = index
        columns[(-a, -b)] = index
    return columns


COLUMNS = bond_columns()
BONDS = {0: (1, 2, 3), 1: (-2, -1, 0, 1, 2), 2: (-2, -1, 0, 1, 2), 3: (0,)}
OFFSETS = [(a, b) for b, offsets in BONDS.items() for a in offsets]


def length_of(a, b):
    return math.sqrt(a * a + b * b)


class Plan:
    def __init__(self, cols):
        self.cols = cols
        self.wide = cols + 2 * REACH
        self.own = range(REACH, REACH + cols)
        self.low = range(0, REACH)
        self.high = range(REACH + cols, self.wide)
        self.near_b = range(REACH, 2 * REACH)
        self.near_a = range(cols, cols + REACH)
        every = [
            (b, a, i)
            for b, offsets in BONDS.items()
            for i in range(self.wide)
            for a in offsets
            if 0 <= i + a < self.wide and (i in self.own or i + a in self.own)
        ]
        inner = [k for k in every if k[2] in self.own and k[2] + k[1] in self.own]
        self.inner = inner
        self.inner_a = [k for k in inner if k[2] in self.near_a or k[2] + k[1] in self.near_a]
        self.inner_b = [k for k in inner if k not in self.inner_a]
        self.cross_a = [k for k in every if max(k[2], k[2] + k[1]) in self.high]
        self.cross_b = [k for k in every if min(k[2], k[2] + k[1]) in self.low]
        self.late = [k for k in every if min(k[2], k[2] + k[1]) < 2 * REACH]
        self.early = [k for k in every if k not in self.late]
        self.inner_early = [k for k in self.early if k in inner]
        self.inner_late = [k for k in self.late if k in inner]
        self.inner_start = self.span(self.inner_early).start
        self.start_a = min(min(k[2], k[2] + k[1]) for k in self.inner_a)


    def span(self, keys):
        ends = [x for _, a, i in keys for x in (i, i + a)]
        return range(min(ends), max(ends) + 1)


class Grid:
    def __init__(self, subs):
        self.subs = subs
        self.lane = lax.broadcasted_iota(jnp.int32, (subs, LANES), 1)
        self.y = lax.broadcasted_iota(jnp.int32, (subs, LANES), 0) * LANES + self.lane
        self.total = subs * LANES
        self.exists = {b: self.y < self.total - b for b in range(1, REACH + 1)}

    def ahead(self, row):
        after = pltpu.roll(row, self.subs - 1, axis=0)
        return {
            b: pltpu.roll(jnp.where(self.lane < b, after, row), LANES - b, axis=1) for b in range(1, REACH + 1)
        }

    def back(self, rows):
        total = None
        for b, row in rows.items():
            before = pltpu.roll(row, 1, axis=0)
            moved = pltpu.roll(jnp.where(self.lane >= LANES - b, before, row), b, axis=1)
            total = moved if total is None else total + moved
        return total

    def ring(self, a):
        total = None
        for b in range(-REACH, REACH + 1):
            if 0 < a * a + b * b <= 9:
                exists = (self.y + b >= 0) & (self.y + b < self.total)
                term = jnp.where(exists, length_of(a, b), 0.0)
                total = term if total is None else total + term
        return total


class Store:
    def __init__(self, *parts):
        self.parts = parts

    def at(self, column, *lead):
        for ref, first, columns, head in self.parts:
            if column in columns:
                return ref, (*head, *lead, column - first)
        raise KeyError(column)

    def get(self, column, *lead):
        ref, index = self.at(column, *lead)
        return ref[index]

    def put(self, column, value, *lead):
        ref, index = self.at(column, *lead)
        ref[index] = value


def frame():
    odd = lax.axis_index("tile") % 2 == 1
    return odd, jnp.where(odd, -1.0, 1.0).astype(jnp.float32)


def sides(tiles):
    tile = lax.axis_index("tile")
    has_a = (tile % 2 == 1) | (tile + 1 < tiles)
    has_b = jnp.where(tile % 2 == 1, tile + 1 < tiles, tile > 0)
    return has_a, has_b


def keep_row(grid, rows, column, row):
    for c in range(3):
        rows.put(column, row[c], 0, c)
        for b, moved in grid.ahead(row[c]).items():
            rows.put(column, moved + float(b) if c == 1 else moved, b, c)


def separation(rows, b, a, i, here):
    there = [rows.get(i + a, b, c) for c in range(3)]
    here_x = here[0] - float(a) if a else here[0]
    return there[0] - here_x, there[1] - here[1], there[2] - here[2]


def by_row(keys):
    groups = {}
    for b, a, i in keys:
        groups.setdefault((b, i), []).append(a)
    return groups.items()


def extension_sums(grid, rows, keys, mask_of, keep):
    sums = {}
    shifted = {}
    for (b, i), offsets in by_row(keys):
        here = [rows.get(i, 0, c) for c in range(3)]
        for a in offsets:
            sep = separation(rows, b, a, i, here)
            q = sep[0] * sep[0] + sep[1] * sep[1] + sep[2] * sep[2]
            r = lax.rsqrt(q)
            keep((b, a, i), r, sep)
            e = q * r - length_of(a, b)
            mask = mask_of(b)
            if mask is not None:
                e = jnp.where(mask, e, 0.0)
            sums[i] = sums[i] + e if i in sums else e
            if b == 0:
                sums[i + a] = sums[i + a] + e if i + a in sums else e
            else:
                key = (i + a, b)
                shifted[key] = shifted[key] + e if key in shifted else e
    for x in sorted({x for x, _ in shifted}):
        total = grid.back({b: shifted[(x, b)] for b in range(1, REACH + 1) if (x, b) in shifted})
        sums[x] = sums[x] + total if x in sums else total
    return sums


def chunk_of(plies, most):
    return max(n for n in range(1, most + 1) if plies % n == 0)


def for_plies(plies, most, body):
    count = chunk_of(plies, most)

    def step(n, carry):
        for k in range(count):
            body(n * count + k)
        return carry

    lax.fori_loop(0, plies // count, step, 0)


def own_row(plan, u_ref, odd, sign, p, c, column):
    x = column - REACH
    at = jnp.where(odd, plan.cols - 1 - x, x)
    row = u_ref[c, p, pl.ds(at, u_ref.shape[2] // plan.cols, stride=plan.cols), :]
    return row * sign if c == 0 else row


def pack_kernel(plan, u_ref, message):
    odd, sign = frame()
    for p in range(u_ref.shape[1]):
        for c in range(2):
            for n, column in enumerate(plan.near_a):
                message[0, p, c * REACH + n] = own_row(plan, u_ref, odd, sign, p, c, column)


def near_a_kernel(plan, after_ref, u_ref, message, base_ref, rows_ref, sums_ref, inverse_ref, first_ref, second_ref):
    plies = base_ref.shape[0]
    odd, sign = frame()
    grid = Grid(base_ref.shape[-2])
    slots = {key: n for n, key in enumerate(plan.inner_a)}

    def ply(p):
        rows = Store((rows_ref, plan.start_a, range(plan.start_a, plan.own.stop), (p,)))
        for x in plan.own:
            row = [own_row(plan, u_ref, odd, sign, p, c, x) for c in range(3)]
            for c in range(3):
                base_ref[p, c, x - REACH] = row[c]
            if x >= plan.start_a:
                keep_row(grid, rows, x, row)

        def keep(key, r, sep):
            inverse_ref[p, slots[key]] = r

        sums = extension_sums(grid, rows, plan.inner_a, grid.exists.get, keep)
        for x in rows.parts[0][2]:
            sums_ref[p, x - plan.start_a] = sums[x]
            if x in plan.near_a:
                message[0, p, x - plan.near_a.start] = base_ref[p, 2, x - REACH]
                message[0, p, REACH + x - plan.near_a.start] = sums[x]

    for_plies(plies, 3, ply)
    upper = lax.axis_index("ply") % 2 == 1
    for c in range(3):
        for x in range(plan.cols):
            low, high = base_ref[0, c, x], base_ref[plies - 1, c, x]
            first_ref[0, c, x] = jnp.where(upper, low, high)
            second_ref[0, c, x] = jnp.where(upper, high, low)


def near_b_kernel(
    plan, base_ref, rows_a_ref, sums_a_ref, rows_ref, sums_ref, inverse_ref
):
    plies = rows_a_ref.shape[0]
    grid = Grid(rows_a_ref.shape[-2])
    slots = {key: n for n, key in enumerate(plan.inner_b)}
    fresh = range(REACH, plan.start_a)
    tall = range(plan.start_a, plan.own.stop)

    def ply(p):
        rows = Store((rows_ref, REACH, fresh, (p,)), (rows_a_ref, plan.start_a, tall, (p,)))
        for x in fresh:
            keep_row(grid, rows, x, [base_ref[p, c, x - REACH] for c in range(3)])

        def keep(key, r, sep):
            inverse_ref[p, slots[key]] = r

        sums = extension_sums(grid, rows, plan.inner_b, grid.exists.get, keep)
        for x in range(REACH, plan.near_a.start):
            total = sums[x] + sums_a_ref[p, x - plan.start_a] if x >= plan.start_a else sums[x]
            sums_ref[p, x - REACH] = total

    for_plies(plies, 2, ply)


def weight_kernel(
    plan, tiles, slabs, angle_ref, table_ref, stiff_ref, after_ref, weight_ref, pair_ref, factor_ref, spring_ref
):
    plies = factor_ref.shape[0]
    odd, _ = frame()
    slab = lax.axis_index("ply")
    layers = slabs * plies

    def fill(ref, at, value):
        ref[at] = jnp.full(ref.shape[-2:], value, jnp.float32)

    for p in range(plies):
        for n, (a, b) in enumerate(OFFSETS):
            column = COLUMNS[(a, b)]
            mirrored = COLUMNS[(-a, b)]
            shear = table_ref[angle_ref[p], column if column == mirrored else jnp.where(odd, mirrored, column)]
            fill(factor_ref, (p, 2 * n), 3.0 * bulk_modulus - 5.0 * shear)
            fill(factor_ref, (p, 2 * n + 1), 15.0 / length_of(a, b) * shear)
        layer = slab * plies + p
        up = jnp.where(layer < layers - 1, stiff_ref[jnp.minimum(layer, layers - 2)], 0.0)
        down = jnp.where(layer > 0, stiff_ref[jnp.maximum(layer - 1, 0)], 0.0)
        fill(spring_ref, (p, 0), up)
        fill(spring_ref, (p, 1), down)
        fill(spring_ref, (p, 2), up if p < plies - 1 else 0.0)
        fill(spring_ref, (p, 3), down if p > 0 else 0.0)
    grid = Grid(weight_ref.shape[-2])
    ones = jnp.ones((grid.subs, LANES), jnp.int32)
    has_a, has_b = (ones * side.astype(jnp.int32) > 0 for side in sides(tiles))
    ring = {a: grid.ring(a) for a in range(REACH + 1)}
    weight = {}
    for x in range(plan.wide):
        mass = ring[0]
        for a in range(-REACH, REACH + 1):
            term = ring[abs(a)]
            if x in plan.own and x + a in plan.low:
                term = jnp.where(has_b, term, 0.0)
            if x in plan.own and x + a in plan.high:
                term = jnp.where(has_a, term, 0.0)
            if a:
                mass = mass + term
        weight[x] = 1.0 / mass
        weight_ref[x] = 3.0 * (weight[x] * weight[x])
    moved = {x: {0: weight[x], **grid.ahead(weight[x])} for x in range(plan.wide)}
    for n, (b, a, i) in enumerate(plan.early + plan.late):
        pair_ref[n] = weight[i] + moved[i + a][b]


def factors_of(factor_ref, p):
    def of(a, b):
        n = OFFSETS.index((a, b))
        return factor_ref[p, 2 * n], factor_ref[p, 2 * n + 1]

    return of


def collect(plan, grid, keys, push_of, force):
    held = {}
    last = {}
    for b, a, i in keys:
        last[(i + a, b)] = i
    for (b, i), offsets in by_row(keys):
        mine = None
        for a in offsets:
            j = i + a
            push = push_of((b, a, i))
            if i in plan.own:
                mine = push if mine is None else [mine[c] + push[c] for c in range(3)]
            if j in plan.own:
                held[(j, b)] = [held[(j, b)][c] + push[c] for c in range(3)] if (j, b) in held else push
        if mine is not None:
            force(i, mine)
        for j, _ in [k for k in held if k[1] == b and last[k] == i]:
            total = held.pop((j, b))
            force(j, [-(grid.back({b: total[c]}) if b else total[c]) for c in range(3)])
    assert not held


def whole_push(rows, strains, factors, inverse, pair, mask_of, key):
    b, a, i = key
    sep = separation(rows, b, a, i, [rows.get(i, 0, c) for c in range(3)])
    return push_from(strains, factors, inverse(key), sep, pair, mask_of, key)


def push_from(strains, factors, r, sep, pair, mask_of, key):
    b, a, i = key
    alpha, beta = factors(a, b)
    f = (alpha * r) * (strains.get(i, 0) + strains.get(i + a, b)) + (beta * pair(key)) * (1.0 - length_of(a, b) * r)
    mask = mask_of(b)
    if mask is not None:
        f = jnp.where(mask, f, 0.0)
    return [f * sep[c] for c in range(3)]


def inner_kernel(
    plan, after_ref, factor_ref, rows_a_ref, rows_b_ref, inverse_a_ref, inverse_b_ref, pair_ref, vector_ref, force_ref
):
    keys = plan.inner_late
    plies = rows_a_ref.shape[0]
    grid = Grid(rows_a_ref.shape[-2])
    in_a = {key: n for n, key in enumerate(plan.inner_a)}
    in_b = {key: n for n, key in enumerate(plan.inner_b)}
    in_pair = {key: n for n, key in enumerate(plan.early + plan.late)}
    in_vector = {key: n for n, key in enumerate(keys)}

    def ply(p):
        rows = Store(
            (rows_b_ref, REACH, range(REACH, plan.start_a), (p,)),
            (rows_a_ref, plan.start_a, range(plan.start_a, plan.own.stop), (p,)),
        )
        factors = factors_of(factor_ref, p)
        span = plan.span(keys)
        started = set()
        def push_of(key):
            b, a, i = key
            alpha, beta = factors(a, b)
            sep = separation(rows, b, a, i, [rows.get(i, 0, c) for c in range(3)])
            r = inverse_a_ref[p, in_a[key]] if key in in_a else inverse_b_ref[p, in_b[key]]
            scale = alpha * r
            f = (beta * pair_ref[in_pair[key]]) * (1.0 - length_of(a, b) * r)
            if b:
                scale = jnp.where(grid.exists[b], scale, 0.0)
                f = jnp.where(grid.exists[b], f, 0.0)
            for c in range(3):
                vector_ref[p, in_vector[key], c] = scale * sep[c]
            return [f * sep[c] for c in range(3)]

        def force(x, values):
            for c in range(3):
                at = (p, c, x - span.start)
                force_ref[at] = force_ref[at] + values[c] if x in started else values[c]
            started.add(x)

        collect(plan, grid, keys, push_of, force)
        assert started == set(span)

    for_plies(plies, 2, ply)


def send_kernel(plan, wanted, after_ref, base_ref, sums_b_ref, message):
    for at, (p, n) in enumerate(wanted):
        x = n % REACH
        message[0, at] = sums_b_ref[p, x] if n >= 3 * REACH else base_ref[p, n // REACH, x]


def strain_kernel(
    plan, tiles, after_ref, got_ref, got_more_ref, rows_a_ref, rows_b_ref, sums_a_ref, sums_b_ref, weight_ref,
    halo_ref, strain_ref, inverse_ref,
):
    plies = rows_a_ref.shape[0]
    grid = Grid(rows_a_ref.shape[-2])
    in_cross = {key: n for n, key in enumerate(plan.cross_a)}
    start = 2 * REACH
    mask_of = cross_mask_a(grid, tiles)

    def ply(p):
        rows = Store(
            (rows_b_ref, REACH, range(REACH, plan.start_a), (p,)),
            (rows_a_ref, plan.start_a, range(plan.start_a, plan.own.stop), (p,)),
            (halo_ref, plan.high.start, plan.high, (p,)),
        )
        strains = Store((strain_ref, start, range(start, plan.wide), (p,)))
        for j in range(REACH):
            row = [got_ref[0, p, j], got_ref[0, p, REACH + j], got_more_ref[0, p, j]]
            keep_row(grid, rows, plan.wide - 1 - j, [-row[0], row[1], row[2]])

        def keep(key, r, sep):
            inverse_ref[p, in_cross[key]] = r

        sums = extension_sums(grid, rows, plan.cross_a, mask_of, keep)
        for x in range(start, plan.wide):
            if x in plan.high:
                total = got_more_ref[0, p, REACH + plan.wide - 1 - x]
            elif x >= plan.near_a.start:
                total = sums_a_ref[p, x - plan.start_a]
            else:
                total = sums_b_ref[p, x - REACH]
            if x in sums:
                total = total + sums[x]
            strain = total * weight_ref[x]
            strains.put(x, strain, 0)
            for b, moved in grid.ahead(strain).items():
                strains.put(x, moved, b)

    for_plies(plies, 3, ply)


def cross_mask_a(grid, tiles):
    if tiles % 2 == 0:
        return grid.exists.get
    has_a = jnp.ones((grid.subs, LANES), jnp.int32) * sides(tiles)[0].astype(jnp.int32) > 0
    return {b: grid.exists[b] & has_a if b else has_a for b in range(REACH + 1)}.get


def early_kernel(
    plan, tiles, rows_a_ref, rows_b_ref, halo_ref, strain_ref, inverse_ref, inverse_a_ref, inverse_b_ref, pair_ref,
    factor_ref, spring_ref, inner_ref, first_ref, second_ref, force_ref,
):
    plies = rows_a_ref.shape[0]
    grid = Grid(rows_a_ref.shape[-2])
    in_a = {key: n for n, key in enumerate(plan.inner_a)}
    in_b = {key: n for n, key in enumerate(plan.inner_b)}
    in_cross = {key: n for n, key in enumerate(plan.cross_a)}
    in_pair = {key: n for n, key in enumerate(plan.early + plan.late)}
    start = 2 * REACH
    cross_mask = cross_mask_a(grid, tiles)
    late = plan.span(plan.inner_late)

    def ply(p):
        def rows_of(q, *more):
            return Store(
                (rows_b_ref, REACH, range(REACH, plan.start_a), (q,)),
                (rows_a_ref, plan.start_a, range(plan.start_a, plan.own.stop), (q,)),
                *more,
            )

        rows = rows_of(p, (halo_ref, plan.high.start, plan.high, (p,)))
        strains = Store((strain_ref, start, range(start, plan.wide), (p,)))
        factors = factors_of(factor_ref, p)
        up, down = spring_ref[p, 2], spring_ref[p, 3]
        over, under = rows_of(jnp.minimum(p + 1, plies - 1)), rows_of(jnp.maximum(p - 1, 0))
        for x in plan.own:
            for c in range(3):
                here = rows.get(x, 0, c)
                spring = up * (over.get(x, 0, c) - here) + down * (under.get(x, 0, c) - here)
                if x in late:
                    spring = spring + inner_ref[p, c, x - REACH]
                force_ref[p, c, x - REACH] = spring

        def inverse(key):
            if key in in_cross:
                return inverse_ref[p, in_cross[key]]
            return inverse_a_ref[p, in_a[key]] if key in in_a else inverse_b_ref[p, in_b[key]]

        def push_of(key):
            mask_of = cross_mask if key in in_cross else grid.exists.get
            return whole_push(rows, strains, factors, inverse, lambda k: pair_ref[in_pair[k]], mask_of, key)

        def force(x, values):
            for c in range(3):
                force_ref[p, c, x - REACH] = force_ref[p, c, x - REACH] + values[c]

        collect(plan, grid, plan.early, push_of, force)

    for_plies(plies, 2, ply)
    upper = lax.axis_index("ply") % 2 == 1
    for p, n, one, two in ((plies - 1, 0, second_ref, first_ref), (0, 1, first_ref, second_ref)):
        rows = Store(
            (rows_b_ref, REACH, range(REACH, plan.start_a), (p,)),
            (rows_a_ref, plan.start_a, range(plan.start_a, plan.own.stop), (p,)),
        )
        for c in range(3):
            for x in plan.own:
                at = (p, c, x - REACH)
                beyond = jnp.where(upper, one[0, c, x - REACH], two[0, c, x - REACH])
                force_ref[at] = force_ref[at] + spring_ref[p, n] * (beyond - rows.get(x, 0, c))


def late_kernel(
    plan, tiles, part, final, wanted, got_ref, more_ref, rows_a_ref, rows_b_ref, sums_b_ref, weight_ref, pair_ref,
    factor_ref, vector_ref, force_in_ref, strain_a_ref, *rest,
):
    if final:
        before_ref, out_hbm, halo_ref, strain_ref, force_ref, out_ref, out_sem, before_sem = rest
        copy_before = pltpu.make_async_copy(before_ref, out_hbm.at[:, pl.ds(0, part.start)], before_sem)
        copy_before.start()
    else:
        out_ref, halo_ref, strain_ref, force_ref = rest
    plies = rows_a_ref.shape[0]
    grid = Grid(rows_a_ref.shape[-2])
    odd, sign = frame()
    in_pair = {key: n for n, key in enumerate(plan.early + plan.late)}
    in_vector = {key: n for n, key in enumerate(plan.inner_late)}
    start = 2 * REACH
    has_b = jnp.ones((grid.subs, LANES), jnp.int32) * sides(tiles)[1].astype(jnp.int32) > 0
    cross_masks = {b: grid.exists[b] & has_b if b else has_b for b in range(REACH + 1)}

    def got_row(p, n):
        for ref, places in zip((got_ref, more_ref), wanted):
            if (p, n) in places:
                return ref[0, places.index((p, n))]

    def ply(p):
        n = p - part.start
        rows = Store(
            (halo_ref, 0, plan.low, (n,)),
            (rows_b_ref, REACH, range(REACH, plan.start_a), (p,)),
            (rows_a_ref, plan.start_a, range(plan.start_a, plan.own.stop), (p,)),
        )
        strains = Store(
            (strain_ref, 0, range(start), (n,)), (strain_a_ref, start, range(start, plan.wide), (p,))
        )
        factors = factors_of(factor_ref, p)
        for j in range(REACH):
            row = [got_row(p, c * REACH + j) for c in range(3)]
            keep_row(grid, rows, REACH - 1 - j, [-row[0], row[1], row[2]])

        crossed = {}

        def keep(key, r, sep):
            crossed[key] = r, sep

        sums = extension_sums(grid, rows, plan.cross_b, cross_masks.get, keep)
        for x in range(start):
            total = got_row(p, 3 * REACH + REACH - 1 - x) if x in plan.low else sums_b_ref[p, x - REACH]
            strain = (total + sums[x]) * weight_ref[x]
            strains.put(x, strain, 0)
            for b, moved in grid.ahead(strain).items():
                strains.put(x, moved, b)
        for c in range(3):
            for x in plan.own:
                force_ref[n, c, x - REACH] = force_in_ref[p, c, x - REACH]

        def push_of(key):
            if key in crossed:
                r, sep = crossed[key]
                return push_from(strains, factors, r, sep, lambda k: pair_ref[in_pair[k]], cross_masks.get, key)
            b, a, i = key
            total = strains.get(i, 0) + strains.get(i + a, b)
            return [vector_ref[p, in_vector[key], c] * total for c in range(3)]

        def force(x, values):
            for c in range(3):
                force_ref[n, c, x - REACH] = force_ref[n, c, x - REACH] + values[c]

        collect(plan, grid, plan.late, push_of, force)
        for x in plan.own:
            at = jnp.where(odd, plan.cols - 1 - (x - REACH), x - REACH)
            for c in range(3):
                value = force_ref[n, c, x - REACH]
                out_ref[c, n, pl.ds(at, grid.subs, stride=plan.cols), :] = value * sign if c == 0 else value

    for p in part:
        ply(p)
    if final:
        copy_out = pltpu.make_async_copy(out_ref, out_hbm.at[:, pl.ds(part.start, len(part))], out_sem)
        copy_out.start()
        copy_before.wait()
        copy_out.wait()


def local(displacement, angle_index, bond_table, interface_stiffness):
    comps, plies, cols, length = displacement.shape
    subs = length // LANES
    tiles = lax.axis_size("tile")
    slabs = lax.axis_size("ply")
    assert length % LANES == 0 and cols >= 2 * REACH
    plan = Plan(cols)
    view = (
        displacement.reshape(comps, plies, cols, subs, LANES)
        .transpose(0, 1, 3, 2, 4)
        .reshape(comps, plies, subs * cols, LANES)
    )
    whole = pl.BlockSpec(memory_space=pltpu.VMEM)
    scalars = pl.BlockSpec(memory_space=pltpu.SMEM)

    def array(*shape):
        return jax.ShapeDtypeStruct((*shape, subs, LANES), jnp.float32)

    def scratch(*shape):
        return pltpu.VMEM((*shape, subs, LANES), jnp.float32)

    def call(body, name, ins, outs, out_specs=None, scratches=(), cost=1):
        return pl.pallas_call(
            body,
            out_shape=outs,
            in_specs=ins,
            out_specs=out_specs or [whole] * len(outs),
            scratch_shapes=list(scratches),
            compiler_params=pltpu.CompilerParams(vmem_limit_bytes=VMEM_LIMIT),
            cost_estimate=pl.CostEstimate(flops=cost, bytes_accessed=1, transcendentals=0),
            name=name,
        )

    swap_a = [(i, i ^ 1) for i in range(tiles) if (i ^ 1) < tiles]
    swap_b = []
    for slab in range(slabs):
        for tile in range(tiles):
            other = tile + 1 if tile % 2 else tile - 1
            if 0 <= other < tiles:
                swap_b.append((slab * tiles + tile, slab * tiles + other))
            elif (slab ^ 1) < slabs:
                swap_b.append((slab * tiles + tile, (slab ^ 1) * tiles + tile))
    swap_first = [(i, i ^ 1) for i in range(slabs) if (i ^ 1) < slabs]
    swap_second = [(i, j) for k in range(1, slabs - 1, 2) for i, j in ((k, k + 1), (k + 1, k))]
    if slabs % 2 == 0:
        swap_second += [(0, slabs - 1), (slabs - 1, 0)]
    tall = plan.own.stop - plan.start_a
    short = plan.start_a - REACH

    (message_a,) = call(
        lambda *refs: pack_kernel(plan, *refs),
        "pack",
        [whole],
        [array(1, plies, 2 * REACH)],
    )(view)
    got_a = lax.ppermute(message_a, "tile", swap_a)

    more_a, base, rows_a, sums_a, inverse_a, first, second = call(
        lambda *refs: near_a_kernel(plan, *refs),
        "near_a",
        [whole] * 2,
        [
            array(1, plies, 2 * REACH), array(plies, 3, cols), array(plies, REACH + 1, 3, tall), array(plies, tall),
            array(plies, len(plan.inner_a)), array(1, 3, cols), array(1, 3, cols),
        ],
    )(message_a, view)
    got_more_a = lax.ppermute(more_a, "tile", swap_a)
    got_second = lax.ppermute(second, "ply", swap_second)
    got_first = lax.ppermute(first, "ply", swap_first)

    rows_b, sums_b, inverse_b = call(
        lambda *refs: near_b_kernel(plan, *refs),
        "near_b",
        [whole] * 3,
        [
            array(plies, REACH + 1, 3, short), array(plies, plan.near_a.start - REACH),
            array(plies, len(plan.inner_b)),
        ],
    )(base, rows_a, sums_a)

    weight, pair, factor, spring = call(
        lambda *refs: weight_kernel(plan, tiles, slabs, *refs),
        "weights",
        [scalars] * 3 + [whole],
        [
            array(plan.wide), array(len(plan.early) + len(plan.late)), array(plies, 2 * len(OFFSETS)),
            array(plies, 4),
        ],
    )(angle_index, bond_table, interface_stiffness, got_first)

    vector_late, inner_late = call(
        lambda *refs: inner_kernel(plan, *refs),
        "inner",
        [whole] * 7,
        [array(plies, len(plan.inner_late), 3), array(plies, 3, len(plan.span(plan.inner_late)))],
    )(got_second, factor, rows_a, rows_b, inverse_a, inverse_b, pair)

    count = plies - plies // 3
    parts = [range(count), range(count, plies)]
    width = 4 * REACH
    wanted = [
        [(p, n) for p in parts[0] for n in range(width)] + [(p, n) for p in parts[1] for n in range(EXTRA)],
        [(p, n) for p in parts[1] for n in range(EXTRA, width)],
    ]

    def send_part(places, name, after):
        (message,) = call(
            lambda *refs: send_kernel(plan, places, *refs), name, [whole] * 3, [array(1, len(places))]
        )(after, base, sums_b)
        return message, lax.ppermute(message, ("ply", "tile"), swap_b)

    _, got_b = send_part(wanted[0], "send", got_a)
    message_b, got_rest = send_part(wanted[1], "send_rest", inner_late)

    halo_a, strain, inverse_cross = call(
        lambda *refs: strain_kernel(plan, tiles, *refs),
        "strain",
        [whole] * 8,
        [
            array(plies, REACH + 1, 3, REACH), array(plies, REACH + 1, plan.wide - 2 * REACH),
            array(plies, len(plan.cross_a)),
        ],
    )(message_b, got_a, got_more_a, rows_a, rows_b, sums_a, sums_b, weight)

    (force,) = call(
        lambda *refs: early_kernel(plan, tiles, *refs),
        "early",
        [whole] * 13,
        [array(plies, 3, cols)],
        cost=EARLY_COST,
    )(
        rows_a, rows_b, halo_a, strain, inverse_cross, inverse_a, inverse_b, pair, factor, spring, inner_late,
        got_first, got_second,
    )

    out = []
    for part in parts:
        final = part.stop == plies
        result = jax.ShapeDtypeStruct((comps, len(part), *view.shape[2:]), jnp.float32)
        scratches = [
            scratch(len(part), REACH + 1, 3, REACH), scratch(len(part), REACH + 1, 2 * REACH),
            scratch(len(part), 3, cols),
        ]
        if final:
            scratches += [
                pltpu.VMEM(result.shape, jnp.float32), pltpu.SemaphoreType.DMA, pltpu.SemaphoreType.DMA,
            ]
        out = call(
            lambda *refs: late_kernel(plan, tiles, part, final, wanted, *refs),
            "late_rest" if final else "late",
            [whole] * (11 + len(out)),
            [jax.ShapeDtypeStruct(view.shape, jnp.float32) if final else result],
            out_specs=[pl.BlockSpec(memory_space=pltpu.HBM)] if final else None,
            scratches=scratches,
            cost=LATE_COST,
        )(
            got_b, got_rest if final else got_b, rows_a, rows_b, sums_b, weight, pair, factor, vector_late, force, strain, *out,
        )
    (out,) = out
    return (
        out.reshape(comps, plies, subs, cols, LANES)
        .transpose(0, 1, 3, 2, 4)
        .reshape(comps, plies, cols, length)
    )


def solution(mesh):
    placed = (P(None, "ply", "tile", None), P("ply"), P(), P())
    return jax.shard_map(
        local, mesh=mesh, in_specs=placed, out_specs=P(None, "ply", "tile", None), check_vma=False
    )
```
